32 devices in a mesh: dp: 16 (over z, y, core), tensor: 2 (over x).
Axes of the slice: x: 2, y: 2, z: 4, core: 2. Of those that a mesh axis runs over, the one named last changes fastest.
Arguments:
- hidden_in: bfloat16 [64, 512, 768], P(('dp', 'tensor')), may hold values from -6 to 6
- seq_lengths: int32 [64], P('dp'), may hold values from 64 to 512, as said below
- live_seqs: int32 [32], P('dp'), may hold values from 1 to 2, as said below
- out_grad: bfloat16 [64, 512, 768], P(('dp', 'tensor')), may hold values from -6 to 6
- query_key_value_matrix: bfloat16 [768, 3, 768], P(None, None, 'tensor'), may hold values from -0.3125 to 0.3125
- query_bias: bfloat16 [768], P('tensor'), may hold values from -3 to 3
- value_bias: bfloat16 [768], P('tensor'), may hold values from -1.1953125 to 1.1953125
- projection_matrix: bfloat16 [768, 768], P('tensor'), may hold values from -1.25 to 1.25
- proj_bias: bfloat16 [768], replicated, may hold values from -2 to 2
- norm1_gain: bfloat16 [768], replicated, may hold values from 0.5 to 1.5
- norm1_shift: bfloat16 [768], replicated, may hold values from -2 to 2
- up_matrix: bfloat16 [768, 3072], P(None, 'tensor'), may hold values from -0.21875 to 0.21875
- up_bias: bfloat16 [3072], P('tensor'), may hold values from -3 to 3
- down_matrix: bfloat16 [3072, 768], P('tensor'), may hold values from -0.15625 to 0.15625
- down_bias: bfloat16 [768], replicated, may hold values from -2 to 2
- norm2_gain: bfloat16 [768], replicated, may hold values from 0.5 to 1.5
- norm2_shift: bfloat16 [768], replicated, may hold values from -2 to 2
Outputs:
- out_hidden: bfloat16 [64, 512, 768], P(('dp', 'tensor'))
- grad_hidden: bfloat16 [64, 512, 768], P(('dp', 'tensor'))
- grad_qkv_weight: float32 [768, 3, 768], P(None, None, 'tensor')
- grad_query_bias: float32 [768], P('tensor')
- grad_value_bias: float32 [768], P('tensor')
- grad_proj_weight: float32 [768, 768], P('tensor')
- grad_proj_bias: float32 [768], replicated
- grad_norm1_gain: float32 [768], replicated
- grad_norm1_shift: float32 [768], replicated
- grad_up_weight: float32 [768, 3072], P(None, 'tensor')
- grad_up_bias: float32 [3072], P('tensor')
- grad_down_weight: float32 [3072, 768], P('tensor')
- grad_down_bias: float32 [768], replicated
- grad_norm2_gain: float32 [768], replicated
- grad_norm2_shift: float32 [768], replicated
The draws below stay inside these ranges and needn't reach their ends.
Inputs may be any that keep to these rules, and one draw needn't show every extreme that they name: `seq_lengths`: valid tokens of each sequence slot; slots past it are padding. Every draw holds a sequence of 512 tokens and one of 64. `live_seqs`: how many of a device's 2 sequence slots, the first ones, hold a sequence; entry k is the device at index k of dp+tensor. Some device holds 2 and some 1 in every draw.
All inputs are finite; a program needn't handle non-finite values.
Results may differ from the reference program's by a relative error of at most 0.02.
Values may be sent and summed in bfloat16 or wider, within the bound.
No kernel may reach another device: no remote copies, remote signals or barrier semaphores. Data moves between devices by JAX's collectives and lax.ppermute only.
A program may use at most 192 MiB of HBM per device.

```python
import jax
import jax.numpy as jnp
from jax import lax

D = 768
H = 12
HS = 64
FF = 3072
LEN = 512
SEQ_LOC = 2
SEQS = 64
N_TENSOR = 2


def draw_seq_lengths(key, part):
    key = jax.random.fold_in(key, 7)
    first, second, third = jax.random.split(key, 3)
    one_draw = jax.random.randint(first, (SEQS,), 1, LEN + 1)
    two_draw = jax.random.randint(second, (SEQS,), 1, LEN + 1)
    drawn = jnp.maximum(one_draw * two_draw // LEN, LEN // 8)
    order = jax.random.permutation(third, SEQS)
    drawn = drawn.at[order[0]].set(LEN).at[order[1]].set(LEN // 8)
    return drawn.astype(jnp.int32)


def draw_live_seqs(key, part):
    key = jax.random.fold_in(key, 11)
    first, second = jax.random.split(key, 2)
    count = SEQS // SEQ_LOC
    drawn = jax.random.randint(first, (count,), 1, SEQ_LOC + 1)
    order = jax.random.permutation(second, count)
    drawn = drawn.at[order[0]].set(SEQ_LOC).at[order[1]].set(1)
    return drawn.astype(jnp.int32)


def level_of(own_key, dims, shards, smallest, largest):
    level, own = 1.0, jax.random.fold_in(own_key, 6)
    for axis_at, parts in shards:
        heights = jnp.exp(jax.random.uniform(jax.random.fold_in(own, axis_at), (parts,), jnp.float32, smallest / len(shards), largest / len(shards)))
        level = level * jnp.repeat(heights, dims[axis_at] // parts).reshape([-1 if axis == axis_at else 1 for axis in range(len(dims))])
    return level


def normal_values(stream_key, shape, deviation, reach, shards=(), held_as=jnp.bfloat16):
    values = jax.random.normal(stream_key, shape, jnp.float32) * deviation
    if len(shards) > 0:
        values = level_of(stream_key, shape, shards, -0.22, 0.18) * values
    return jnp.clip(values, min=-reach, max=reach).astype(held_as)


def setup_inputs(seed: int = 0) -> dict:
    arg_keys = jax.random.split(jax.random.key(seed), 18)
    hidden_in = normal_values(arg_keys[0], (SEQS, LEN, D), 1.0, 6.0, ((0, 32),))
    seq_lengths = draw_seq_lengths(jax.random.fold_in(arg_keys[17], 71), 0)
    live_seqs = draw_live_seqs(jax.random.fold_in(arg_keys[17], 71), 0)
    out_grad = normal_values(arg_keys[3], (SEQS, LEN, D), 1.0, 6.0, ((0, 32),))
    query_key_value_matrix = normal_values(arg_keys[4], (D, 3, D), (D // 2) ** -0.5, 0.3125, ((2, 2),))
    query_bias = normal_values(arg_keys[5], (D,), 0.5, 3.0, ((0, 2),))
    value_bias = normal_values(arg_keys[6], (D,), 0.2, 1.1953125, ((0, 2),))
    projection_matrix = normal_values(arg_keys[7], (D, D), (D // 32) ** -0.5, 1.25, ((0, 2),))
    proj_bias = normal_values(arg_keys[8], (D,), 0.3, 2.0)
    norm1_gain = jnp.clip(1.0 + 0.1 * jax.random.normal(arg_keys[9], (D,), jnp.float32), 0.5, 1.5).astype(jnp.bfloat16)
    norm1_shift = normal_values(arg_keys[10], (D,), 0.3, 2.0)
    up_matrix = normal_values(arg_keys[11], (D, FF), D ** -0.5, 0.21875, ((1, 2),))
    up_bias = normal_values(arg_keys[12], (FF,), 0.5, 3.0, ((0, 2),))
    down_matrix = normal_values(arg_keys[13], (FF, D), (FF // 2) ** -0.5, 0.15625, ((0, 2),))
    down_bias = normal_values(arg_keys[14], (D,), 0.3, 2.0)
    norm2_gain = jnp.clip(1.0 + 0.1 * jax.random.normal(arg_keys[15], (D,), jnp.float32), 0.5, 1.5).astype(jnp.bfloat16)
    norm2_shift = normal_values(arg_keys[16], (D,), 0.3, 2.0)
    return dict(hidden_in=hidden_in, seq_lengths=seq_lengths, live_seqs=live_seqs, out_grad=out_grad, query_key_value_matrix=query_key_value_matrix, query_bias=query_bias, value_bias=value_bias, projection_matrix=projection_matrix, proj_bias=proj_bias, norm1_gain=norm1_gain, norm1_shift=norm1_shift, up_matrix=up_matrix, up_bias=up_bias, down_matrix=down_matrix, down_bias=down_bias, norm2_gain=norm2_gain, norm2_shift=norm2_shift)


epsilon = 1e-06

@jax.custom_vjp
def low(v):
    return lax.optimization_barrier(v.astype(jnp.bfloat16)).astype(jnp.float32)

@jax.custom_vjp
def low_back(v):
    return v

def low_keep(v):
    return (low(v), None)

def low_pass(kept, grad):
    return (grad,)

def back_keep(v):
    return (v, None)

def back_low(kept, grad):
    return (low(grad),)
low.defvjp(low_keep, low_pass)
low_back.defvjp(back_keep, back_low)

def layer_norm(resid, gain, shift):
    average = lax.optimization_barrier(jnp.mean(resid, -1, keepdims=True))
    centred = resid - average
    variance = lax.optimization_barrier(jnp.mean(centred * centred, -1, keepdims=True))
    return centred * lax.rsqrt(variance + epsilon) * gain + shift

def block_forward(inputs, lengths, weights):
    qkv_w, q_bias, v_bias, p_weight, p_bias, gain_one, shift_one, u_weight, u_bias, d_weight, d_bias, gain_two, shift_two = weights
    highest = lax.Precision.HIGHEST
    group, length, feature_width = inputs.shape
    bias_terms = jnp.stack([q_bias, jnp.zeros_like(q_bias), v_bias])
    qkv = jnp.einsum('gld,dce->glce', inputs, qkv_w, precision=highest) + bias_terms
    qkv = low(low_back(qkv))
    heads = qkv.reshape(group, length, 3, H, HS)
    query, key_rows, value_rows = (heads[:, :, 0], heads[:, :, 1], heads[:, :, 2])
    scores = low_back(jnp.einsum('gqhe,gkhe->ghqk', query, key_rows, precision=highest) * 0.125)
    valid = jnp.arange(length, dtype=jnp.int32)[None, :] < lengths[:, None]
    scores = jnp.where(valid[:, None, None, :], scores, -1000000000.0)
    probs = low(jax.nn.softmax(scores, axis=-1))
    attended_rows = jnp.einsum('ghqk,gkhe->gqhe', probs, value_rows, precision=highest)
    attended_rows = low(low_back(attended_rows.reshape(group, length, feature_width)))
    branch = low_back(jnp.einsum('gle,ed->gld', attended_rows, p_weight, precision=highest))
    normed = layer_norm(inputs + branch + p_bias, gain_one, shift_one)
    pre_act = low_back(jnp.einsum('gld,df->glf', low(normed), u_weight, precision=highest) + u_bias)
    activated_hidden = low(jax.nn.gelu(pre_act, approximate=False))
    branch_two = low_back(jnp.einsum('glf,fd->gld', activated_hidden, d_weight, precision=highest))
    return layer_norm(normed + branch_two + d_bias, gain_two, shift_two)

def reference(hidden_in, seq_lengths, live_seqs, out_grad, query_key_value_matrix, query_bias, value_bias, projection_matrix, proj_bias, norm1_gain, norm1_shift, up_matrix, up_bias, down_matrix, down_bias, norm2_gain, norm2_shift):
    weights = tuple((w.astype(jnp.float32) for w in (query_key_value_matrix, query_bias, value_bias, projection_matrix, proj_bias, norm1_gain, norm1_shift, up_matrix, up_bias, down_matrix, down_bias, norm2_gain, norm2_shift)))
    owned = jnp.repeat(live_seqs, SEQ_LOC)
    slot_place = jnp.arange(SEQS, dtype=jnp.int32) % SEQ_LOC
    eff_len = jnp.where(slot_place < owned, seq_lengths, 0).astype(jnp.int32)
    group = SEQ_LOC * N_TENSOR
    groups = SEQS // group
    inputs_all = hidden_in.astype(jnp.float32).reshape(groups, group, LEN, D)
    lengths_all = eff_len.reshape(groups, group)
    grads_all = out_grad.astype(jnp.float32).reshape(groups, group, LEN, D)

    def step(totals, item):
        inputs_part, length_part, grad_part = item
        result, pull = jax.vjp(lambda inner, params: block_forward(inner, length_part, params), inputs_part, weights)
        live = jnp.arange(LEN, dtype=jnp.int32)[None, :] < length_part[:, None]
        grad_in, grad_weights = pull(jnp.where(live[:, :, None], grad_part, 0.0))
        totals = jax.tree.map(jnp.add, totals, grad_weights)
        return (totals, (result.astype(jnp.bfloat16), grad_in.astype(jnp.bfloat16)))
    zeros = jax.tree.map(jnp.zeros_like, weights)
    totals, (results, grad_inputs) = lax.scan(step, zeros, (inputs_all, lengths_all, grads_all))
    return (results.reshape(SEQS, LEN, D), grad_inputs.reshape(SEQS, LEN, D), totals[0], totals[1], totals[2], totals[3], totals[4], totals[5], totals[6], totals[7], totals[8], totals[9], totals[10], totals[11], totals[12])
```

```python
import jax
import jax.numpy as jnp
from jax import lax
from jax.experimental import pallas as pl
from jax.experimental.pallas import tpu as pltpu
from jax.sharding import PartitionSpec as P

HS = 64
epsilon = 1e-06
f32 = jnp.float32
bf16 = jnp.bfloat16


def flip(value):
    return lax.ppermute(value, "tensor", [(0, 1), (1, 0)])


def hop(value, mask):
    count = lax.axis_size("dp")
    return lax.ppermute(value, "dp", [(i, i ^ mask) for i in range(count)])


def dp_groups():
    count = lax.axis_size("dp")
    bits = count.bit_length() - 1
    groups, at = [], 0
    for width in [1, 1] + [2] * bits:
        width = min(width, bits - at)
        if width > 0:
            groups.append((at, width))
        at += width
    return groups


def member(group):
    at, width = group
    return (lax.axis_index("dp") >> at) & ((1 << width) - 1)


def pick(rows, pieces, which):
    count, width = rows.shape
    return lax.dynamic_index_in_dim(rows.reshape(pieces, count // pieces, width), which, 0, keepdims=False)


def gather_direct(own):
    core = member((0, 1))
    first = flip(pick(own, 2, core))
    second = hop(first, 1)
    low = jnp.where(core == 0, first, second)
    high = jnp.where(core == 0, second, first)
    return jnp.concatenate([low, high], 0)


def gather_quarters(own):
    core, row = member((0, 1)), member((1, 1))
    quarter = lax.axis_index("dp") & 3
    mine = flip(pick(own, 4, quarter))
    beside = hop(mine, 2)
    low = jnp.where(row == 0, mine, beside)
    high = jnp.where(row == 0, beside, mine)
    low_pair, high_pair = hop(low, 1), hop(high, 1)
    parts = [
        jnp.where(core == 0, low, low_pair),
        jnp.where(core == 0, low_pair, low),
        jnp.where(core == 0, high, high_pair),
        jnp.where(core == 0, high_pair, high),
    ]
    return jnp.concatenate(parts, 0)


def reduce_gradient(own, other):
    groups = dp_groups()
    core = member(groups[0])
    half = own.shape[0] // 2
    sent = jnp.concatenate([pick(own, 2, 1 - core), pick(other, 2, 1 - core)], 0).astype(bf16)
    came = hop(sent, 1)
    total = pick(own, 2, core).astype(f32) + came[:half].astype(f32)
    away = (pick(other, 2, core).astype(f32) + came[half:].astype(f32)).astype(bf16)
    total = total + flip(away).astype(f32)
    for group in groups[1:]:
        at, width = group
        pieces = 1 << width
        me = member(group)
        low = total.astype(bf16)
        came = [hop(pick(low, pieces, me ^ j), j << at) for j in range(1, pieces)]
        total = pick(total, pieces, me)
        for piece in came:
            total = total + piece.astype(f32)
    result = total.astype(bf16)[None]
    for group in groups[:0:-1]:
        at, width = group
        pieces = 1 << width
        slots = [result] + [hop(result, j << at) for j in range(1, pieces)]
        result = jnp.concatenate(slots, 0)
    result = jnp.concatenate([result, hop(result, 1)], 0)
    place = jnp.int32(0)
    for group in groups:
        place = (place << group[1]) | member(group)
    return unpermute(result, place)


def unpermute(slots, place):
    count, rows, width = slots.shape

    def kernel(place_ref, in_ref, out_ref):
        out_ref[...] = in_ref[...].astype(f32)

    out = pl.pallas_call(
        kernel,
        out_shape=jax.ShapeDtypeStruct(slots.shape, f32),
        grid_spec=pltpu.PrefetchScalarGridSpec(
            num_scalar_prefetch=1,
            grid=(count,),
            in_specs=[pl.BlockSpec((1, rows, width), lambda k, place_ref: (k ^ place_ref[0], 0, 0))],
            out_specs=pl.BlockSpec((1, rows, width), lambda k, place_ref: (k, 0, 0)),
        ),
        name="unpermute",
    )(place[None], slots)
    return out.reshape(count * rows, width)


def reduce_vector(own, other):
    total = own + flip(other)
    mask = 1
    while mask < lax.axis_size("dp"):
        total = total + hop(total, mask)
        mask *= 2
    return total


def normalize(resid, gain, shift):
    average = jnp.mean(resid, -1, keepdims=True)
    centred = resid - average
    inverse = lax.rsqrt(jnp.mean(centred * centred, -1, keepdims=True) + epsilon)
    scaled = centred * inverse
    return (scaled * gain + shift, scaled, inverse)


def norm_back(grad_rows, gain, scaled, inverse):
    weighted = grad_rows * gain
    back = inverse * (
        weighted
        - jnp.mean(weighted, -1, keepdims=True)
        - scaled * jnp.mean(weighted * scaled, -1, keepdims=True)
    )
    return (back, jnp.sum(grad_rows * scaled, 0), jnp.sum(grad_rows, 0))


def masked_scores(query, key_rows, length):
    scores = jnp.einsum("qhe,khe->hqk", query, key_rows, preferred_element_type=f32) * 0.125
    valid = lax.iota(jnp.int32, key_rows.shape[0]) < length
    return jnp.where(valid[None, None, :], scores, -1000000000.0)


def attend(inputs):
    query, key_rows, value_rows, length = inputs
    probs = jax.nn.softmax(masked_scores(query, key_rows, length), axis=-1)
    return jnp.einsum("hqk,khe->qhe", probs.astype(bf16), value_rows, preferred_element_type=f32).astype(bf16)


def attend_back(inputs):
    query, key_rows, value_rows, g_out, length = inputs
    probs = jax.nn.softmax(masked_scores(query, key_rows, length), axis=-1)
    g_probs = jnp.einsum("qhe,khe->hqk", g_out, value_rows, preferred_element_type=f32)
    delta = jnp.sum(g_probs * probs, -1, keepdims=True)
    g_scores = (probs * (g_probs - delta)).astype(bf16)
    g_query = jnp.einsum("hqk,khe->qhe", g_scores, key_rows, preferred_element_type=f32) * 0.125
    g_key = jnp.einsum("hqk,qhe->khe", g_scores, query, preferred_element_type=f32) * 0.125
    g_value = jnp.einsum("hqk,qhe->khe", probs.astype(bf16), g_out, preferred_element_type=f32)
    return tuple(g.astype(bf16) for g in (g_query, g_key, g_value))


def dot(a, b):
    return jnp.dot(a, b, preferred_element_type=f32)


def dot_t(a, b):
    return lax.dot_general(a, b, (((1,), (1,)), ((), ())), preferred_element_type=f32)


def t_dot(a, b):
    return lax.dot_general(a, b, (((0,), (0,)), ((), ())), preferred_element_type=f32)


def gelu_both(inner):
    cumulative = 0.5 * (1.0 + lax.erf(inner * 0.7071067811865476))
    density = 0.3989422804014327 * jnp.exp(-0.5 * inner * inner)
    return inner * cumulative, cumulative + inner * density


def body(
    hidden_in, seq_lengths, live_seqs, out_grad, query_key_value_matrix, query_bias, value_bias,
    projection_matrix, proj_bias, norm1_gain, norm1_shift, up_matrix, up_bias, down_matrix,
    down_bias, norm2_gain, norm2_shift,
):
    seq_count, length, features = hidden_in.shape
    width = query_key_value_matrix.shape[2]
    heads = width // HS
    tokens = seq_count * length
    gain_one, shift_one = norm1_gain.astype(f32), norm1_shift.astype(f32)
    gain_two, shift_two = norm2_gain.astype(f32), norm2_shift.astype(f32)
    side = lax.axis_index("tensor")
    own_len = lax.dynamic_slice_in_dim(seq_lengths, side * seq_count, seq_count)
    owned = lax.dynamic_index_in_dim(live_seqs, side, 0, keepdims=False)
    own_len = jnp.where(lax.iota(jnp.int32, seq_count) < owned, own_len, 0)

    x = hidden_in.reshape(tokens, features)
    qkv_w = query_key_value_matrix.reshape(features, 3 * width)
    qkv_o = gather_direct(qkv_w)
    up_t = up_matrix
    biases = jnp.concatenate([query_bias, value_bias, up_bias])
    biases_o = flip(biases)
    proj_o = gather_quarters(projection_matrix)
    up_o = gather_quarters(up_t)
    down_o = gather_quarters(down_matrix)

    def project(weight, bias):
        bias = jnp.concatenate([bias[:width], jnp.zeros((width,), bias.dtype), bias[width : 2 * width]])
        rows = (dot(x, weight) + bias.astype(f32)).astype(bf16)
        return rows.reshape(seq_count, length, 3, heads, HS)

    def forward(rows):
        out = lax.map(attend, (rows[:, :, 0], rows[:, :, 1], rows[:, :, 2], own_len))
        return out.reshape(tokens, width)

    qkv_rows = [project(qkv_w, biases), project(qkv_o, biases_o)]
    attended = [forward(rows) for rows in qkv_rows]
    projs = [projection_matrix, proj_o]
    ups = [up_matrix, up_o]
    downs = [down_matrix, down_o]
    up_biases = [biases[2 * width :].astype(f32), biases_o[2 * width :].astype(f32)]
    branch = dot(attended[0], projs[0]) + dot(attended[1], projs[1])
    resid_one = x.astype(f32) + branch + proj_bias.astype(f32)
    normed_one, scaled_one, inverse_one = normalize(resid_one, gain_one, shift_one)
    normed_low = normed_one.astype(bf16)
    activated, slopes = [], []
    for k in range(2):
        act, slope = gelu_both(dot(normed_low, ups[k]) + up_biases[k])
        activated.append(act.astype(bf16))
        slopes.append(slope.astype(bf16))
    branch = dot(activated[0], downs[0]) + dot(activated[1], downs[1])
    resid_two = normed_one + branch + down_bias.astype(f32)
    normed_two, scaled_two, inverse_two = normalize(resid_two, gain_two, shift_two)
    out_hidden = normed_two.astype(bf16).reshape(hidden_in.shape)

    live = lax.iota(jnp.int32, length)[None, :] < own_len[:, None]
    out_back = jnp.where(live[:, :, None], out_grad.astype(f32), 0.0).reshape(tokens, features)
    g_resid_two, grad_gain_two, grad_shift_two = norm_back(out_back, gain_two, scaled_two, inverse_two)
    grad_down_bias = jnp.sum(g_resid_two, 0)
    g_mlp = g_resid_two.astype(bf16)
    down_grad = reduce_gradient(*[t_dot(act, g_mlp).astype(bf16) for act in activated])
    g_pre = [(dot_t(g_mlp, downs[k]) * slopes[k].astype(f32)).astype(bf16) for k in range(2)]
    up_grad = reduce_gradient(*[t_dot(normed_low, g).astype(bf16) for g in g_pre])
    grad_up_bias = [jnp.sum(g.astype(f32), 0) for g in g_pre]
    g_normed = g_resid_two + dot_t(g_pre[0], ups[0]) + dot_t(g_pre[1], ups[1])
    g_resid_one, grad_gain_one, grad_shift_one = norm_back(g_normed, gain_one, scaled_one, inverse_one)
    grad_proj_bias = jnp.sum(g_resid_one, 0)
    g_attn = g_resid_one.astype(bf16)
    proj_grad = reduce_gradient(*[t_dot(rows, g_attn).astype(bf16) for rows in attended])
    g_qkv = []
    for k in range(2):
        g_att = dot_t(g_attn, projs[k]).astype(bf16).reshape(seq_count, length, heads, HS)
        rows = qkv_rows[k]
        parts = lax.map(attend_back, (rows[:, :, 0], rows[:, :, 1], rows[:, :, 2], g_att, own_len))
        g_qkv.append(jnp.concatenate([p.reshape(tokens, width) for p in parts], 1))
    qkv_grad = reduce_gradient(*[t_dot(x, g).astype(bf16) for g in g_qkv])
    sums = [jnp.sum(g.astype(f32), 0) for g in g_qkv]
    grad_hidden = (g_resid_one + dot_t(g_qkv[0], qkv_w) + dot_t(g_qkv[1], qkv_o)).astype(bf16)
    shared = [grad_proj_bias, grad_gain_one, grad_shift_one, grad_down_bias, grad_gain_two, grad_shift_two]
    vector = reduce_vector(
        *[jnp.concatenate(shared + [sums[k][:width], sums[k][2 * width :], grad_up_bias[k]]) for k in range(2)]
    )
    cuts = [features * k for k in range(1, 7)] + [6 * features + width, 6 * features + 2 * width]
    vector = jnp.split(vector, cuts)
    return (
        out_hidden,
        grad_hidden.reshape(hidden_in.shape),
        qkv_grad.reshape(features, 3, width),
        vector[6],
        vector[7],
        proj_grad,
        vector[0],
        vector[1],
        vector[2],
        up_grad,
        vector[8],
        down_grad,
        vector[3],
        vector[4],
        vector[5],
    )


def solution(mesh):
    rows = P(("dp", "tensor"), None, None)
    placed = (
        rows, P("dp"), P("dp"), rows, P(None, None, "tensor"), P("tensor"), P("tensor"),
        P("tensor", None), P(), P(), P(), P(None, "tensor"), P("tensor"), P("tensor", None),
        P(), P(), P(),
    )
    outs = (
        rows, rows, P(None, None, "tensor"), P("tensor"), P("tensor"), P("tensor", None), P(), P(),
        P(), P(None, "tensor"), P("tensor"), P("tensor", None), P(), P(), P(),
    )
    return jax.shard_map(body, mesh=mesh, in_specs=placed, out_specs=outs, check_vma=False)
```

```python
import jax
import jax.numpy as jnp
from jax import lax
from jax.experimental import pallas as pl
from jax.experimental.pallas import tpu as pltpu
from jax.sharding import PartitionSpec as P

HS = 64
epsilon = 1e-06
f32 = jnp.float32
bf16 = jnp.bfloat16


def flip(value):
    return lax.ppermute(value, "tensor", [(0, 1), (1, 0)])


def hop(value, mask):
    count = lax.axis_size("dp")
    return lax.ppermute(value, "dp", [(i, i ^ mask) for i in range(count)])


def dp_groups():
    count = lax.axis_size("dp")
    bits = count.bit_length() - 1
    groups, at = [], 0
    for width in [1, 1] + [2] * bits:
        width = min(width, bits - at)
        if width > 0:
            groups.append((at, width))
        at += width
    return groups


def member(group):
    at, width = group
    return (lax.axis_index("dp") >> at) & ((1 << width) - 1)


def pick(rows, pieces, which):
    count, width = rows.shape
    return lax.dynamic_index_in_dim(rows.reshape(pieces, count // pieces, width), which, 0, keepdims=False)


def tie(value, *holders):
    arrays = [value] + [array for holder in holders for array in holder.came]
    arrays = lax.optimization_barrier(tuple(arrays))
    at = 1
    for holder in holders:
        holder.came = list(arrays[at : at + len(holder.came)])
        at += len(holder.came)
    return arrays[0]


def by_bit(bit, zero, one):
    return jnp.where(bit == 0, zero, one)


class Gather:
    def __init__(self, sent, spread):
        self.spread = spread
        self.came = [flip(sent)]

    def beside(self):
        row = member((1, 1))
        (mine,) = self.came
        (other,) = self.came = [hop(mine, 2)]
        self.mine = mine

    def cores(self):
        if self.spread:
            row = member((1, 1))
            (other,) = self.came
            self.parts = [by_bit(row, self.mine, other), by_bit(row, other, self.mine)]
        else:
            self.parts = self.came
        self.came = [hop(part, 1) for part in self.parts]

    def finish(self):
        core = member((0, 1))
        rows = []
        for mine, other in zip(self.parts, self.came):
            rows += [by_bit(core, mine, other), by_bit(core, other, mine)]
        return jnp.concatenate(rows, 0)


class Reduction:
    def __init__(self):
        self.groups = dp_groups()

    def cores(self, own, other):
        self.core = member(self.groups[0])
        self.own, self.other = own, other
        self.came = [hop(pick(rows, 2, 1 - self.core), 1) for rows in (other, own)]

    def sides(self):
        away = pick(self.other, 2, self.core).astype(f32) + self.came[0].astype(f32)
        self.total = pick(self.own, 2, self.core).astype(f32) + self.came[1].astype(f32)
        self.came = [flip(away.astype(bf16))]

    def settle(self):
        for rows in self.came:
            self.total = self.total + rows.astype(f32)

    def scatter(self, group):
        self.settle()
        at, width = group
        pieces, me = 1 << width, member(group)
        low = self.total.astype(bf16)
        self.came = [hop(pick(low, pieces, me ^ j), j << at) for j in range(1, pieces)]
        self.total = pick(self.total, pieces, me)

    def gather(self, k):
        if k == len(self.groups) - 1:
            self.settle()
            self.result = self.total.astype(bf16)
        else:
            self.result = assemble([self.result] + self.came, member(self.groups[k + 1]), bf16)
        at, width = self.groups[k]
        self.came = [hop(self.result, j << at) for j in range(1, 1 << width)]

    def finish(self, split=1):
        return assemble([self.result] + self.came, self.core, f32, split)

    def rest(self, split=1):
        for group in self.groups[1:]:
            self.scatter(group)
        for k in range(len(self.groups) - 1, -1, -1):
            self.gather(k)
        return self.finish(split)


def assemble(slots, me, dtype, split=1):
    count = len(slots)
    rows, width = slots[0].shape
    part = width // split

    def kernel(me_ref, *refs):
        out_ref = refs[-1]
        step = pl.program_id(0) ^ me_ref[0]
        for j in range(count):

            @pl.when(step == j)
            def _():
                if split == 1:
                    out_ref[0] = refs[j][...].astype(dtype)
                else:
                    for c in range(split):
                        out_ref[0, :, c, :] = refs[j][:, c * part : (c + 1) * part].astype(dtype)

    shape = (count, rows, width) if split == 1 else (count, rows, split, part)
    out = pl.pallas_call(
        kernel,
        out_shape=jax.ShapeDtypeStruct(shape, dtype),
        grid_spec=pltpu.PrefetchScalarGridSpec(
            num_scalar_prefetch=1,
            grid=(count,),
            in_specs=[pl.BlockSpec((rows, width), lambda k, _: (0, 0)) for _ in slots],
            out_specs=pl.BlockSpec((1,) + shape[1:], lambda k, _: (k,) + (0,) * (len(shape) - 1)),
        ),
        compiler_params=pltpu.CompilerParams(vmem_limit_bytes=48 * 1024 * 1024),
        cost_estimate=pl.CostEstimate(flops=0, bytes_accessed=count * rows * width * 6, transcendentals=0),
        name="assemble",
    )(me[None].astype(jnp.int32), *slots)
    return out.reshape((count * rows,) + shape[2:])


def flatten_qkv(matrix, core):
    rows, three, part = matrix.shape
    block = rows // 4

    def kernel(core_ref, in_ref, out_ref, sent_ref):
        for c in range(three):
            out_ref[:, c * part : (c + 1) * part] = in_ref[:, c, :]

        @pl.when(pl.program_id(0) < 2)
        def _():
            sent_ref[...] = out_ref[...]

    return pl.pallas_call(
        kernel,
        out_shape=(
            jax.ShapeDtypeStruct((rows, three * part), matrix.dtype),
            jax.ShapeDtypeStruct((rows // 2, three * part), matrix.dtype),
        ),
        grid_spec=pltpu.PrefetchScalarGridSpec(
            num_scalar_prefetch=1,
            grid=(4,),
            in_specs=[pl.BlockSpec((block, three, part), lambda k, c: ((k + 2 * c[0]) % 4, 0, 0))],
            out_specs=[
                pl.BlockSpec((block, three * part), lambda k, c: ((k + 2 * c[0]) % 4, 0)),
                pl.BlockSpec((block, three * part), lambda k, c: (jnp.minimum(k, 1), 0)),
            ],
        ),
        compiler_params=pltpu.CompilerParams(vmem_limit_bytes=32 * 1024 * 1024),
        name="flatten_qkv",
    )(core[None].astype(jnp.int32), matrix)


def reduce_vector(own, other):
    total = own + flip(other)
    mask = 1
    while mask < lax.axis_size("dp"):
        total = total + hop(total, mask)
        mask *= 2
    return total


def normalize(resid, gain, shift):
    average = jnp.mean(resid, -1, keepdims=True)
    centred = resid - average
    inverse = lax.rsqrt(jnp.mean(centred * centred, -1, keepdims=True) + epsilon)
    scaled = centred * inverse
    return (scaled * gain + shift, scaled, inverse)


def norm_back(grad_rows, gain, scaled, inverse):
    weighted = grad_rows * gain
    back = inverse * (
        weighted
        - jnp.mean(weighted, -1, keepdims=True)
        - scaled * jnp.mean(weighted * scaled, -1, keepdims=True)
    )
    return (back, jnp.sum(grad_rows * scaled, 0), jnp.sum(grad_rows, 0))


def head_lanes(shape, head):
    return (lax.broadcasted_iota(jnp.int32, shape, 1) >= HS) == (head == 1)


def only_head(rows, head):
    return jnp.where(head_lanes(rows.shape, head), rows, jnp.zeros_like(rows))


def attend_kernel(length_ref, query_ref, key_ref, value_ref, out_ref):
    total = query_ref.shape[0]
    length = length_ref[pl.program_id(0)]
    step = min(total, 256)
    block = min(total, 128)

    def with_keys(count):
        keys, values = key_ref[:count, :], value_ref[:count, :]
        valid = lax.broadcasted_iota(jnp.int32, (1, count), 1) < length
        for at in range(0, total, step):
            query = query_ref[at : at + step, :] * jnp.bfloat16(0.125)
            parts = []
            for head in range(2):
                scores = jnp.where(valid, dot_t(only_head(query, head), keys), -1000000000.0)
                shifted = jnp.exp(scores - jnp.max(scores, -1, keepdims=True))
                probs = shifted * (1.0 / jnp.sum(shifted, -1, keepdims=True))
                parts.append(dot(probs.astype(bf16), values))
            out_ref[at : at + step, :] = jnp.where(head_lanes(parts[0].shape, 0), *parts).astype(bf16)

    @pl.when(length == 0)
    def _():
        average = jnp.sum(value_ref[...].astype(f32), 0, keepdims=True) * (1.0 / total)
        out_ref[...] = jnp.broadcast_to(average, out_ref.shape).astype(bf16)

    for count in range(block, total + 1, block):
        pl.when((length > count - block) & (length <= count))(lambda count=count: with_keys(count))


def attend(qkv, own_len):
    tokens, width = qkv.shape[0], qkv.shape[1] // 3
    seqs = own_len.shape[0]
    length, pairs = tokens // seqs, width // (2 * HS)
    block = (length, 2 * HS)
    return pl.pallas_call(
        attend_kernel,
        out_shape=jax.ShapeDtypeStruct((tokens, width), bf16),
        grid_spec=pltpu.PrefetchScalarGridSpec(
            num_scalar_prefetch=1,
            grid=(seqs, pairs),
            in_specs=[pl.BlockSpec(block, lambda s, p, _, c=c: (s, c * pairs + p)) for c in range(3)],
            out_specs=pl.BlockSpec(block, lambda s, p, _: (s, p)),
        ),
        compiler_params=pltpu.CompilerParams(vmem_limit_bytes=48 * 1024 * 1024),
        cost_estimate=pl.CostEstimate(
            flops=seqs * pairs * length * length * 512, bytes_accessed=tokens * width * 8, transcendentals=0
        ),
        name="attend",
    )(own_len, qkv, qkv, qkv)


def attend_back_kernel(length_ref, query_ref, key_ref, value_ref, g_out_ref, out_ref):
    total = query_ref.shape[0]
    pairs = out_ref.shape[1] // (6 * HS)
    length = length_ref[pl.program_id(0)]
    pair = pl.program_id(1)
    block = min(total, 128)
    lanes = [pl.ds(pl.multiple_of((c * pairs + pair) * 2 * HS, 2 * HS), 2 * HS) for c in range(3)]

    def with_keys(count):
        keys, values = key_ref[:count, :], value_ref[:count, :]
        valid = lax.broadcasted_iota(jnp.int32, (count, 1), 0) < length
        step = min(count, 256)
        starts = list(range(0, count, step))
        g_key = jnp.zeros((count, 2 * HS), f32)
        g_value = jnp.zeros((count, 2 * HS), f32)
        for at in starts:
            end = min(at + step, count)
            query = query_ref[at:end, :] * jnp.bfloat16(0.125)
            g_out = g_out_ref[at:end, :]
            g_query = jnp.zeros((end - at, 2 * HS), f32)
            for head in range(2):
                query_head, g_head = only_head(query, head), only_head(g_out, head)
                scores = jnp.where(valid, dot_t(keys, query_head), -1000000000.0)
                shifted = jnp.exp(scores - jnp.max(scores, 0, keepdims=True))
                probs = shifted * (1.0 / jnp.sum(shifted, 0, keepdims=True))
                g_probs = dot_t(values, g_head)
                delta = jnp.sum(g_probs * probs, 0, keepdims=True)
                g_scores = (probs * (g_probs - delta)).astype(bf16)
                g_key = g_key + dot(g_scores, query_head)
                g_value = g_value + dot(probs.astype(bf16), g_head)
                g_query = g_query + t_dot(g_scores, only_head(keys, head))
            out_ref[at:end, lanes[0]] = (g_query * 0.125).astype(bf16)
        out_ref[:count, lanes[1]] = g_key.astype(bf16)
        out_ref[:count, lanes[2]] = g_value.astype(bf16)
        if count < total:
            for c in range(3):
                out_ref[count:, lanes[c]] = jnp.zeros((total - count, 2 * HS), bf16)

    @pl.when(length == 0)
    def _():
        for c in range(3):
            out_ref[:, lanes[c]] = jnp.zeros((total, 2 * HS), bf16)

    for count in range(block, total + 1, block):
        pl.when((length > count - block) & (length <= count))(lambda count=count: with_keys(count))


def attend_back(qkv, g_out, own_len):
    tokens, width = g_out.shape
    seqs = own_len.shape[0]
    length, pairs = tokens // seqs, width // (2 * HS)
    block = (length, 2 * HS)
    return pl.pallas_call(
        attend_back_kernel,
        out_shape=jax.ShapeDtypeStruct((tokens, 3 * width), bf16),
        grid_spec=pltpu.PrefetchScalarGridSpec(
            num_scalar_prefetch=1,
            grid=(seqs, pairs),
            in_specs=[pl.BlockSpec(block, lambda s, p, _, c=c: (s, c * pairs + p)) for c in range(3)]
            + [pl.BlockSpec(block, lambda s, p, _: (s, p))],
            out_specs=pl.BlockSpec((length, 3 * width), lambda s, p, _: (s, 0)),
        ),
        compiler_params=pltpu.CompilerParams(vmem_limit_bytes=48 * 1024 * 1024),
        cost_estimate=pl.CostEstimate(
            flops=seqs * pairs * length * length * 1280, bytes_accessed=tokens * width * 14, transcendentals=0
        ),
        name="attend_back",
    )(own_len, qkv, qkv, qkv, g_out)


def dot(a, b):
    return jnp.dot(a, b, preferred_element_type=f32)


def dot_t(a, b):
    return lax.dot_general(a, b, (((1,), (1,)), ((), ())), preferred_element_type=f32)


def t_dot(a, b):
    return lax.dot_general(a, b, (((0,), (0,)), ((), ())), preferred_element_type=f32)


def gelu_both(inner):
    cumulative = 0.5 * (1.0 + lax.erf(inner * 0.7071067811865476))
    density = 0.3989422804014327 * jnp.exp(-0.5 * inner * inner)
    return inner * cumulative, cumulative + inner * density


def body(
    hidden_in, seq_lengths, live_seqs, out_grad, query_key_value_matrix, query_bias, value_bias,
    projection_matrix, proj_bias, norm1_gain, norm1_shift, up_matrix, up_bias, down_matrix,
    down_bias, norm2_gain, norm2_shift,
):
    seq_count, length, features = hidden_in.shape
    width = query_key_value_matrix.shape[2]
    heads = width // HS
    tokens = seq_count * length
    gain_one, shift_one = norm1_gain.astype(f32), norm1_shift.astype(f32)
    gain_two, shift_two = norm2_gain.astype(f32), norm2_shift.astype(f32)
    side = lax.axis_index("tensor")
    own_len = lax.dynamic_slice_in_dim(seq_lengths, side * seq_count, seq_count)
    owned = lax.dynamic_index_in_dim(live_seqs, side, 0, keepdims=False)
    own_len = jnp.where(lax.iota(jnp.int32, seq_count) < owned, own_len, 0)

    x = hidden_in.reshape(tokens, features)
    core, quarter = lax.axis_index("dp") & 1, lax.axis_index("dp") & 3
    qkv_w, qkv_sent = flatten_qkv(query_key_value_matrix, core)
    biases = jnp.concatenate([query_bias, value_bias, up_bias])
    biases_o = flip(biases)
    qkv_get = Gather(qkv_sent, False)
    proj_get = Gather(pick(projection_matrix, 4, quarter), True)
    up_get = Gather(pick(up_matrix, 4, quarter), True)
    down_get = Gather(pick(down_matrix, 4, quarter), True)

    def project(weight, bias):
        bias = jnp.concatenate([bias[:width], jnp.zeros((width,), bias.dtype), bias[width : 2 * width]])
        return (dot(x, weight) + bias.astype(f32)).astype(bf16)

    qkv_rows = [project(qkv_w, biases)]
    attended = [attend(qkv_rows[0], own_len)]
    attended[0] = tie(attended[0], qkv_get, proj_get)
    qkv_get.cores()
    proj_get.beside()
    qkv_o = qkv_get.finish()
    qkv_rows.append(project(qkv_o, biases_o))
    qkv_rows[1] = tie(qkv_rows[1], proj_get, up_get)
    proj_get.cores()
    up_get.beside()
    attended.append(attend(qkv_rows[1], own_len))
    attended[1] = tie(attended[1], proj_get, up_get, down_get)
    up_get.cores()
    down_get.beside()
    proj_o = proj_get.finish()
    projs = [projection_matrix, proj_o]
    up_biases = [biases[2 * width :].astype(f32), biases_o[2 * width :].astype(f32)]
    branch = dot(attended[0], projs[0]) + dot(attended[1], projs[1])
    resid_one = x.astype(f32) + branch + proj_bias.astype(f32)
    normed_one, scaled_one, inverse_one = normalize(resid_one, gain_one, shift_one)
    normed_low = normed_one.astype(bf16)
    normed_low = tie(normed_low, up_get)
    ups = [up_matrix, up_get.finish()]
    activated, slopes = [], []
    for k in range(2):
        act, slope = gelu_both(dot(normed_low, ups[k]) + up_biases[k])
        activated.append(act.astype(bf16))
        slopes.append(slope.astype(bf16))
        if k == 0:
            normed_low = tie(normed_low, down_get)
            down_get.cores()
    downs = [down_matrix, down_get.finish()]
    branch = dot(activated[0], downs[0]) + dot(activated[1], downs[1])
    resid_two = normed_one + branch + down_bias.astype(f32)
    normed_two, scaled_two, inverse_two = normalize(resid_two, gain_two, shift_two)
    out_hidden = normed_two.astype(bf16).reshape(hidden_in.shape)

    live = lax.iota(jnp.int32, length)[None, :] < own_len[:, None]
    out_back = jnp.where(live[:, :, None], out_grad.astype(f32), 0.0).reshape(tokens, features)
    g_resid_two, grad_gain_two, grad_shift_two = norm_back(out_back, gain_two, scaled_two, inverse_two)
    grad_down_bias = jnp.sum(g_resid_two, 0)
    g_mlp = g_resid_two.astype(bf16)
    down_sum, up_sum, proj_sum, qkv_sum = Reduction(), Reduction(), Reduction(), Reduction()
    groups = down_sum.groups
    last = len(groups) - 1
    down_sum.cores(*[t_dot(act, g_mlp).astype(bf16) for act in activated])
    g_pre = [(dot_t(g_mlp, downs[k]) * slopes[k].astype(f32)).astype(bf16) for k in range(2)]
    g_pre[0] = tie(g_pre[0], down_sum)
    down_sum.sides()
    up_sum.cores(*[t_dot(normed_low, g).astype(bf16) for g in g_pre])
    grad_up_bias = [jnp.sum(g.astype(f32), 0) for g in g_pre]
    g_normed = g_resid_two + dot_t(g_pre[0], ups[0]) + dot_t(g_pre[1], ups[1])
    g_resid_one, grad_gain_one, grad_shift_one = norm_back(g_normed, gain_one, scaled_one, inverse_one)
    grad_proj_bias = jnp.sum(g_resid_one, 0)
    g_attn = g_resid_one.astype(bf16)
    g_attn = tie(g_attn, up_sum)
    up_sum.sides()
    proj_sum.cores(*[t_dot(rows, g_attn).astype(bf16) for rows in attended])
    g_att = [dot_t(g_attn, projs[k]).astype(bf16) for k in range(2)]
    g_att[1] = tie(g_att[1], proj_sum)
    proj_sum.sides()
    g_qkv_o = attend_back(qkv_rows[1], g_att[1], own_len)
    g_qkv_o = tie(g_qkv_o, down_sum)
    down_sum.scatter(groups[1])
    q_grad_o = t_dot(x, g_qkv_o).astype(bf16)
    g_att[0] = tie(g_att[0], down_sum)
    for group in groups[2:]:
        down_sum.scatter(group)
    g_qkv = attend_back(qkv_rows[0], g_att[0], own_len)
    g_qkv = [g_qkv, g_qkv_o]
    g_qkv[0] = tie(g_qkv[0], down_sum, up_sum)
    qkv_sum.cores(t_dot(x, g_qkv[0]).astype(bf16), q_grad_o)
    sums = [jnp.sum(g.astype(f32), 0) for g in g_qkv]
    grad_hidden = (g_resid_one + dot_t(g_qkv[0], qkv_w) + dot_t(g_qkv[1], qkv_o)).astype(bf16)
    qkv_sum.sides()
    for group in groups[1:]:
        up_sum.scatter(group)
    for k in range(last, -1, -1):
        down_sum.gather(k)
    down_grad = down_sum.finish()
    for k in range(last, -1, -1):
        up_sum.gather(k)
    up_grad = up_sum.finish()
    proj_grad = proj_sum.rest()
    qkv_grad = qkv_sum.rest(3)
    shared = [grad_proj_bias, grad_gain_one, grad_shift_one, grad_down_bias, grad_gain_two, grad_shift_two]
    vector = reduce_vector(
        *[jnp.concatenate(shared + [sums[k][:width], sums[k][2 * width :], grad_up_bias[k]]) for k in range(2)]
    )
    cuts = [features * k for k in range(1, 7)] + [6 * features + width, 6 * features + 2 * width]
    vector = jnp.split(vector, cuts)
    return (
        out_hidden,
        grad_hidden.reshape(hidden_in.shape),
        qkv_grad,
        vector[6],
        vector[7],
        proj_grad,
        vector[0],
        vector[1],
        vector[2],
        up_grad,
        vector[8],
        down_grad,
        vector[3],
        vector[4],
        vector[5],
    )


def solution(mesh):
    rows = P(("dp", "tensor"), None, None)
    placed = (
        rows, P("dp"), P("dp"), rows, P(None, None, "tensor"), P("tensor"), P("tensor"),
        P("tensor", None), P(), P(), P(), P(None, "tensor"), P("tensor"), P("tensor", None),
        P(), P(), P(),
    )
    outs = (
        rows, rows, P(None, None, "tensor"), P("tensor"), P("tensor"), P("tensor", None), P(), P(),
        P(), P(None, "tensor"), P("tensor"), P("tensor", None), P(), P(), P(),
    )
    return jax.shard_map(body, mesh=mesh, in_specs=placed, out_specs=outs, check_vma=False)
```

```python
import jax
import jax.numpy as jnp
from jax import lax
from jax.experimental import pallas as pl
from jax.experimental.pallas import tpu as pltpu
from jax.sharding import PartitionSpec as P

HS = 64
epsilon = 1e-06
f32 = jnp.float32
bf16 = jnp.bfloat16


def flip(value):
    return lax.ppermute(value, "tensor", [(0, 1), (1, 0)])


def hop(value, mask):
    count = lax.axis_size("dp")
    return lax.ppermute(value, "dp", [(i, i ^ mask) for i in range(count)])


def dp_groups():
    count = lax.axis_size("dp")
    bits = count.bit_length() - 1
    groups, at = [], 0
    for width in [1, 1] + [2] * bits:
        width = min(width, bits - at)
        if width > 0:
            groups.append((at, width))
        at += width
    return groups


def member(group):
    at, width = group
    return (lax.axis_index("dp") >> at) & ((1 << width) - 1)


def pick(rows, pieces, which):
    count, width = rows.shape
    return lax.dynamic_index_in_dim(rows.reshape(pieces, count // pieces, width), which, 0, keepdims=False)


def tie(values, *holders):
    arrays = list(values) + [array for holder in holders for array in holder.came]
    arrays = list(lax.optimization_barrier(tuple(arrays)))
    at = len(values)
    for holder in holders:
        holder.came = arrays[at : at + len(holder.came)]
        at += len(holder.came)
    return arrays[: len(values)]


def by_bit(bit, zero, one):
    return jnp.where(bit == 0, zero, one)


class Gather:
    def __init__(self, sent, spread):
        self.spread = spread
        self.came = [flip(sent)]

    def beside(self):
        row = member((1, 1))
        (mine,) = self.came
        (other,) = self.came = [hop(mine, 2)]
        self.mine = mine

    def cores(self):
        if self.spread:
            row = member((1, 1))
            (other,) = self.came
            self.parts = [by_bit(row, self.mine, other), by_bit(row, other, self.mine)]
        else:
            self.parts = self.came
        self.came = [hop(part, 1) for part in self.parts]

    def finish(self):
        core = member((0, 1))
        rows = []
        for mine, other in zip(self.parts, self.came):
            rows += [by_bit(core, mine, other), by_bit(core, other, mine)]
        return jnp.concatenate(rows, 0)


class Reduction:
    def __init__(self):
        self.groups = dp_groups()

    def other_cores(self, other):
        self.core = member(self.groups[0])
        self.other = other
        self.came = [hop(pick(other, 2, 1 - self.core), 1)]

    def own_cores(self, own):
        self.own = own
        self.came = self.came + [hop(pick(own, 2, 1 - self.core), 1)]

    def cores(self, own, other):
        self.other_cores(other)
        self.own_cores(own)

    def sides(self):
        away = pick(self.other, 2, self.core).astype(f32) + self.came[0].astype(f32)
        self.total = pick(self.own, 2, self.core).astype(f32) + self.came[1].astype(f32)
        self.came = [flip(away.astype(bf16))]

    def settle(self):
        for rows in self.came:
            self.total = self.total + rows.astype(f32)

    def scatter(self, group):
        self.settle()
        at, width = group
        pieces, me = 1 << width, member(group)
        low = self.total.astype(bf16)
        self.came = [hop(pick(low, pieces, me ^ j), j << at) for j in range(1, pieces)]
        self.total = pick(self.total, pieces, me)

    def gather(self, k):
        if k == len(self.groups) - 1:
            self.settle()
            self.result = self.total.astype(bf16)
        else:
            self.result = assemble([self.result] + self.came, member(self.groups[k + 1]), bf16)
        at, width = self.groups[k]
        self.came = [hop(self.result, j << at) for j in range(1, 1 << width)]

    def finish(self):
        return assemble([self.result] + self.came, self.core, f32)


def assemble(slots, me, dtype):
    count = len(slots)
    rows, width = slots[0].shape

    def kernel(me_ref, *refs):
        step = pl.program_id(0) ^ me_ref[0]
        for j in range(count):

            @pl.when(step == j)
            def _():
                refs[-1][0] = refs[j][...].astype(dtype)

    out = pl.pallas_call(
        kernel,
        out_shape=jax.ShapeDtypeStruct((count, rows, width), dtype),
        grid_spec=pltpu.PrefetchScalarGridSpec(
            num_scalar_prefetch=1,
            grid=(count,),
            in_specs=[pl.BlockSpec((rows, width), lambda k, _: (0, 0)) for _ in slots],
            out_specs=pl.BlockSpec((1, rows, width), lambda k, _: (k, 0, 0)),
        ),
        compiler_params=pltpu.CompilerParams(vmem_limit_bytes=48 * 1024 * 1024),
        cost_estimate=pl.CostEstimate(flops=0, bytes_accessed=count * rows * width * 6, transcendentals=0),
        name="assemble",
    )(me[None].astype(jnp.int32), *slots)
    return out.reshape(count * rows, width)


class VectorSum:
    def __init__(self, own, other):
        self.total, self.mask = own, 1
        self.came = [flip(other)]

    def hop(self):
        if self.mask < lax.axis_size("dp"):
            self.total = self.total + self.came[0]
            self.came = [hop(self.total, self.mask)]
            self.mask *= 2

    def finish(self):
        while self.mask < lax.axis_size("dp"):
            self.hop()
        return self.total + self.came[0]


def stack_rows(vectors, features):
    count = -(-len(vectors) // 8) * 8
    place = lax.broadcasted_iota(jnp.int32, (count, features), 0)
    out = jnp.zeros((count, features), f32)
    for k, vector in enumerate(vectors):
        out = jnp.where(place == k, vector[None, :], out)
    return out


def normalize(resid, gain, shift):
    average = jnp.mean(resid, -1, keepdims=True)
    centred = resid - average
    inverse = lax.rsqrt(jnp.mean(centred * centred, -1, keepdims=True) + epsilon)
    scaled = centred * inverse
    return (scaled * gain + shift, scaled, inverse)


def norm_back(grad_rows, gain, scaled, inverse):
    weighted = grad_rows * gain
    back = inverse * (
        weighted
        - jnp.mean(weighted, -1, keepdims=True)
        - scaled * jnp.mean(weighted * scaled, -1, keepdims=True)
    )
    return (back, jnp.sum(grad_rows * scaled, 0), jnp.sum(grad_rows, 0))


def head_lanes(shape, head):
    return (lax.broadcasted_iota(jnp.int32, shape, 1) >= HS) == (head == 1)


def only_head(rows, head):
    return jnp.where(head_lanes(rows.shape, head), rows, jnp.zeros_like(rows))


def attend_kernel(length_ref, query_ref, key_ref, value_ref, out_ref):
    total = query_ref.shape[0]
    length = length_ref[pl.program_id(0)]
    step = min(total, 256)
    block = min(total, 128)

    def with_keys(count):
        keys, values = key_ref[:count, :], value_ref[:count, :]
        valid = lax.broadcasted_iota(jnp.int32, (1, count), 1) < length
        for at in range(0, total, step):
            query = query_ref[at : at + step, :] * jnp.bfloat16(0.125)
            parts = []
            for head in range(2):
                scores = jnp.where(valid, dot_t(only_head(query, head), keys), -1000000000.0)
                shifted = jnp.exp(scores - jnp.max(scores, -1, keepdims=True))
                probs = shifted * (1.0 / jnp.sum(shifted, -1, keepdims=True))
                parts.append(dot(probs.astype(bf16), values))
            out_ref[at : at + step, :] = jnp.where(head_lanes(parts[0].shape, 0), *parts).astype(bf16)

    @pl.when(length == 0)
    def _():
        average = jnp.sum(value_ref[...].astype(f32), 0, keepdims=True) * (1.0 / total)
        out_ref[...] = jnp.broadcast_to(average, out_ref.shape).astype(bf16)

    for count in range(block, total + 1, block):
        pl.when((length > count - block) & (length <= count))(lambda count=count: with_keys(count))


def attend(qkv, own_len):
    _, tokens, width = qkv.shape
    seqs = own_len.shape[0]
    length, pairs = tokens // seqs, width // (2 * HS)
    block = (length, 2 * HS)
    return pl.pallas_call(
        attend_kernel,
        out_shape=jax.ShapeDtypeStruct((tokens, width), bf16),
        grid_spec=pltpu.PrefetchScalarGridSpec(
            num_scalar_prefetch=1,
            grid=(seqs, pairs),
            in_specs=[pl.BlockSpec((None,) + block, lambda s, p, _, c=c: (c, s, p)) for c in range(3)],
            out_specs=pl.BlockSpec(block, lambda s, p, _: (s, p)),
        ),
        compiler_params=pltpu.CompilerParams(vmem_limit_bytes=48 * 1024 * 1024),
        cost_estimate=pl.CostEstimate(
            flops=seqs * pairs * length * length * 512, bytes_accessed=tokens * width * 8, transcendentals=0
        ),
        name="attend",
    )(own_len, qkv, qkv, qkv)


def attend_back_kernel(length_ref, query_ref, key_ref, value_ref, g_out_ref, out_ref):
    total = query_ref.shape[0]
    length = length_ref[pl.program_id(0)]
    pair = pl.program_id(1)
    block = min(total, 128)
    lanes = pl.ds(pl.multiple_of(pair * 2 * HS, 2 * HS), 2 * HS)

    def with_keys(count):
        keys, values = key_ref[:count, :], value_ref[:count, :]
        valid = lax.broadcasted_iota(jnp.int32, (count, 1), 0) < length
        step = min(count, 256)
        starts = list(range(0, count, step))
        g_key = jnp.zeros((count, 2 * HS), f32)
        g_value = jnp.zeros((count, 2 * HS), f32)
        for at in starts:
            end = min(at + step, count)
            query = query_ref[at:end, :] * jnp.bfloat16(0.125)
            g_out = g_out_ref[at:end, :]
            g_query = jnp.zeros((end - at, 2 * HS), f32)
            for head in range(2):
                query_head, g_head = only_head(query, head), only_head(g_out, head)
                scores = jnp.where(valid, dot_t(keys, query_head), -1000000000.0)
                shifted = jnp.exp(scores - jnp.max(scores, 0, keepdims=True))
                probs = shifted * (1.0 / jnp.sum(shifted, 0, keepdims=True))
                g_probs = dot_t(values, g_head)
                delta = jnp.sum(g_probs * probs, 0, keepdims=True)
                g_scores = (probs * (g_probs - delta)).astype(bf16)
                g_key = g_key + dot(g_scores, query_head)
                g_value = g_value + dot(probs.astype(bf16), g_head)
                g_query = g_query + t_dot(g_scores, only_head(keys, head))
            out_ref[0, at:end, lanes] = (g_query * 0.125).astype(bf16)
        out_ref[1, :count, lanes] = g_key.astype(bf16)
        out_ref[2, :count, lanes] = g_value.astype(bf16)
        if count < total:
            for c in range(3):
                out_ref[c, count:, lanes] = jnp.zeros((total - count, 2 * HS), bf16)

    @pl.when(length == 0)
    def _():
        for c in range(3):
            out_ref[c, :, lanes] = jnp.zeros((total, 2 * HS), bf16)

    for count in range(block, total + 1, block):
        pl.when((length > count - block) & (length <= count))(lambda count=count: with_keys(count))


def attend_back(qkv, g_out, own_len):
    tokens, width = g_out.shape
    seqs = own_len.shape[0]
    length, pairs = tokens // seqs, width // (2 * HS)
    block = (length, 2 * HS)
    return pl.pallas_call(
        attend_back_kernel,
        out_shape=jax.ShapeDtypeStruct((3, tokens, width), bf16),
        grid_spec=pltpu.PrefetchScalarGridSpec(
            num_scalar_prefetch=1,
            grid=(seqs, pairs),
            in_specs=[pl.BlockSpec((None,) + block, lambda s, p, _, c=c: (c, s, p)) for c in range(3)]
            + [pl.BlockSpec(block, lambda s, p, _: (s, p))],
            out_specs=pl.BlockSpec((3, length, width), lambda s, p, _: (0, s, 0)),
        ),
        compiler_params=pltpu.CompilerParams(vmem_limit_bytes=48 * 1024 * 1024),
        cost_estimate=pl.CostEstimate(
            flops=seqs * pairs * length * length * 1280, bytes_accessed=tokens * width * 14, transcendentals=0
        ),
        name="attend_back",
    )(own_len, qkv, qkv, qkv, g_out)


def dot(a, b):
    return jnp.dot(a, b, preferred_element_type=f32)


def dot_t(a, b):
    return lax.dot_general(a, b, (((1,), (1,)), ((), ())), preferred_element_type=f32)


def t_dot(a, b):
    return lax.dot_general(a, b, (((0,), (0,)), ((), ())), preferred_element_type=f32)


def gelu_both(inner):
    cumulative = 0.5 * (1.0 + lax.erf(inner * 0.7071067811865476))
    density = 0.3989422804014327 * jnp.exp(-0.5 * inner * inner)
    return inner * cumulative, cumulative + inner * density


def body(
    hidden_in, seq_lengths, live_seqs, out_grad, query_key_value_matrix, query_bias, value_bias,
    projection_matrix, proj_bias, norm1_gain, norm1_shift, up_matrix, up_bias, down_matrix,
    down_bias, norm2_gain, norm2_shift,
):
    seq_count, length, features = hidden_in.shape
    width = query_key_value_matrix.shape[2]
    heads = width // HS
    tokens = seq_count * length
    gain_one, shift_one = norm1_gain.astype(f32), norm1_shift.astype(f32)
    gain_two, shift_two = norm2_gain.astype(f32), norm2_shift.astype(f32)
    side = lax.axis_index("tensor")
    own_len = lax.dynamic_slice_in_dim(seq_lengths, side * seq_count, seq_count)
    owned = lax.dynamic_index_in_dim(live_seqs, side, 0, keepdims=False)
    own_len = jnp.where(lax.iota(jnp.int32, seq_count) < owned, own_len, 0)

    x = hidden_in.reshape(tokens, features)
    core, quarter = lax.axis_index("dp") & 1, lax.axis_index("dp") & 3
    biases = jnp.concatenate([query_bias, value_bias, up_bias])
    biases_o = flip(biases)
    qkv_w = query_key_value_matrix.transpose(1, 0, 2).reshape(3 * features, width)
    proj_get = Gather(pick(projection_matrix, 4, quarter), True)
    qkv_get = Gather(pick(qkv_w, 2, core), False)
    up_get = Gather(pick(up_matrix, 4, quarter), True)
    down_get = Gather(pick(down_matrix, 4, quarter), True)

    def project(weight, bias):
        bias = jnp.stack([bias[:width], jnp.zeros((width,), bias.dtype), bias[width : 2 * width]])
        rows = jnp.einsum("tv,cvw->ctw", x, weight.reshape(3, features, width), preferred_element_type=f32)
        return (rows + bias.astype(f32)[:, None, :]).astype(bf16)

    qkv_rows = [project(qkv_w, biases)]
    attended = [attend(qkv_rows[0], own_len)]
    attended = tie(attended, qkv_get, proj_get, up_get)
    qkv_get.cores()
    proj_get.beside()
    up_get.beside()
    qkv_o = qkv_get.finish()
    qkv_rows.append(project(qkv_o, biases_o))
    qkv_rows = tie(qkv_rows, proj_get, down_get)
    proj_get.cores()
    down_get.beside()
    attended.append(attend(qkv_rows[1], own_len))
    attended = tie(attended, proj_get, up_get)
    up_get.cores()
    projs = [projection_matrix, proj_get.finish()]
    up_biases = [biases[2 * width :].astype(f32), biases_o[2 * width :].astype(f32)]
    branch = dot(attended[0], projs[0]) + dot(attended[1], projs[1])
    resid_one = x.astype(f32) + branch + proj_bias.astype(f32)
    normed_one, scaled_one, inverse_one = normalize(resid_one, gain_one, shift_one)
    normed_low = normed_one.astype(bf16)
    (normed_low,) = tie([normed_low], up_get, down_get)
    down_get.cores()
    ups = [up_matrix, up_get.finish()]
    activated, slopes = [], []
    for k in range(2):
        act, slope = gelu_both(dot(normed_low, ups[k]) + up_biases[k])
        activated.append(act.astype(bf16))
        slopes.append(slope.astype(bf16))
    downs = [down_matrix, down_get.finish()]
    branch = dot(activated[0], downs[0]) + dot(activated[1], downs[1])
    resid_two = normed_one + branch + down_bias.astype(f32)
    normed_two, scaled_two, inverse_two = normalize(resid_two, gain_two, shift_two)
    out_hidden = normed_two.astype(bf16).reshape(hidden_in.shape)

    live = lax.iota(jnp.int32, length)[None, :] < own_len[:, None]
    out_back = jnp.where(live[:, :, None], out_grad.astype(f32), 0.0).reshape(tokens, features)
    g_resid_two, grad_gain_two, grad_shift_two = norm_back(out_back, gain_two, scaled_two, inverse_two)
    grad_down_bias = jnp.sum(g_resid_two, 0)
    g_mlp = g_resid_two.astype(bf16)
    down_sum, up_sum, proj_sum, qkv_sum = Reduction(), Reduction(), Reduction(), Reduction()
    groups = down_sum.groups
    last = len(groups) - 1
    down_sum.cores(*[t_dot(act, g_mlp).astype(bf16) for act in activated])
    g_pre = [(dot_t(g_mlp, downs[k]) * slopes[k].astype(f32)).astype(bf16) for k in range(2)]
    g_pre = tie(g_pre, down_sum)
    down_sum.sides()
    up_sum.cores(*[t_dot(normed_low, g).astype(bf16) for g in g_pre])
    grad_up_bias = [jnp.sum(g.astype(f32), 0) for g in g_pre]
    g_normed = g_resid_two + dot_t(g_pre[0], ups[0]) + dot_t(g_pre[1], ups[1])
    g_resid_one, grad_gain_one, grad_shift_one = norm_back(g_normed, gain_one, scaled_one, inverse_one)
    grad_proj_bias = jnp.sum(g_resid_one, 0)
    g_attn = g_resid_one.astype(bf16)
    (g_attn,) = tie([g_attn], up_sum)
    proj_sum.cores(*[t_dot(rows, g_attn).astype(bf16) for rows in attended])
    g_att = [dot_t(g_attn, projs[k]).astype(bf16) for k in range(2)]
    g_qkv_o = attend_back(qkv_rows[1], g_att[1], own_len)
    (g_qkv_o,) = tie([g_qkv_o], proj_sum, down_sum)
    down_sum.scatter(groups[1])
    up_sum.sides()
    proj_sum.sides()

    def weight_grad(g):
        return jnp.einsum("tv,ctw->cvw", x, g, preferred_element_type=f32).astype(bf16).reshape(-1, width)

    qkv_sum.other_cores(weight_grad(g_qkv_o))
    g_att = tie(g_att, qkv_sum)
    g_qkv = [attend_back(qkv_rows[0], g_att[0], own_len), g_qkv_o]
    g_qkv = tie(g_qkv, down_sum)
    down_sum.scatter(groups[2])
    qkv_sum.own_cores(weight_grad(g_qkv[0]))
    sums = [jnp.sum(g.astype(f32), 1) for g in g_qkv]
    shared = [grad_proj_bias, grad_gain_one, grad_shift_one, grad_down_bias, grad_gain_two, grad_shift_two]
    ups_rows = up_bias.shape[0] // features
    vectors = []
    for k in range(2):
        up_rows = [grad_up_bias[k][r * features : (r + 1) * features] for r in range(ups_rows)]
        vectors.append(stack_rows(shared + up_rows + [jnp.concatenate([sums[k][0], sums[k][2]])], features))
    qkv_w3, qkv_o3 = [w.reshape(3, features, width) for w in (qkv_w, qkv_o)]
    grad_hidden = (
        g_resid_one
        + jnp.einsum("ctw,cvw->tv", g_qkv[0], qkv_w3, preferred_element_type=f32)
        + jnp.einsum("ctw,cvw->tv", g_qkv[1], qkv_o3, preferred_element_type=f32)
    ).astype(bf16)
    for group in groups[3:]:
        down_sum.scatter(group)

    def step(*holders):
        tie([], *holders)

    (grad_hidden,) = tie([grad_hidden], up_sum, proj_sum, down_sum, qkv_sum)
    qkv_sum.sides()
    up_sum.scatter(groups[1])
    proj_sum.settle()
    proj_half = proj_sum.total.astype(bf16)
    proj_total = lax.psum(jnp.concatenate([proj_half * (core == k).astype(bf16) for k in range(2)], 0), "dp")
    down_sum.gather(last)
    step(up_sum, down_sum)
    for group in groups[2:]:
        up_sum.scatter(group)
    down_sum.gather(last - 1)
    vector_sum = VectorSum(*vectors)
    step(qkv_sum, up_sum, down_sum, vector_sum)
    qkv_sum.scatter(groups[1])
    up_sum.gather(last)
    for k in range(last - 2, -1, -1):
        down_sum.gather(k)
    vector_sum.hop()
    step(qkv_sum, up_sum, down_sum, vector_sum)
    down_grad = down_sum.finish()
    for group in groups[2:]:
        qkv_sum.scatter(group)
    up_sum.gather(last - 1)
    vector_sum.hop()
    step(qkv_sum, up_sum, vector_sum)
    qkv_sum.gather(last)
    for k in range(last - 2, -1, -1):
        up_sum.gather(k)
    vector_sum.hop()
    step(qkv_sum, up_sum, vector_sum)
    qkv_sum.gather(last - 1)
    up_grad = up_sum.finish()
    vector_sum.hop()
    step(qkv_sum, vector_sum)
    for k in range(last - 2, -1, -1):
        qkv_sum.gather(k)
    vector = vector_sum.finish()
    qkv_grad = qkv_sum.finish()
    proj_grad = proj_total.astype(f32)
    grad_hidden = grad_hidden.reshape(hidden_in.shape)
    return (
        out_hidden,
        grad_hidden,
        qkv_grad.reshape(3, features, width).transpose(1, 0, 2),
        vector[6 + ups_rows, :width],
        vector[6 + ups_rows, width:],
        proj_grad,
        vector[0],
        vector[1],
        vector[2],
        up_grad,
        vector[6 : 6 + ups_rows].reshape(-1),
        down_grad,
        vector[3],
        vector[4],
        vector[5],
    )


def solution(mesh):
    rows = P(("dp", "tensor"), None, None)
    placed = (
        rows, P("dp"), P("dp"), rows, P(None, None, "tensor"), P("tensor"), P("tensor"),
        P("tensor", None), P(), P(), P(), P(None, "tensor"), P("tensor"), P("tensor", None),
        P(), P(), P(),
    )
    outs = (
        rows, rows, P(None, None, "tensor"), P("tensor"), P("tensor"), P("tensor", None), P(), P(),
        P(), P(None, "tensor"), P("tensor"), P("tensor", None), P(), P(), P(),
    )
    return jax.shard_map(body, mesh=mesh, in_specs=placed, out_specs=outs, check_vma=False)
```

```python
import jax
import jax.numpy as jnp
from jax import lax
from jax.experimental import pallas as pl
from jax.experimental.pallas import tpu as pltpu
from jax.sharding import PartitionSpec as P

HS = 64
epsilon = 1e-06
f32 = jnp.float32
bf16 = jnp.bfloat16


def flip(value):
    return lax.ppermute(value, "tensor", [(0, 1), (1, 0)])


def hop(value, mask):
    count = lax.axis_size("dp")
    return lax.ppermute(value, "dp", [(i, i ^ mask) for i in range(count)])


def dp_groups():
    count = lax.axis_size("dp")
    bits = count.bit_length() - 1
    groups, at = [], 0
    for width in [1, 1] + [2] * bits:
        width = min(width, bits - at)
        if width > 0:
            groups.append((at, width))
        at += width
    return groups


def member(group):
    at, width = group
    return (lax.axis_index("dp") >> at) & ((1 << width) - 1)


def pick(rows, pieces, which):
    count, width = rows.shape
    return lax.dynamic_index_in_dim(rows.reshape(pieces, count // pieces, width), which, 0, keepdims=False)


def tie(values, *holders):
    arrays = list(values) + [array for holder in holders for array in holder.came]
    arrays = list(lax.optimization_barrier(tuple(arrays)))
    at = len(values)
    for holder in holders:
        holder.came = arrays[at : at + len(holder.came)]
        at += len(holder.came)
    return arrays[: len(values)]


def by_bit(bit, zero, one):
    return jnp.where(bit == 0, zero, one)


class Gather:
    def __init__(self, sent, spread):
        self.spread = spread
        self.came = [flip(sent)]

    def beside(self):
        row = member((1, 1))
        (mine,) = self.came
        (other,) = self.came = [hop(mine, 2)]
        self.mine = mine

    def cores(self):
        if self.spread:
            row = member((1, 1))
            (other,) = self.came
            self.parts = [by_bit(row, self.mine, other), by_bit(row, other, self.mine)]
        else:
            self.parts = self.came
        self.came = [hop(part, 1) for part in self.parts]

    def finish(self):
        core = member((0, 1))
        rows = []
        for mine, other in zip(self.parts, self.came):
            rows += [by_bit(core, mine, other), by_bit(core, other, mine)]
        return jnp.concatenate(rows, 0)


class Reduction:
    def __init__(self):
        self.groups = dp_groups()

    def cores(self, own, other):
        self.core = member(self.groups[0])
        self.keep = [other[0], own[0]]
        self.came = [hop(other[1], 1), hop(own[1], 1)]

    def join(self, reduction):
        width = self.keep[0].shape[1]

        def narrow(rows):
            return [rows[:, at : at + width] for at in range(0, rows.shape[1], width)]

        self.keep = [jnp.concatenate([a] + narrow(b), 0) for a, b in zip(self.keep, reduction.keep)]
        self.came = [jnp.concatenate([a] + narrow(b), 0) for a, b in zip(self.came, reduction.came)]

    def sides(self):
        away = self.keep[0].astype(f32) + self.came[0].astype(f32)
        self.total = self.keep[1].astype(f32) + self.came[1].astype(f32)
        self.came = [flip(away.astype(bf16))]

    def settle(self):
        for rows in self.came:
            self.total = self.total + rows.astype(f32)

    def scatter(self, group):
        self.settle()
        at, width = group
        pieces, me = 1 << width, member(group)
        low = self.total.astype(bf16)
        self.came = [hop(pick(low, pieces, me ^ j), j << at) for j in range(1, pieces)]
        self.total = pick(self.total, pieces, me)

    def gather(self, k):
        if k == len(self.groups) - 1:
            self.settle()
            self.result = self.total.astype(bf16)
        else:
            self.result = assemble([self.result] + self.came, member(self.groups[k + 1]), bf16)
        at, width = self.groups[k]
        self.came = [hop(self.result, j << at) for j in range(1, 1 << width)]

    def finish(self, **shape):
        return assemble([self.result] + self.came, self.core, f32, **shape)


def assemble(slots, me, dtype, planes=1, skip=0, width=None):
    count = len(slots)
    have = slots[0].shape[1]
    wide = 1 if width is None else width // have
    rows = (slots[0].shape[0] - skip if planes == 1 else slots[0].shape[0] // (planes + 1) * planes) // planes // wide
    if planes > 1:
        skip = 0

    def kernel(me_ref, *refs):
        step = pl.program_id(0) ^ me_ref[0]
        for j in range(count):

            @pl.when(step == j)
            def _():
                for plane in range(planes):
                    for part in range(wide):
                        at = skip + (plane * wide + part) * rows
                        refs[-1][plane, 0, :, part * have : (part + 1) * have] = refs[j][at : at + rows, :].astype(dtype)

    out = pl.pallas_call(
        kernel,
        out_shape=jax.ShapeDtypeStruct((planes, count, rows, wide * have), dtype),
        grid_spec=pltpu.PrefetchScalarGridSpec(
            num_scalar_prefetch=1,
            grid=(count,),
            in_specs=[pl.BlockSpec(slot.shape, lambda k, _: (0, 0)) for slot in slots],
            out_specs=pl.BlockSpec((planes, 1, rows, wide * have), lambda k, _: (0, k, 0, 0)),
        ),
        compiler_params=pltpu.CompilerParams(vmem_limit_bytes=48 * 1024 * 1024),
        cost_estimate=pl.CostEstimate(flops=0, bytes_accessed=count * rows * have * 6, transcendentals=0),
        name="assemble",
    )(me[None].astype(jnp.int32), *slots)
    return out.reshape(planes * count * rows, wide * have)


class VectorSum:
    def __init__(self, own, other):
        self.total, self.mask = own, 1
        self.came = [flip(other)]

    def hop(self):
        if self.mask < lax.axis_size("dp"):
            self.total = self.total + self.came[0]
            self.came = [hop(self.total, self.mask)]
            self.mask *= 2

    def finish(self):
        while self.mask < lax.axis_size("dp"):
            self.hop()
        return self.total + self.came[0]


def halves(rows, core):
    return pick(rows, 2, core), pick(rows, 2, 1 - core)


def stack_rows(vectors, features):
    count = -(-len(vectors) // 8) * 8
    place = lax.broadcasted_iota(jnp.int32, (count, features), 0)
    out = jnp.zeros((count, features), f32)
    for k, vector in enumerate(vectors):
        out = jnp.where(place == k, vector[None, :], out)
    return out


def normalize(resid, gain, shift):
    average = jnp.mean(resid, -1, keepdims=True)
    centred = resid - average
    inverse = lax.rsqrt(jnp.mean(centred * centred, -1, keepdims=True) + epsilon)
    scaled = centred * inverse
    return (scaled * gain + shift, scaled, inverse)


def head_lanes(shape, head):
    return (lax.broadcasted_iota(jnp.int32, shape, 1) >= HS) == (head == 1)


def only_head(rows, head):
    return jnp.where(head_lanes(rows.shape, head), rows, jnp.zeros_like(rows))


def attend_kernel(length_ref, query_ref, key_ref, value_ref, out_ref):
    total = query_ref.shape[0]
    length = length_ref[pl.program_id(0)]
    step = min(total, 256)
    block = min(total, 128)

    def with_keys(count):
        keys, values = key_ref[:count, :], value_ref[:count, :]
        valid = lax.broadcasted_iota(jnp.int32, (1, count), 1) < length
        for at in range(0, total, step):
            query = query_ref[at : at + step, :] * jnp.bfloat16(0.125)
            parts = []
            for head in range(2):
                scores = jnp.where(valid, dot_t(only_head(query, head), keys), -1000000000.0)
                shifted = jnp.exp(scores - jnp.max(scores, -1, keepdims=True))
                probs = shifted * (1.0 / jnp.sum(shifted, -1, keepdims=True))
                parts.append(dot(probs.astype(bf16), values))
            out_ref[at : at + step, :] = jnp.where(head_lanes(parts[0].shape, 0), *parts).astype(bf16)

    @pl.when(length == 0)
    def _():
        average = jnp.sum(value_ref[...].astype(f32), 0, keepdims=True) * (1.0 / total)
        out_ref[...] = jnp.broadcast_to(average, out_ref.shape).astype(bf16)

    for count in range(block, total + 1, block):
        pl.when((length > count - block) & (length <= count))(lambda count=count: with_keys(count))


def attend(qkv, own_len):
    _, tokens, width = qkv.shape
    seqs = own_len.shape[0]
    length, pairs = tokens // seqs, width // (2 * HS)
    block = (length, 2 * HS)
    return pl.pallas_call(
        attend_kernel,
        out_shape=jax.ShapeDtypeStruct((tokens, width), bf16),
        grid_spec=pltpu.PrefetchScalarGridSpec(
            num_scalar_prefetch=1,
            grid=(seqs, pairs),
            in_specs=[pl.BlockSpec((None,) + block, lambda s, p, _, c=c: (c, s, p)) for c in range(3)],
            out_specs=pl.BlockSpec(block, lambda s, p, _: (s, p)),
        ),
        compiler_params=pltpu.CompilerParams(vmem_limit_bytes=48 * 1024 * 1024),
        cost_estimate=pl.CostEstimate(
            flops=seqs * pairs * length * length * 512, bytes_accessed=tokens * width * 8, transcendentals=0
        ),
        name="attend",
    )(own_len, qkv, qkv, qkv)


def attend_back_kernel(length_ref, query_ref, key_ref, value_ref, g_out_ref, out_ref):
    total = query_ref.shape[0]
    length = length_ref[pl.program_id(0)]
    pair = pl.program_id(1)
    block = min(total, 128)
    lanes = pl.ds(pl.multiple_of(pair * 2 * HS, 2 * HS), 2 * HS)

    def with_keys(count):
        keys, values = key_ref[:count, :], value_ref[:count, :]
        valid = lax.broadcasted_iota(jnp.int32, (count, 1), 0) < length
        step = min(count, 256)
        starts = list(range(0, count, step))
        g_key = jnp.zeros((count, 2 * HS), f32)
        g_value = jnp.zeros((count, 2 * HS), f32)
        for at in starts:
            end = min(at + step, count)
            query = query_ref[at:end, :] * jnp.bfloat16(0.125)
            g_out = g_out_ref[at:end, :]
            g_query = jnp.zeros((end - at, 2 * HS), f32)
            for head in range(2):
                query_head, g_head = only_head(query, head), only_head(g_out, head)
                scores = jnp.where(valid, dot_t(keys, query_head), -1000000000.0)
                shifted = jnp.exp(scores - jnp.max(scores, 0, keepdims=True))
                probs = shifted * (1.0 / jnp.sum(shifted, 0, keepdims=True))
                g_probs = dot_t(values, g_head)
                delta = jnp.sum(g_probs * probs, 0, keepdims=True)
                g_scores = (probs * (g_probs - delta)).astype(bf16)
                g_key = g_key + dot(g_scores, query_head)
                g_value = g_value + dot(probs.astype(bf16), g_head)
                g_query = g_query + t_dot(g_scores, only_head(keys, head))
            out_ref[0, at:end, lanes] = (g_query * 0.125).astype(bf16)
        out_ref[1, :count, lanes] = g_key.astype(bf16)
        out_ref[2, :count, lanes] = g_value.astype(bf16)
        if count < total:
            for c in range(3):
                out_ref[c, count:, lanes] = jnp.zeros((total - count, 2 * HS), bf16)

    @pl.when(length == 0)
    def _():
        for c in range(3):
            out_ref[c, :, lanes] = jnp.zeros((total, 2 * HS), bf16)

    for count in range(block, total + 1, block):
        pl.when((length > count - block) & (length <= count))(lambda count=count: with_keys(count))


def attend_back(qkv, g_out, own_len):
    tokens, width = g_out.shape
    seqs = own_len.shape[0]
    length, pairs = tokens // seqs, width // (2 * HS)
    block = (length, 2 * HS)
    return pl.pallas_call(
        attend_back_kernel,
        out_shape=jax.ShapeDtypeStruct((3, tokens, width), bf16),
        grid_spec=pltpu.PrefetchScalarGridSpec(
            num_scalar_prefetch=1,
            grid=(seqs, pairs),
            in_specs=[pl.BlockSpec((None,) + block, lambda s, p, _, c=c: (c, s, p)) for c in range(3)]
            + [pl.BlockSpec(block, lambda s, p, _: (s, p))],
            out_specs=pl.BlockSpec((3, length, width), lambda s, p, _: (0, s, 0)),
        ),
        compiler_params=pltpu.CompilerParams(vmem_limit_bytes=48 * 1024 * 1024),
        cost_estimate=pl.CostEstimate(
            flops=seqs * pairs * length * length * 1280, bytes_accessed=tokens * width * 14, transcendentals=0
        ),
        name="attend_back",
    )(own_len, qkv, qkv, qkv, g_out)


def dot(a, b):
    return jnp.dot(a, b, preferred_element_type=f32)


def dot_t(a, b):
    return lax.dot_general(a, b, (((1,), (1,)), ((), ())), preferred_element_type=f32)


def t_dot(a, b):
    return lax.dot_general(a, b, (((0,), (0,)), ((), ())), preferred_element_type=f32)


def gelu_both(inner):
    cumulative = 0.5 * (1.0 + lax.erf(inner * 0.7071067811865476))
    density = 0.3989422804014327 * jnp.exp(-0.5 * inner * inner)
    return inner * cumulative, cumulative + inner * density


def row_block(tokens):
    return min(tokens, 256)


def whole(array):
    return pl.BlockSpec(array.shape, lambda *_: (0,) * array.ndim, pipeline_mode=pl.Buffered(1))


def place_rows(vectors, shape):
    place = lax.broadcasted_iota(jnp.int32, shape, 0)
    out = jnp.zeros(shape, f32)
    for k, vector in enumerate(vectors):
        out = jnp.where(place == k, vector, out)
    return out


def norm_back(grad_rows, gain, scaled, inverse):
    weighted = grad_rows * gain
    return inverse * (
        weighted
        - jnp.mean(weighted, -1, keepdims=True)
        - scaled * jnp.mean(weighted * scaled, -1, keepdims=True)
    )


def second_norm(base, act, down, out_grad, vectors, own_len):
    tokens, features = base.shape
    hidden = act.shape[1]
    block = row_block(tokens)
    length = tokens // own_len.shape[0]
    vectors = [vector.reshape(1, features) for vector in vectors]

    def kernel(length_ref, base_ref, act_ref, down_ref, grad_ref, bias_ref, gain_ref, shift_ref, out_ref, back_ref, low_ref, sums_ref):
        step = pl.program_id(0)
        resid = base_ref[...] + dot(act_ref[...], down_ref[...]) + bias_ref[...].astype(f32)
        gain = gain_ref[...].astype(f32)
        normed, scaled, inverse = normalize(resid, gain, shift_ref[...].astype(f32))
        out_ref[...] = normed.astype(bf16)
        at = step * block + lax.broadcasted_iota(jnp.int32, (block, 1), 0)
        live = (at % length) < length_ref[step * block // length]
        grad = jnp.where(live, grad_ref[...].astype(f32), 0.0)
        back = norm_back(grad, gain, scaled, inverse)
        back_ref[...] = back
        low_ref[...] = back.astype(bf16)
        sums = [jnp.sum(rows, 0, keepdims=True) for rows in (back, grad * scaled, grad)]

        @pl.when(step == 0)
        def _():
            sums_ref[...] = jnp.zeros_like(sums_ref)

        sums_ref[...] += place_rows(sums, sums_ref.shape)

    rows = pl.BlockSpec((block, features), lambda k, _: (k, 0))
    return pl.pallas_call(
        kernel,
        out_shape=(
            jax.ShapeDtypeStruct((tokens, features), bf16),
            jax.ShapeDtypeStruct((tokens, features), f32),
            jax.ShapeDtypeStruct((tokens, features), bf16),
            jax.ShapeDtypeStruct((8, features), f32),
        ),
        grid_spec=pltpu.PrefetchScalarGridSpec(
            num_scalar_prefetch=1,
            grid=(tokens // block,),
            in_specs=[rows, pl.BlockSpec((block, hidden), lambda k, _: (k, 0)), whole(down), rows]
            + [whole(vector) for vector in vectors],
            out_specs=[rows, rows, rows, pl.BlockSpec((8, features), lambda k, _: (0, 0))],
        ),
        compiler_params=pltpu.CompilerParams(vmem_limit_bytes=48 * 1024 * 1024),
        cost_estimate=pl.CostEstimate(
            flops=2 * tokens * features * hidden, bytes_accessed=tokens * features * 20, transcendentals=0
        ),
        name="second_norm",
    )(own_len, base, act, down, out_grad, *vectors)


def hidden_back(g_resid, slopes, scaled, inverse, gain, downs, ups, projs, own_len):
    tokens, features = g_resid.shape
    hidden, width = slopes[0].shape[1], projs[0].shape[0]
    block = row_block(tokens)
    length = tokens // own_len.shape[0]
    cut = min(hidden, 768)
    gain = gain.reshape(1, features)

    def kernel(
        length_ref, g_ref, slope_a, slope_b, scaled_ref, inverse_ref, gain_ref, down_a, down_b, up_a, up_b, proj_a, proj_b,
        pre_a, pre_b, resid_ref, low_ref, att_a, att_b, sums_ref, bias_ref,
    ):
        step = pl.program_id(0)

        @pl.when(step == 0)
        def _():
            sums_ref[...] = jnp.zeros_like(sums_ref)
            bias_ref[...] = jnp.zeros_like(bias_ref)

        start = step * block
        live = (start % length) < length_ref[start // length]

        @pl.when(live)
        def _():
            total = g_ref[...]
            low = total.astype(bf16)
            for k, (slope, down, up, pre) in enumerate(
                ((slope_a, down_a, up_a, pre_a), (slope_b, down_b, up_b, pre_b))
            ):
                for at in range(0, hidden, cut):
                    part = slice(at, at + cut)
                    g_pre = (dot_t(low, down[part, :]) * slope[:, part].astype(f32)).astype(bf16)
                    pre[:, part] = g_pre
                    row = jnp.sum(g_pre.astype(f32), 0, keepdims=True)
                    bias_ref[:, part] += place_rows([row if j == k else jnp.zeros_like(row) for j in range(2)], (8, cut))
                    total = total + dot_t(g_pre, up[:, part])
            scaled = scaled_ref[...]
            back = norm_back(total, gain_ref[...].astype(f32), scaled, inverse_ref[...])
            resid_ref[...] = back
            low = back.astype(bf16)
            low_ref[...] = low
            att_a[...] = dot_t(low, proj_a[...]).astype(bf16)
            att_b[...] = dot_t(low, proj_b[...]).astype(bf16)
            sums = [jnp.sum(rows, 0, keepdims=True) for rows in (back, total * scaled, total)]
            sums_ref[...] += place_rows(sums, sums_ref.shape)

        @pl.when(jnp.logical_not(live))
        def _():
            for ref in (pre_a, pre_b, resid_ref, low_ref, att_a, att_b):
                ref[...] = jnp.zeros_like(ref)

    def rows(size):
        return pl.BlockSpec((block, size), lambda k, _: (k, 0))

    def shape(size, dtype):
        return jax.ShapeDtypeStruct((tokens, size), dtype)

    return pl.pallas_call(
        kernel,
        out_shape=(
            shape(hidden, bf16), shape(hidden, bf16), shape(features, f32), shape(features, bf16),
            shape(width, bf16), shape(width, bf16),
            jax.ShapeDtypeStruct((8, features), f32), jax.ShapeDtypeStruct((8, hidden), f32),
        ),
        grid_spec=pltpu.PrefetchScalarGridSpec(
            num_scalar_prefetch=1,
            grid=(tokens // block,),
            in_specs=[rows(features), rows(hidden), rows(hidden), rows(features), rows(1)]
            + [whole(array) for array in (gain, *downs, *ups, *projs)],
            out_specs=[
                rows(hidden), rows(hidden), rows(features), rows(features), rows(width), rows(width),
                pl.BlockSpec((8, features), lambda k, _: (0, 0)), pl.BlockSpec((8, hidden), lambda k, _: (0, 0)),
            ],
        ),
        compiler_params=pltpu.CompilerParams(vmem_limit_bytes=56 * 1024 * 1024),
        cost_estimate=pl.CostEstimate(
            flops=8 * tokens * features * hidden, bytes_accessed=tokens * hidden * 12, transcendentals=0
        ),
        name="hidden_back",
    )(own_len, g_resid, *slopes, scaled, inverse, gain, *downs, *ups, *projs)


def plane_grads(flat, g, core):
    features, tokens = flat.shape
    planes, _, width = g.shape
    half = features // 2

    def kernel(core_ref, flat_ref, g_ref, out_ref):
        out_ref[...] = dot(flat_ref[...], g_ref[...]).astype(bf16)

    return pl.pallas_call(
        kernel,
        out_shape=jax.ShapeDtypeStruct((2, planes, half, width), bf16),
        grid_spec=pltpu.PrefetchScalarGridSpec(
            num_scalar_prefetch=1,
            grid=(2, planes),
            in_specs=[
                pl.BlockSpec((half, tokens), lambda h, c, core: (h, 0)),
                pl.BlockSpec((None, tokens, width), lambda h, c, core: (c, 0, 0)),
            ],
            out_specs=pl.BlockSpec((None, None, half, width), lambda h, c, core: (h ^ core[0], c, 0, 0)),
        ),
        compiler_params=pltpu.CompilerParams(vmem_limit_bytes=48 * 1024 * 1024),
        cost_estimate=pl.CostEstimate(
            flops=2 * tokens * features * width * planes, bytes_accessed=tokens * width * planes * 4, transcendentals=0
        ),
        name="plane_grads",
    )(core[None], flat, g)


def input_grad(g_resid, gs, weights):
    tokens, features = g_resid.shape
    planes, _, width = gs[0].shape
    block = row_block(tokens)

    def kernel(resid_ref, g_a, g_b, weight_a, weight_b, out_ref):
        total = resid_ref[...]
        for g, weight in ((g_a, weight_a), (g_b, weight_b)):
            for c in range(planes):
                total = total + dot_t(g[c], weight[c])
        out_ref[...] = total.astype(bf16)

    rows = pl.BlockSpec((block, features), lambda k: (k, 0))
    plane_rows = pl.BlockSpec((planes, block, width), lambda k: (0, k, 0))
    return pl.pallas_call(
        kernel,
        out_shape=jax.ShapeDtypeStruct((tokens, features), bf16),
        grid_spec=pl.GridSpec(
            grid=(tokens // block,),
            in_specs=[rows, plane_rows, plane_rows] + [whole(weight) for weight in weights],
            out_specs=rows,
        ),
        compiler_params=pltpu.CompilerParams(vmem_limit_bytes=48 * 1024 * 1024),
        cost_estimate=pl.CostEstimate(
            flops=4 * tokens * features * width * planes, bytes_accessed=tokens * width * planes * 6, transcendentals=0
        ),
        name="input_grad",
    )(g_resid, *gs, *weights)


def body(
    hidden_in, seq_lengths, live_seqs, out_grad, query_key_value_matrix, query_bias, value_bias,
    projection_matrix, proj_bias, norm1_gain, norm1_shift, up_matrix, up_bias, down_matrix,
    down_bias, norm2_gain, norm2_shift,
):
    seq_count, length, features = hidden_in.shape
    width = query_key_value_matrix.shape[2]
    heads = width // HS
    tokens = seq_count * length
    gain_one, shift_one = norm1_gain.astype(f32), norm1_shift.astype(f32)
    side = lax.axis_index("tensor")
    own_len = lax.dynamic_slice_in_dim(seq_lengths, side * seq_count, seq_count)
    owned = lax.dynamic_index_in_dim(live_seqs, side, 0, keepdims=False)
    own_len = jnp.where(lax.iota(jnp.int32, seq_count) < owned, own_len, 0)

    x = hidden_in.reshape(tokens, features)
    core, quarter = lax.axis_index("dp") & 1, lax.axis_index("dp") & 3
    qkv_w = query_key_value_matrix.transpose(1, 0, 2).reshape(3 * features, width)
    qkv_get = Gather(pick(qkv_w, 2, core), False)
    biases = jnp.concatenate([query_bias, value_bias, up_bias])
    biases_o = flip(biases)
    proj_get = Gather(pick(projection_matrix, 4, quarter), True)
    up_get = Gather(pick(up_matrix, 4, quarter), True)
    down_get = Gather(pick(down_matrix, 4, quarter), True)

    def project(weight, bias):
        bias = jnp.stack([bias[:width], jnp.zeros((width,), bias.dtype), bias[width : 2 * width]])
        rows = jnp.einsum("tv,cvw->ctw", x, weight.reshape(3, features, width), preferred_element_type=f32)
        return (rows + bias.astype(f32)[:, None, :]).astype(bf16)

    qkv_rows = [project(qkv_w, biases)]
    attended = [attend(qkv_rows[0], own_len)]
    attended = tie(attended, qkv_get)
    qkv_get.cores()
    qkv_o = qkv_get.finish()
    qkv_rows.append(project(qkv_o, biases_o))
    qkv_rows = tie(qkv_rows, proj_get, up_get)
    proj_get.beside()
    up_get.beside()
    attended.append(attend(qkv_rows[1], own_len))
    attended = tie(attended, proj_get, down_get)
    proj_get.cores()
    down_get.beside()
    flat = x.T
    attended = tie(attended, proj_get)
    projs = [projection_matrix, proj_get.finish()]
    up_biases = [biases[2 * width :].astype(f32), biases_o[2 * width :].astype(f32)]
    branch = dot(attended[0], projs[0]) + dot(attended[1], projs[1])
    resid_one = x.astype(f32) + branch + proj_bias.astype(f32)
    normed_one, scaled_one, inverse_one = normalize(resid_one, gain_one, shift_one)
    normed_low = normed_one.astype(bf16)
    activated, slopes = [], []
    ups = [up_matrix]
    downs = [down_matrix]
    base = normed_one
    for k in range(2):
        act, slope = gelu_both(dot(normed_low, ups[k]) + up_biases[k])
        act, slope = act.astype(bf16), slope.astype(bf16)
        if k == 0:
            act, normed_low, slope = tie([act, normed_low, slope], up_get)
            up_get.cores()
            base = base + dot(act, downs[0])
            base, normed_low = tie([base, normed_low], down_get, up_get)
            down_get.cores()
            ups.append(up_get.finish())
        activated.append(act)
        slopes.append(slope)
    (activated[1],) = tie([activated[1]], down_get)
    downs.append(down_get.finish())
    out_hidden, g_resid_two, g_mlp, sums_two = second_norm(
        base, activated[1], downs[1], out_grad.reshape(tokens, features), [down_bias, norm2_gain, norm2_shift], own_len
    )
    out_hidden = out_hidden.reshape(hidden_in.shape)

    down_sum, up_sum, proj_sum, qkv_sum = Reduction(), Reduction(), Reduction(), Reduction()
    groups = down_sum.groups
    last = len(groups) - 1
    down_sum.cores(*[halves(t_dot(act, g_mlp).astype(bf16), core) for act in activated])
    g_pre_a, g_pre_b, g_resid_one, g_attn, att_a, att_b, sums_one, bias_sums = hidden_back(
        g_resid_two, slopes, scaled_one, inverse_one, norm1_gain, downs, ups, projs, own_len
    )
    g_pre, g_att = [g_pre_a, g_pre_b], [att_a, att_b]
    g_pre = tie(g_pre, down_sum)
    down_sum.sides()
    up_sum.cores(*[halves(t_dot(normed_low, g).astype(bf16), core) for g in g_pre])
    (g_attn,) = tie([g_attn], up_sum)
    proj_sum.cores(*[halves(t_dot(rows, g_attn).astype(bf16), core) for rows in attended])
    g_att = tie(g_att, proj_sum)
    g_qkv_o = attend_back(qkv_rows[1], g_att[1], own_len)

    def plane_halves(g):
        grads = plane_grads(flat, g, core)
        return [grads[k].reshape(-1, width) for k in range(2)]

    (g_qkv_o,) = tie([g_qkv_o], down_sum)
    up_sum.sides()
    down_sum.scatter(groups[1])
    grads_o = plane_halves(g_qkv_o)
    (g_att[0],) = tie([g_att[0]], down_sum)
    for group in groups[2:]:
        down_sum.scatter(group)
    g_qkv = [attend_back(qkv_rows[0], g_att[0], own_len), g_qkv_o]
    qkv_sum.cores(plane_halves(g_qkv[0]), grads_o)
    sums = [jnp.sum(g.astype(f32), 1) for g in g_qkv]
    ups_rows = up_bias.shape[0] // features
    vectors = []
    for k in range(2):
        up_rows = [bias_sums[k, r * features : (r + 1) * features] for r in range(ups_rows)]
        shared = [sums_one[r] for r in range(3)] + [sums_two[r] for r in range(3)]
        vectors.append(stack_rows(shared + up_rows + [jnp.concatenate([sums[k][0], sums[k][2]])], features))

    def step(*holders):
        tie([], *holders)

    step(up_sum, down_sum, qkv_sum)
    qkv_sum.join(proj_sum)
    qkv_sum.sides()
    up_sum.scatter(groups[1])
    down_sum.gather(last)
    (g_resid_one,) = tie([g_resid_one], up_sum, down_sum)
    grad_hidden = input_grad(g_resid_one, g_qkv, [w.reshape(3, features, width) for w in (qkv_w, qkv_o)])
    for group in groups[2:]:
        up_sum.scatter(group)
    down_sum.gather(last - 1)
    vector_sum = VectorSum(*vectors)
    step(qkv_sum, up_sum, down_sum, vector_sum)
    qkv_sum.scatter(groups[1])
    up_sum.gather(last)
    for k in range(last - 2, -1, -1):
        down_sum.gather(k)
    vector_sum.hop()
    step(qkv_sum, up_sum, down_sum, vector_sum)
    down_grad = down_sum.finish()
    for group in groups[2:]:
        qkv_sum.scatter(group)
    up_sum.gather(last - 1)
    vector_sum.hop()
    step(qkv_sum, up_sum, vector_sum)
    qkv_sum.gather(last)
    for k in range(last - 2, -1, -1):
        up_sum.gather(k)
    vector_sum.hop()
    step(qkv_sum, up_sum, vector_sum)
    qkv_sum.gather(last - 1)
    up_grad = up_sum.finish()
    vector_sum.hop()
    step(qkv_sum, vector_sum)
    for k in range(last - 2, -1, -1):
        qkv_sum.gather(k)
    vector = vector_sum.finish()
    qkv_grad = qkv_sum.finish(planes=3)
    proj_grad = qkv_sum.finish(skip=3 * features // 2, width=features)
    grad_hidden = grad_hidden.reshape(hidden_in.shape)
    return (
        out_hidden,
        grad_hidden,
        qkv_grad.reshape(3, features, width).transpose(1, 0, 2),
        vector[6 + ups_rows, :width],
        vector[6 + ups_rows, width:],
        proj_grad,
        vector[0],
        vector[1],
        vector[2],
        up_grad,
        vector[6 : 6 + ups_rows].reshape(-1),
        down_grad,
        vector[3],
        vector[4],
        vector[5],
    )


def solution(mesh):
    rows = P(("dp", "tensor"), None, None)
    placed = (
        rows, P("dp"), P("dp"), rows, P(None, None, "tensor"), P("tensor"), P("tensor"),
        P("tensor", None), P(), P(), P(), P(None, "tensor"), P("tensor"), P("tensor", None),
        P(), P(), P(),
    )
    outs = (
        rows, rows, P(None, None, "tensor"), P("tensor"), P("tensor"), P("tensor", None), P(), P(),
        P(), P(None, "tensor"), P("tensor"), P("tensor", None), P(), P(), P(),
    )
    return jax.shard_map(body, mesh=mesh, in_specs=placed, out_specs=outs, check_vma=False)
```

```python
import jax
import jax.numpy as jnp
from jax import lax
from jax.experimental import pallas as pl
from jax.experimental.pallas import tpu as pltpu
from jax.sharding import PartitionSpec as P

HS = 64
epsilon = 1e-06
f32 = jnp.float32
bf16 = jnp.bfloat16
LIGHT = pl.CostEstimate(flops=1, bytes_accessed=1, transcendentals=0)


def flip(value):
    return lax.ppermute(value, "tensor", [(0, 1), (1, 0)])


def hop(value, mask):
    count = lax.axis_size("dp")
    return lax.ppermute(value, "dp", [(i, i ^ mask) for i in range(count)])


def dp_groups():
    count = lax.axis_size("dp")
    bits = count.bit_length() - 1
    groups, at = [], 0
    for width in [1, 1] + [2] * bits:
        width = min(width, bits - at)
        if width > 0:
            groups.append((at, width))
        at += width
    return groups


def member(group):
    at, width = group
    return (lax.axis_index("dp") >> at) & ((1 << width) - 1)


def pick(rows, pieces, which):
    count, width = rows.shape
    return lax.dynamic_index_in_dim(rows.reshape(pieces, count // pieces, width), which, 0, keepdims=False)


def tie(values, *holders):
    arrays = list(values) + [array for holder in holders for array in holder.came]
    arrays = list(lax.optimization_barrier(tuple(arrays)))
    at = len(values)
    for holder in holders:
        holder.came = arrays[at : at + len(holder.came)]
        at += len(holder.came)
    return arrays[: len(values)]


class Waiting:
    def __init__(self, came):
        self.came = came


def by_bit(bit, zero, one):
    return jnp.where(bit == 0, zero, one)


class Gather:
    def __init__(self, sent, spread):
        self.spread = spread
        self.came = [flip(sent)]

    def beside(self):
        row = member((1, 1))
        (mine,) = self.came
        (other,) = self.came = [hop(mine, 2)]
        self.mine = mine

    def cores(self):
        if self.spread:
            row = member((1, 1))
            (other,) = self.came
            self.parts = [by_bit(row, self.mine, other), by_bit(row, other, self.mine)]
        else:
            self.parts = self.came
        self.came = [hop(part, 1) for part in self.parts]

    def finish(self):
        core = member((0, 1))
        rows = []
        for mine, other in zip(self.parts, self.came):
            rows += [by_bit(core, mine, other), by_bit(core, other, mine)]
        return jnp.concatenate(rows, 0)


class Reduction:
    def __init__(self):
        self.groups = dp_groups()

    def cores(self, other):
        self.core = member(self.groups[0])
        self.keep = other[0]
        self.came = [hop(other[1], 1)]

    def sides(self, split=1):
        away = (self.keep.astype(f32) + self.came[0].astype(f32)).astype(bf16)
        rows = away.shape[0] // split
        self.came = [flip(away[at : at + rows]) for at in range(0, away.shape[0], rows)]

    def own_cores(self, own):
        self.total = own[0].astype(f32)
        self.own_came = hop(own[1], 1)

    def meet(self):
        self.came = [jnp.concatenate(self.came, 0) if len(self.came) > 1 else self.came[0], self.own_came]

    def settle(self):
        for rows in self.came:
            self.total = self.total + rows.astype(f32)

    def scatter(self, group):
        self.settle()
        at, width = group
        pieces, me = 1 << width, member(group)
        low = self.total.astype(bf16)
        self.came = [hop(pick(low, pieces, me ^ j), j << at) for j in range(1, pieces)]
        self.total = pick(self.total, pieces, me)

    def gather(self, k):
        if k == len(self.groups) - 1:
            self.settle()
            self.result = self.total.astype(bf16)
        else:
            self.result = assemble([self.result] + self.came, member(self.groups[k + 1]), bf16)
        at, width = self.groups[k]
        self.came = [hop(self.result, j << at) for j in range(1, 1 << width)]

    def finish(self, **shape):
        return assemble([self.result] + self.came, self.core, f32, **shape)


def assemble(slots, me, dtype, planes=1, skip=0, width=None):
    count = len(slots)
    have = slots[0].shape[1]
    wide = 1 if width is None else width // have
    rows = (slots[0].shape[0] - skip if planes == 1 else slots[0].shape[0] // (planes + 1) * planes) // planes // wide
    if planes > 1:
        skip = 0

    def kernel(me_ref, *refs):
        step = pl.program_id(0) ^ me_ref[0]
        for j in range(count):

            @pl.when(step == j)
            def _():
                for plane in range(planes):
                    for part in range(wide):
                        at = skip + (plane * wide + part) * rows
                        refs[-1][plane, 0, :, part * have : (part + 1) * have] = refs[j][at : at + rows, :].astype(dtype)

    out = pl.pallas_call(
        kernel,
        out_shape=jax.ShapeDtypeStruct((planes, count, rows, wide * have), dtype),
        grid_spec=pltpu.PrefetchScalarGridSpec(
            num_scalar_prefetch=1,
            grid=(count,),
            in_specs=[pl.BlockSpec(slot.shape, lambda k, _: (0, 0)) for slot in slots],
            out_specs=pl.BlockSpec((planes, 1, rows, wide * have), lambda k, _: (0, k, 0, 0)),
        ),
        compiler_params=pltpu.CompilerParams(vmem_limit_bytes=48 * 1024 * 1024),
        cost_estimate=LIGHT,
        name="assemble",
    )(me[None].astype(jnp.int32), *slots)
    return out.reshape(planes * count * rows, wide * have)


class VectorSum:
    def __init__(self, own, other):
        self.total, self.mask = own, 1
        self.came = [flip(other)]

    def hop(self):
        if self.mask < lax.axis_size("dp"):
            self.total = self.total + self.came[0]
            self.came = [hop(self.total, self.mask)]
            self.mask *= 2

    def finish(self):
        while self.mask < lax.axis_size("dp"):
            self.hop()
        return self.total + self.came[0]


def halves(rows, core):
    return pick(rows, 2, core), pick(rows, 2, 1 - core)


def joined(first, second):
    width = first[0].shape[1]
    return [
        jnp.concatenate([a] + [b[:, at : at + width] for at in range(0, b.shape[1], width)], 0)
        for a, b in zip(first, second)
    ]


def stack_rows(vectors, features):
    count = -(-len(vectors) // 8) * 8
    place = lax.broadcasted_iota(jnp.int32, (count, features), 0)
    out = jnp.zeros((count, features), f32)
    for k, vector in enumerate(vectors):
        out = jnp.where(place == k, vector[None, :], out)
    return out


def normalize(resid, gain, shift):
    average = jnp.mean(resid, -1, keepdims=True)
    centred = resid - average
    inverse = lax.rsqrt(jnp.mean(centred * centred, -1, keepdims=True) + epsilon)
    scaled = centred * inverse
    return (scaled * gain + shift, scaled, inverse)


def head_lanes(shape, head):
    return (lax.broadcasted_iota(jnp.int32, shape, 1) >= HS) == (head == 1)


def only_head(rows, head):
    return jnp.where(head_lanes(rows.shape, head), rows, jnp.zeros_like(rows))


def attend_kernel(length_ref, query_ref, key_ref, value_ref, out_ref):
    total = query_ref.shape[0]
    length = length_ref[pl.program_id(0)]
    step = min(total, 256)
    block = min(total, 128)

    def with_keys(count):
        keys, values = key_ref[:count, :], value_ref[:count, :]
        valid = lax.broadcasted_iota(jnp.int32, (1, count), 1) < length
        for at in range(0, total, step):
            query = query_ref[at : at + step, :] * jnp.bfloat16(0.125)
            parts = []
            for head in range(2):
                scores = jnp.where(valid, dot_t(only_head(query, head), keys), -1000000000.0)
                shifted = jnp.exp(scores - jnp.max(scores, -1, keepdims=True))
                probs = shifted * (1.0 / jnp.sum(shifted, -1, keepdims=True))
                parts.append(dot(probs.astype(bf16), values))
            out_ref[at : at + step, :] = jnp.where(head_lanes(parts[0].shape, 0), *parts).astype(bf16)

    @pl.when(length == 0)
    def _():
        average = jnp.sum(value_ref[...].astype(f32), 0, keepdims=True) * (1.0 / total)
        out_ref[...] = jnp.broadcast_to(average, out_ref.shape).astype(bf16)

    for count in range(block, total + 1, block):
        pl.when((length > count - block) & (length <= count))(lambda count=count: with_keys(count))


def attend(qkv, own_len):
    _, tokens, width = qkv.shape
    seqs = own_len.shape[0]
    length, pairs = tokens // seqs, width // (2 * HS)
    block = (length, 2 * HS)
    return pl.pallas_call(
        attend_kernel,
        out_shape=jax.ShapeDtypeStruct((tokens, width), bf16),
        grid_spec=pltpu.PrefetchScalarGridSpec(
            num_scalar_prefetch=1,
            grid=(seqs, pairs),
            in_specs=[pl.BlockSpec((None,) + block, lambda s, p, _, c=c: (c, s, p)) for c in range(3)],
            out_specs=pl.BlockSpec(block, lambda s, p, _: (s, p)),
        ),
        compiler_params=pltpu.CompilerParams(vmem_limit_bytes=48 * 1024 * 1024),
        cost_estimate=LIGHT,
        name="attend",
    )(own_len, qkv, qkv, qkv)


def attend_back_kernel(length_ref, query_ref, key_ref, value_ref, g_out_ref, out_ref):
    total = query_ref.shape[0]
    length = length_ref[pl.program_id(0)]
    pair = pl.program_id(1)
    block = min(total, 128)
    lanes = pl.ds(pl.multiple_of(pair * 2 * HS, 2 * HS), 2 * HS)

    def with_keys(count):
        keys, values = key_ref[:count, :], value_ref[:count, :]
        valid = lax.broadcasted_iota(jnp.int32, (count, 1), 0) < length
        step = min(count, 256)
        starts = list(range(0, count, step))
        g_key = jnp.zeros((count, 2 * HS), f32)
        g_value = jnp.zeros((count, 2 * HS), f32)
        for at in starts:
            end = min(at + step, count)
            query = query_ref[at:end, :] * jnp.bfloat16(0.125)
            g_out = g_out_ref[at:end, :]
            g_query = jnp.zeros((end - at, 2 * HS), f32)
            for head in range(2):
                query_head, g_head = only_head(query, head), only_head(g_out, head)
                scores = jnp.where(valid, dot_t(keys, query_head), -1000000000.0)
                shifted = jnp.exp(scores - jnp.max(scores, 0, keepdims=True))
                probs = shifted * (1.0 / jnp.sum(shifted, 0, keepdims=True))
                g_probs = dot_t(values, g_head)
                delta = jnp.sum(g_probs * probs, 0, keepdims=True)
                g_scores = (probs * (g_probs - delta)).astype(bf16)
                g_key = g_key + dot(g_scores, query_head)
                g_value = g_value + dot(probs.astype(bf16), g_head)
                g_query = g_query + t_dot(g_scores, only_head(keys, head))
            out_ref[0, at:end, lanes] = (g_query * 0.125).astype(bf16)
        out_ref[1, :count, lanes] = g_key.astype(bf16)
        out_ref[2, :count, lanes] = g_value.astype(bf16)
        if count < total:
            for c in range(3):
                out_ref[c, count:, lanes] = jnp.zeros((total - count, 2 * HS), bf16)

    @pl.when(length == 0)
    def _():
        for c in range(3):
            out_ref[c, :, lanes] = jnp.zeros((total, 2 * HS), bf16)

    for count in range(block, total + 1, block):
        pl.when((length > count - block) & (length <= count))(lambda count=count: with_keys(count))


def attend_back(qkv, g_out, own_len):
    tokens, width = g_out.shape
    seqs = own_len.shape[0]
    length, pairs = tokens // seqs, width // (2 * HS)
    block = (length, 2 * HS)
    return pl.pallas_call(
        attend_back_kernel,
        out_shape=jax.ShapeDtypeStruct((3, tokens, width), bf16),
        grid_spec=pltpu.PrefetchScalarGridSpec(
            num_scalar_prefetch=1,
            grid=(seqs, pairs),
            in_specs=[pl.BlockSpec((None,) + block, lambda s, p, _, c=c: (c, s, p)) for c in range(3)]
            + [pl.BlockSpec(block, lambda s, p, _: (s, p))],
            out_specs=pl.BlockSpec((3, length, width), lambda s, p, _: (0, s, 0)),
        ),
        compiler_params=pltpu.CompilerParams(vmem_limit_bytes=48 * 1024 * 1024),
        cost_estimate=LIGHT,
        name="attend_back",
    )(own_len, qkv, qkv, qkv, g_out)


def dot(a, b):
    return jnp.dot(a, b, preferred_element_type=f32)


def dot_t(a, b):
    return lax.dot_general(a, b, (((1,), (1,)), ((), ())), preferred_element_type=f32)


def t_dot(a, b):
    return lax.dot_general(a, b, (((0,), (0,)), ((), ())), preferred_element_type=f32)


def gelu_both(inner):
    cumulative = 0.5 * (1.0 + lax.erf(inner * 0.7071067811865476))
    density = 0.3989422804014327 * jnp.exp(-0.5 * inner * inner)
    return inner * cumulative, cumulative + inner * density


def row_block(tokens):
    return min(tokens, 256)


def whole(array):
    return pl.BlockSpec(array.shape, lambda *_: (0,) * array.ndim, pipeline_mode=pl.Buffered(1))


def place_rows(vectors, shape):
    place = lax.broadcasted_iota(jnp.int32, shape, 0)
    out = jnp.zeros(shape, f32)
    for k, vector in enumerate(vectors):
        out = jnp.where(place == k, vector, out)
    return out


def norm_back(grad_rows, gain, scaled, inverse):
    weighted = grad_rows * gain
    return inverse * (
        weighted
        - jnp.mean(weighted, -1, keepdims=True)
        - scaled * jnp.mean(weighted * scaled, -1, keepdims=True)
    )


def first_norm(rows, projs, x, vectors):
    tokens, features = x.shape
    width = rows[0].shape[1]
    block = row_block(tokens)
    vectors = [vector.reshape(1, features) for vector in vectors]

    def kernel(att_a, att_b, proj_a, proj_b, x_ref, bias_ref, gain_ref, shift_ref, resid_ref, low_ref):
        branch = dot(att_a[...], proj_a[...]) + dot(att_b[...], proj_b[...])
        resid = x_ref[...].astype(f32) + branch + bias_ref[...].astype(f32)
        resid_ref[...] = resid
        low_ref[...] = normalize(resid, gain_ref[...].astype(f32), shift_ref[...].astype(f32))[0].astype(bf16)

    def blocks(size):
        return pl.BlockSpec((block, size), lambda k: (k, 0))

    return pl.pallas_call(
        kernel,
        out_shape=(jax.ShapeDtypeStruct((tokens, features), f32), jax.ShapeDtypeStruct((tokens, features), bf16)),
        grid_spec=pl.GridSpec(
            grid=(tokens // block,),
            in_specs=[blocks(width)] * 2 + [whole(proj) for proj in projs] + [blocks(features)]
            + [whole(vector) for vector in vectors],
            out_specs=[blocks(features)] * 2,
        ),
        compiler_params=pltpu.CompilerParams(vmem_limit_bytes=32 * 1024 * 1024),
        cost_estimate=LIGHT,
        name="first_norm",
    )(*rows, *projs, x, *vectors)


def hidden_half(low, up, up_bias, branch=None):
    tokens, features = low.shape
    hidden = up.shape[1]
    block = row_block(tokens)
    cut = min(hidden, 512)

    def kernel(low_ref, up_ref, bias_ref, *refs):
        act_ref, slope_ref = refs[4:6] if branch else refs
        low = low_ref[...]
        for at in range(0, hidden, cut):
            part = slice(at, at + cut)
            act, slope = gelu_both(dot(low, up_ref[:, part]) + bias_ref[:, part].astype(f32))
            act_ref[:, part] = act.astype(bf16)
            slope_ref[:, part] = slope.astype(bf16)
        if branch:
            resid_ref, gain_ref, shift_ref, down_ref = refs[:4]
            normed = normalize(resid_ref[...], gain_ref[...].astype(f32), shift_ref[...].astype(f32))[0]
            refs[6][...] = normed + dot(act_ref[...], down_ref[...])

    def blocks(size):
        return pl.BlockSpec((block, size), lambda k: (k, 0))

    args = [low, up, up_bias.reshape(1, hidden)]
    in_specs = [blocks(features)] + [whole(array) for array in args[1:]]
    out_shape = [jax.ShapeDtypeStruct((tokens, hidden), bf16)] * 2
    out_specs = [blocks(hidden)] * 2
    if branch:
        resid, gain, shift, down = branch
        more = [gain.reshape(1, features), shift.reshape(1, features), down]
        args += [resid] + more
        in_specs += [blocks(features)] + [whole(array) for array in more]
        out_shape.append(jax.ShapeDtypeStruct((tokens, features), f32))
        out_specs.append(blocks(features))
    return pl.pallas_call(
        kernel,
        out_shape=out_shape,
        grid_spec=pl.GridSpec(grid=(tokens // block,), in_specs=in_specs, out_specs=out_specs),
        compiler_params=pltpu.CompilerParams(vmem_limit_bytes=48 * 1024 * 1024),
        cost_estimate=LIGHT,
        name="hidden_half",
    )(*args)


def second_norm(base, act, down, out_grad, vectors, own_len):
    tokens, features = base.shape
    hidden = act.shape[1]
    block = row_block(tokens)
    length = tokens // own_len.shape[0]
    vectors = [vector.reshape(1, features) for vector in vectors]

    def kernel(length_ref, base_ref, act_ref, down_ref, grad_ref, bias_ref, gain_ref, shift_ref, out_ref, back_ref, low_ref, sums_ref):
        step = pl.program_id(0)
        resid = base_ref[...] + dot(act_ref[...], down_ref[...]) + bias_ref[...].astype(f32)
        gain = gain_ref[...].astype(f32)
        normed, scaled, inverse = normalize(resid, gain, shift_ref[...].astype(f32))
        out_ref[...] = normed.astype(bf16)
        at = step * block + lax.broadcasted_iota(jnp.int32, (block, 1), 0)
        live = (at % length) < length_ref[step * block // length]
        grad = jnp.where(live, grad_ref[...].astype(f32), 0.0)
        back = norm_back(grad, gain, scaled, inverse)
        back_ref[...] = back
        low_ref[...] = back.astype(bf16)
        sums = [jnp.sum(rows, 0, keepdims=True) for rows in (back, grad * scaled, grad)]

        @pl.when(step == 0)
        def _():
            sums_ref[...] = jnp.zeros_like(sums_ref)

        sums_ref[...] += place_rows(sums, sums_ref.shape)

    rows = pl.BlockSpec((block, features), lambda k, _: (k, 0))
    return pl.pallas_call(
        kernel,
        out_shape=(
            jax.ShapeDtypeStruct((tokens, features), bf16),
            jax.ShapeDtypeStruct((tokens, features), f32),
            jax.ShapeDtypeStruct((tokens, features), bf16),
            jax.ShapeDtypeStruct((8, features), f32),
        ),
        grid_spec=pltpu.PrefetchScalarGridSpec(
            num_scalar_prefetch=1,
            grid=(tokens // block,),
            in_specs=[rows, pl.BlockSpec((block, hidden), lambda k, _: (k, 0)), whole(down), rows]
            + [whole(vector) for vector in vectors],
            out_specs=[rows, rows, rows, pl.BlockSpec((8, features), lambda k, _: (0, 0))],
        ),
        compiler_params=pltpu.CompilerParams(vmem_limit_bytes=48 * 1024 * 1024),
        cost_estimate=LIGHT,
        name="second_norm",
    )(own_len, base, act, down, out_grad, *vectors)


def hidden_back(g_resid, slopes, resid_one, gain, downs, ups, projs, own_len):
    tokens, features = g_resid.shape
    hidden, width = slopes[0].shape[1], projs[0].shape[0]
    block = row_block(tokens)
    length = tokens // own_len.shape[0]
    cut = min(hidden, 768)
    gain = gain.reshape(1, features)

    def kernel(
        length_ref, g_ref, slope_a, slope_b, normed_ref, gain_ref, down_a, down_b, up_a, up_b, proj_a, proj_b,
        pre_a, pre_b, resid_ref, low_ref, att_a, att_b, sums_ref, bias_ref,
    ):
        step = pl.program_id(0)

        @pl.when(step == 0)
        def _():
            sums_ref[...] = jnp.zeros_like(sums_ref)
            bias_ref[...] = jnp.zeros_like(bias_ref)

        start = step * block
        live = (start % length) < length_ref[start // length]

        @pl.when(live)
        def _():
            total = g_ref[...]
            low = total.astype(bf16)
            for k, (slope, down, up, pre) in enumerate(
                ((slope_a, down_a, up_a, pre_a), (slope_b, down_b, up_b, pre_b))
            ):
                for at in range(0, hidden, cut):
                    part = slice(at, at + cut)
                    g_pre = (dot_t(low, down[part, :]) * slope[:, part].astype(f32)).astype(bf16)
                    pre[:, part] = g_pre
                    row = jnp.sum(g_pre.astype(f32), 0, keepdims=True)
                    bias_ref[:, part] += place_rows([row if j == k else jnp.zeros_like(row) for j in range(2)], (8, cut))
                    total = total + dot_t(g_pre, up[:, part])
            gain = gain_ref[...].astype(f32)
            _, scaled, inverse = normalize(normed_ref[...], gain, 0.0)
            back = norm_back(total, gain, scaled, inverse)
            resid_ref[...] = back
            low = back.astype(bf16)
            low_ref[...] = low
            att_a[...] = dot_t(low, proj_a[...]).astype(bf16)
            att_b[...] = dot_t(low, proj_b[...]).astype(bf16)
            sums = [jnp.sum(rows, 0, keepdims=True) for rows in (back, total * scaled, total)]
            sums_ref[...] += place_rows(sums, sums_ref.shape)

        @pl.when(jnp.logical_not(live))
        def _():
            for ref in (pre_a, pre_b, resid_ref, low_ref, att_a, att_b):
                ref[...] = jnp.zeros_like(ref)

    def rows(size):
        return pl.BlockSpec((block, size), lambda k, _: (k, 0))

    def shape(size, dtype):
        return jax.ShapeDtypeStruct((tokens, size), dtype)

    return pl.pallas_call(
        kernel,
        out_shape=(
            shape(hidden, bf16), shape(hidden, bf16), shape(features, f32), shape(features, bf16),
            shape(width, bf16), shape(width, bf16),
            jax.ShapeDtypeStruct((8, features), f32), jax.ShapeDtypeStruct((8, hidden), f32),
        ),
        grid_spec=pltpu.PrefetchScalarGridSpec(
            num_scalar_prefetch=1,
            grid=(tokens // block,),
            in_specs=[rows(features), rows(hidden), rows(hidden), rows(features)]
            + [whole(array) for array in (gain, *downs, *ups, *projs)],
            out_specs=[
                rows(hidden), rows(hidden), rows(features), rows(features), rows(width), rows(width),
                pl.BlockSpec((8, features), lambda k, _: (0, 0)), pl.BlockSpec((8, hidden), lambda k, _: (0, 0)),
            ],
        ),
        compiler_params=pltpu.CompilerParams(vmem_limit_bytes=56 * 1024 * 1024),
        cost_estimate=LIGHT,
        name="hidden_back",
    )(own_len, g_resid, *slopes, resid_one, gain, *downs, *ups, *projs)


def plane_grads(flat, g, core):
    features, tokens = flat.shape
    planes, _, width = g.shape
    half = features // 2

    def kernel(core_ref, flat_ref, g_ref, out_ref):
        out_ref[...] = dot(flat_ref[...], g_ref[...]).astype(bf16)

    return pl.pallas_call(
        kernel,
        out_shape=jax.ShapeDtypeStruct((2, planes, half, width), bf16),
        grid_spec=pltpu.PrefetchScalarGridSpec(
            num_scalar_prefetch=1,
            grid=(2, planes),
            in_specs=[
                pl.BlockSpec((half, tokens), lambda h, c, core: (h, 0)),
                pl.BlockSpec((None, tokens, width), lambda h, c, core: (c, 0, 0)),
            ],
            out_specs=pl.BlockSpec((None, None, half, width), lambda h, c, core: (h ^ core[0], c, 0, 0)),
        ),
        compiler_params=pltpu.CompilerParams(vmem_limit_bytes=48 * 1024 * 1024),
        cost_estimate=LIGHT,
        name="plane_grads",
    )(core[None], flat, g)


def input_grad(g_resid, gs, weights):
    tokens, features = g_resid.shape
    planes, _, width = gs[0].shape
    block = row_block(tokens)

    def kernel(resid_ref, g_a, g_b, weight_a, weight_b, out_ref):
        total = resid_ref[...]
        for g, weight in ((g_a, weight_a), (g_b, weight_b)):
            for c in range(planes):
                total = total + dot_t(g[c], weight[c])
        out_ref[...] = total.astype(bf16)

    rows = pl.BlockSpec((block, features), lambda k: (k, 0))
    plane_rows = pl.BlockSpec((planes, block, width), lambda k: (0, k, 0))
    return pl.pallas_call(
        kernel,
        out_shape=jax.ShapeDtypeStruct((tokens, features), bf16),
        grid_spec=pl.GridSpec(
            grid=(tokens // block,),
            in_specs=[rows, plane_rows, plane_rows] + [whole(weight) for weight in weights],
            out_specs=rows,
        ),
        compiler_params=pltpu.CompilerParams(vmem_limit_bytes=48 * 1024 * 1024),
        cost_estimate=LIGHT,
        name="input_grad",
    )(g_resid, *gs, *weights)


def body(
    hidden_in, seq_lengths, live_seqs, out_grad, query_key_value_matrix, query_bias, value_bias,
    projection_matrix, proj_bias, norm1_gain, norm1_shift, up_matrix, up_bias, down_matrix,
    down_bias, norm2_gain, norm2_shift,
):
    seq_count, length, features = hidden_in.shape
    width = query_key_value_matrix.shape[2]
    heads = width // HS
    tokens = seq_count * length
    side = lax.axis_index("tensor")
    own_len = lax.dynamic_slice_in_dim(seq_lengths, side * seq_count, seq_count)
    owned = lax.dynamic_index_in_dim(live_seqs, side, 0, keepdims=False)
    own_len = jnp.where(lax.iota(jnp.int32, seq_count) < owned, own_len, 0)

    x = hidden_in.reshape(tokens, features)
    core, quarter = lax.axis_index("dp") & 1, lax.axis_index("dp") & 3
    qkv_w = query_key_value_matrix.transpose(1, 0, 2).reshape(3 * features, width)
    qkv_get = Gather(pick(qkv_w, 2, core), False)
    biases = jnp.concatenate([query_bias, value_bias, up_bias])
    biases_o = flip(biases)
    proj_get = Gather(pick(projection_matrix, 2, core), False)
    up_get = Gather(pick(up_matrix, 4, quarter), True)
    down_get = Gather(pick(down_matrix, 2, core), False)

    def project(weight, bias):
        bias = jnp.stack([bias[:width], jnp.zeros((width,), bias.dtype), bias[width : 2 * width]])
        rows = jnp.einsum("tv,cvw->ctw", x, weight.reshape(3, features, width), preferred_element_type=f32)
        return (rows + bias.astype(f32)[:, None, :]).astype(bf16)

    qkv_rows = [project(qkv_w, biases)]
    attended = [attend(qkv_rows[0], own_len)]
    attended = tie(attended, qkv_get)
    qkv_get.cores()
    flat = x.T
    (flat,) = tie([flat], qkv_get)
    qkv_o = qkv_get.finish()
    qkv_rows.append(project(qkv_o, biases_o))
    qkv_rows = tie(qkv_rows, proj_get)
    proj_get.cores()
    attended.append(attend(qkv_rows[1], own_len))
    attended = tie(attended, proj_get, up_get)
    up_get.beside()
    projs = [projection_matrix, proj_get.finish()]
    resid_one, normed_low = first_norm(attended, projs, x, [proj_bias, norm1_gain, norm1_shift])
    ups, downs = [up_matrix], [down_matrix]
    act_a, slope_a, base = hidden_half(
        normed_low, up_matrix, biases[2 * width :], (resid_one, norm1_gain, norm1_shift, down_matrix)
    )
    base, normed_low = tie([base, normed_low], up_get)
    up_get.cores()
    (normed_low,) = tie([normed_low], up_get, down_get)
    down_get.cores()
    ups.append(up_get.finish())
    act_b, slope_b = hidden_half(normed_low, ups[1], biases_o[2 * width :])
    downs.append(down_get.finish())
    activated, slopes = [act_a, act_b], [slope_a, slope_b]
    out_hidden, g_resid_two, g_mlp, sums_two = second_norm(
        base, act_b, downs[1], out_grad.reshape(tokens, features), [down_bias, norm2_gain, norm2_shift], own_len
    )
    out_hidden = out_hidden.reshape(hidden_in.shape)

    down_sum, up_sum, qkv_sum = Reduction(), Reduction(), Reduction()
    groups = down_sum.groups
    last = len(groups) - 1

    def weight_grad(a, b):
        return halves(t_dot(a, b).astype(bf16), core)

    down_sum.cores(weight_grad(act_b, g_mlp))
    down_own = weight_grad(act_a, g_mlp)
    g_resid_two, *down_own = tie([g_resid_two, *down_own], down_sum)
    down_sum.sides()
    down_sum.own_cores(down_own)
    down_sum.meet()
    g_pre_a, g_pre_b, g_resid_one, g_attn, att_a, att_b, sums_one, bias_sums = hidden_back(
        g_resid_two, slopes, resid_one, norm1_gain, downs, ups, projs, own_len
    )
    up_sum.cores(weight_grad(normed_low, g_pre_b))
    g_pre_a, g_attn, att_b = tie([g_pre_a, g_attn, att_b], down_sum, up_sum)
    up_sum.sides()
    down_sum.scatter(groups[1])
    up_sum.own_cores(weight_grad(normed_low, g_pre_a))
    up_sum.meet()
    proj_own, proj_other = [weight_grad(rows, g_attn) for rows in attended]
    g_qkv_o = attend_back(qkv_rows[1], att_b, own_len)

    def plane_halves(g):
        grads = plane_grads(flat, g, core)
        return [grads[k].reshape(-1, width) for k in range(2)]

    qkv_sum.cores(joined(plane_halves(g_qkv_o), proj_other))
    (att_a,) = tie([att_a], qkv_sum, down_sum)
    for group in groups[2:]:
        down_sum.scatter(group)
    (att_a,) = tie([att_a], up_sum, down_sum)
    qkv_sum.sides(2)
    up_sum.scatter(groups[1])
    down_sum.gather(last)
    g_qkv = [attend_back(qkv_rows[0], att_a, own_len), g_qkv_o]
    qkv_sum.own_cores(joined(plane_halves(g_qkv[0]), proj_own))
    sums = [jnp.sum(g.astype(f32), 1) for g in g_qkv]
    ups_rows = up_bias.shape[0] // features
    vectors = []
    for k in range(2):
        up_rows = [bias_sums[k, r * features : (r + 1) * features] for r in range(ups_rows)]
        shared = [sums_one[r] for r in range(3)] + [sums_two[r] for r in range(3)]
        vectors.append(stack_rows(shared + up_rows + [jnp.concatenate([sums[k][0], sums[k][2]])], features))
    vector_sum = VectorSum(*vectors)
    grad_hidden = input_grad(g_resid_one, g_qkv, [w.reshape(3, features, width) for w in (qkv_w, qkv_o)])

    def step(*holders):
        tie([], *holders)

    early = Waiting(qkv_sum.came[:1])
    (grad_hidden,) = tie([grad_hidden], up_sum, down_sum, early)
    qkv_sum.came[:1] = early.came
    qkv_sum.meet()
    for group in groups[2:]:
        up_sum.scatter(group)
    down_sum.gather(last - 1)
    step(qkv_sum, up_sum, down_sum, vector_sum)
    qkv_sum.scatter(groups[1])
    up_sum.gather(last)
    for k in range(last - 2, -1, -1):
        down_sum.gather(k)
    vector_sum.hop()
    step(qkv_sum, up_sum, down_sum, vector_sum)
    down_grad = down_sum.finish()
    for group in groups[2:]:
        qkv_sum.scatter(group)
    up_sum.gather(last - 1)
    vector_sum.hop()
    step(qkv_sum, up_sum, vector_sum)
    qkv_sum.gather(last)
    for k in range(last - 2, -1, -1):
        up_sum.gather(k)
    vector_sum.hop()
    step(qkv_sum, up_sum, vector_sum)
    qkv_sum.gather(last - 1)
    up_grad = up_sum.finish()
    vector_sum.hop()
    step(qkv_sum, vector_sum)
    for k in range(last - 2, -1, -1):
        qkv_sum.gather(k)
    vector = vector_sum.finish()
    qkv_grad = qkv_sum.finish(planes=3)
    proj_grad = qkv_sum.finish(skip=3 * features // 2, width=features)
    grad_hidden = grad_hidden.reshape(hidden_in.shape)
    return (
        out_hidden,
        grad_hidden,
        qkv_grad.reshape(3, features, width).transpose(1, 0, 2),
        vector[6 + ups_rows, :width],
        vector[6 + ups_rows, width:],
        proj_grad,
        vector[0],
        vector[1],
        vector[2],
        up_grad,
        vector[6 : 6 + ups_rows].reshape(-1),
        down_grad,
        vector[3],
        vector[4],
        vector[5],
    )


def solution(mesh):
    rows = P(("dp", "tensor"), None, None)
    placed = (
        rows, P("dp"), P("dp"), rows, P(None, None, "tensor"), P("tensor"), P("tensor"),
        P("tensor", None), P(), P(), P(), P(None, "tensor"), P("tensor"), P("tensor", None),
        P(), P(), P(),
    )
    outs = (
        rows, rows, P(None, None, "tensor"), P("tensor"), P("tensor"), P("tensor", None), P(), P(),
        P(), P(None, "tensor"), P("tensor"), P("tensor", None), P(), P(), P(),
    )
    return jax.shard_map(body, mesh=mesh, in_specs=placed, out_specs=outs, check_vma=False)
```

```python
import jax
import jax.numpy as jnp
from jax import lax
from jax.experimental import pallas as pl
from jax.experimental.pallas import tpu as pltpu
from jax.sharding import PartitionSpec as P

HS = 64
epsilon = 1e-06
f32 = jnp.float32
bf16 = jnp.bfloat16
LIGHT = pl.CostEstimate(flops=1, bytes_accessed=1, transcendentals=0)


def flip(value):
    return lax.ppermute(value, "tensor", [(0, 1), (1, 0)])


def hop(value, mask):
    count = lax.axis_size("dp")
    return lax.ppermute(value, "dp", [(i, i ^ mask) for i in range(count)])


def dp_groups():
    count = lax.axis_size("dp")
    bits = count.bit_length() - 1
    groups, at = [], 0
    for width in [1, 1] + [2] * bits:
        width = min(width, bits - at)
        if width > 0:
            groups.append((at, width))
        at += width
    return groups


def member(group):
    at, width = group
    return (lax.axis_index("dp") >> at) & ((1 << width) - 1)


def pick(rows, pieces, which):
    count, width = rows.shape
    return lax.dynamic_index_in_dim(rows.reshape(pieces, count // pieces, width), which, 0, keepdims=False)


def tie(values, *holders):
    arrays = list(values) + [array for holder in holders for array in holder.came]
    arrays = list(lax.optimization_barrier(tuple(arrays)))
    at = len(values)
    for holder in holders:
        holder.came = arrays[at : at + len(holder.came)]
        at += len(holder.came)
    return arrays[: len(values)]


def by_bit(bit, zero, one):
    return jnp.where(bit == 0, zero, one)


class Gather:
    def __init__(self, sent, spread):
        self.spread = spread
        self.came = [flip(sent)]

    def beside(self):
        row = member((1, 1))
        (mine,) = self.came
        (other,) = self.came = [hop(mine, 2)]
        self.mine = mine

    def cores(self):
        if self.spread:
            row = member((1, 1))
            (other,) = self.came
            self.parts = [by_bit(row, self.mine, other), by_bit(row, other, self.mine)]
        else:
            self.parts = self.came
        self.came = [hop(part, 1) for part in self.parts]

    def finish(self):
        core = member((0, 1))
        rows = []
        for mine, other in zip(self.parts, self.came):
            rows += [by_bit(core, mine, other), by_bit(core, other, mine)]
        return jnp.concatenate(rows, 0)


class Reduction:
    def __init__(self):
        self.groups = dp_groups()

    def cores(self, other):
        self.core = member(self.groups[0])
        self.keep = other[0]
        self.came = [hop(other[1], 1)]

    def sides(self, eighths=6):
        away = (self.keep.astype(f32) + self.came[0].astype(f32)).astype(bf16)
        first = away.shape[0] * eighths // 8
        self.came = [flip(away[:first]), flip(away[first:])]

    def first_side(self, values):
        *values, self.came[0] = lax.optimization_barrier((*values, self.came[0]))
        return values

    def own_cores(self, own):
        self.total = own[0].astype(f32)
        self.own_came = hop(own[1], 1)

    def meet(self):
        self.came = [jnp.concatenate(self.came, 0), self.own_came]

    def settle(self):
        for rows in self.came:
            self.total = self.total + rows.astype(f32)

    def scatter(self, group):
        self.settle()
        at, width = group
        pieces, me = 1 << width, member(group)
        low = self.total.astype(bf16)
        self.came = [hop(pick(low, pieces, me ^ j), j << at) for j in range(1, pieces)]
        self.total = pick(self.total, pieces, me)

    def gather(self, k):
        if k == len(self.groups) - 1:
            self.settle()
            self.result = self.total.astype(bf16)
        else:
            self.result = assemble([self.result] + self.came, member(self.groups[k + 1]), bf16)
        at, width = self.groups[k]
        self.came = [hop(self.result, j << at) for j in range(1, 1 << width)]

    def finish(self, **shape):
        return assemble([self.result] + self.came, self.core, f32, **shape)


def assemble(slots, me, dtype, parts=((0, 0),), rows=None, width=None, planes=1):
    count = len(slots)
    rows = slots[0].shape[0] if rows is None else rows
    width = slots[0].shape[1] if width is None else width
    each = len(parts) // planes

    def kernel(me_ref, *refs):
        step = pl.program_id(0) ^ me_ref[0]
        for j in range(count):

            @pl.when(step == j)
            def _():
                for p, (row, column) in enumerate(parts):
                    at = p % each * rows
                    refs[-1][p // each, 0, at : at + rows, :] = refs[j][
                        row : row + rows, column : column + width
                    ].astype(dtype)

    out = pl.pallas_call(
        kernel,
        out_shape=jax.ShapeDtypeStruct((planes, count, each * rows, width), dtype),
        grid_spec=pltpu.PrefetchScalarGridSpec(
            num_scalar_prefetch=1,
            grid=(count,),
            in_specs=[pl.BlockSpec(slot.shape, lambda k, _: (0, 0)) for slot in slots],
            out_specs=pl.BlockSpec((planes, 1, each * rows, width), lambda k, _: (0, k, 0, 0)),
        ),
        compiler_params=pltpu.CompilerParams(vmem_limit_bytes=48 * 1024 * 1024),
        cost_estimate=LIGHT,
        name="assemble",
    )(me[None].astype(jnp.int32), *slots)
    return out.reshape(planes * count * each * rows, width)


class VectorSum:
    def __init__(self, own, other):
        self.total, self.mask = own, 1
        self.came = [flip(other)]

    def hop(self):
        if self.mask < lax.axis_size("dp"):
            self.total = self.total + self.came[0]
            self.came = [hop(self.total, self.mask)]
            self.mask *= 2

    def finish(self):
        while self.mask < lax.axis_size("dp"):
            self.hop()
        return self.total + self.came[0]


def stack_rows(vectors, features):
    count = -(-len(vectors) // 8) * 8
    place = lax.broadcasted_iota(jnp.int32, (count, features), 0)
    out = jnp.zeros((count, features), f32)
    for k, vector in enumerate(vectors):
        out = jnp.where(place == k, vector[None, :], out)
    return out


def normalize(resid, gain, shift):
    average = jnp.mean(resid, -1, keepdims=True)
    centred = resid - average
    inverse = lax.rsqrt(jnp.mean(centred * centred, -1, keepdims=True) + epsilon)
    scaled = centred * inverse
    return (scaled * gain + shift, scaled, inverse)


def head_lanes(shape, head):
    return (lax.broadcasted_iota(jnp.int32, shape, 1) >= HS) == (head == 1)


def only_head(rows, head):
    return jnp.where(head_lanes(rows.shape, head), rows, jnp.zeros_like(rows))


def attend_kernel(length_ref, query_ref, key_ref, value_ref, out_ref):
    total = query_ref.shape[0]
    length = length_ref[pl.program_id(0)]
    step = min(total, 256)
    block = min(total, 128)

    def with_keys(count):
        keys, values = key_ref[:count, :], value_ref[:count, :]
        valid = lax.broadcasted_iota(jnp.int32, (1, count), 1) < length
        for at in range(0, total, step):
            query = query_ref[at : at + step, :] * jnp.bfloat16(0.125)
            parts = []
            for head in range(2):
                scores = jnp.where(valid, dot_t(only_head(query, head), keys), -1000000000.0)
                shifted = jnp.exp(scores - jnp.max(scores, -1, keepdims=True))
                probs = shifted * (1.0 / jnp.sum(shifted, -1, keepdims=True))
                parts.append(dot(probs.astype(bf16), values))
            out_ref[at : at + step, :] = jnp.where(head_lanes(parts[0].shape, 0), *parts).astype(bf16)

    @pl.when(length == 0)
    def _():
        average = jnp.sum(value_ref[...].astype(f32), 0, keepdims=True) * (1.0 / total)
        out_ref[...] = jnp.broadcast_to(average, out_ref.shape).astype(bf16)

    for count in range(block, total + 1, block):
        pl.when((length > count - block) & (length <= count))(lambda count=count: with_keys(count))


def attend(qkv, own_len):
    _, tokens, width = qkv.shape
    seqs = own_len.shape[0]
    length, pairs = tokens // seqs, width // (2 * HS)
    block = (length, 2 * HS)
    return pl.pallas_call(
        attend_kernel,
        out_shape=jax.ShapeDtypeStruct((tokens, width), bf16),
        grid_spec=pltpu.PrefetchScalarGridSpec(
            num_scalar_prefetch=1,
            grid=(seqs, pairs),
            in_specs=[pl.BlockSpec((None,) + block, lambda s, p, _, c=c: (c, s, p)) for c in range(3)],
            out_specs=pl.BlockSpec(block, lambda s, p, _: (s, p)),
        ),
        compiler_params=pltpu.CompilerParams(vmem_limit_bytes=48 * 1024 * 1024),
        cost_estimate=LIGHT,
        name="attend",
    )(own_len, qkv, qkv, qkv)


def attend_back_kernel(length_ref, query_ref, key_ref, value_ref, g_out_ref, out_ref):
    total = query_ref.shape[0]
    length = length_ref[pl.program_id(0)]
    pair = pl.program_id(1)
    block = min(total, 128)
    lanes = pl.ds(pl.multiple_of(pair * 2 * HS, 2 * HS), 2 * HS)

    def with_keys(count):
        keys, values = key_ref[:count, :], value_ref[:count, :]
        valid = lax.broadcasted_iota(jnp.int32, (count, 1), 0) < length
        step = min(count, 256)
        starts = list(range(0, count, step))
        g_key = jnp.zeros((count, 2 * HS), f32)
        g_value = jnp.zeros((count, 2 * HS), f32)
        for at in starts:
            end = min(at + step, count)
            query = query_ref[at:end, :] * jnp.bfloat16(0.125)
            g_out = g_out_ref[at:end, :]
            g_query = jnp.zeros((end - at, 2 * HS), f32)
            for head in range(2):
                query_head, g_head = only_head(query, head), only_head(g_out, head)
                scores = jnp.where(valid, dot_t(keys, query_head), -1000000000.0)
                shifted = jnp.exp(scores - jnp.max(scores, 0, keepdims=True))
                probs = shifted * (1.0 / jnp.sum(shifted, 0, keepdims=True))
                g_probs = dot_t(values, g_head)
                delta = jnp.sum(g_probs * probs, 0, keepdims=True)
                g_scores = (probs * (g_probs - delta)).astype(bf16)
                g_key = g_key + dot(g_scores, query_head)
                g_value = g_value + dot(probs.astype(bf16), g_head)
                g_query = g_query + t_dot(g_scores, only_head(keys, head))
            out_ref[0, at:end, lanes] = (g_query * 0.125).astype(bf16)
        out_ref[1, :count, lanes] = g_key.astype(bf16)
        out_ref[2, :count, lanes] = g_value.astype(bf16)
        if count < total:
            for c in range(3):
                out_ref[c, count:, lanes] = jnp.zeros((total - count, 2 * HS), bf16)

    @pl.when(length == 0)
    def _():
        for c in range(3):
            out_ref[c, :, lanes] = jnp.zeros((total, 2 * HS), bf16)

    for count in range(block, total + 1, block):
        pl.when((length > count - block) & (length <= count))(lambda count=count: with_keys(count))


def attend_back(qkv, g_out, own_len):
    tokens, width = g_out.shape
    seqs = own_len.shape[0]
    length, pairs = tokens // seqs, width // (2 * HS)
    block = (length, 2 * HS)
    return pl.pallas_call(
        attend_back_kernel,
        out_shape=jax.ShapeDtypeStruct((3, tokens, width), bf16),
        grid_spec=pltpu.PrefetchScalarGridSpec(
            num_scalar_prefetch=1,
            grid=(seqs, pairs),
            in_specs=[pl.BlockSpec((None,) + block, lambda s, p, _, c=c: (c, s, p)) for c in range(3)]
            + [pl.BlockSpec(block, lambda s, p, _: (s, p))],
            out_specs=pl.BlockSpec((3, length, width), lambda s, p, _: (0, s, 0)),
        ),
        compiler_params=pltpu.CompilerParams(vmem_limit_bytes=48 * 1024 * 1024),
        cost_estimate=LIGHT,
        name="attend_back",
    )(own_len, qkv, qkv, qkv, g_out)


def dot(a, b):
    return jnp.dot(a, b, preferred_element_type=f32)


def dot_t(a, b):
    return lax.dot_general(a, b, (((1,), (1,)), ((), ())), preferred_element_type=f32)


def t_dot(a, b):
    return lax.dot_general(a, b, (((0,), (0,)), ((), ())), preferred_element_type=f32)


def gelu_both(inner):
    cumulative = 0.5 * (1.0 + lax.erf(inner * 0.7071067811865476))
    density = 0.3989422804014327 * jnp.exp(-0.5 * inner * inner)
    return inner * cumulative, cumulative + inner * density


def row_block(tokens):
    return min(tokens, 256)


def whole(array):
    return pl.BlockSpec(array.shape, lambda *_: (0,) * array.ndim, pipeline_mode=pl.Buffered(1))


def place_rows(vectors, shape):
    place = lax.broadcasted_iota(jnp.int32, shape, 0)
    out = jnp.zeros(shape, f32)
    for k, vector in enumerate(vectors):
        out = jnp.where(place == k, vector, out)
    return out


def norm_back(grad_rows, gain, scaled, inverse):
    weighted = grad_rows * gain
    return inverse * (
        weighted
        - jnp.mean(weighted, -1, keepdims=True)
        - scaled * jnp.mean(weighted * scaled, -1, keepdims=True)
    )


def first_norm(rows, projs, x, vectors):
    tokens, features = x.shape
    width = rows[0].shape[1]
    block = row_block(tokens)
    vectors = [vector.reshape(1, features) for vector in vectors]

    def kernel(att_a, att_b, proj_a, proj_b, x_ref, bias_ref, gain_ref, shift_ref, resid_ref, low_ref):
        branch = dot(att_a[...], proj_a[...]) + dot(att_b[...], proj_b[...])
        resid = x_ref[...].astype(f32) + branch + bias_ref[...].astype(f32)
        resid_ref[...] = resid
        low_ref[...] = normalize(resid, gain_ref[...].astype(f32), shift_ref[...].astype(f32))[0].astype(bf16)

    def blocks(size):
        return pl.BlockSpec((block, size), lambda k: (k, 0))

    return pl.pallas_call(
        kernel,
        out_shape=(jax.ShapeDtypeStruct((tokens, features), f32), jax.ShapeDtypeStruct((tokens, features), bf16)),
        grid_spec=pl.GridSpec(
            grid=(tokens // block,),
            in_specs=[blocks(width)] * 2 + [whole(proj) for proj in projs] + [blocks(features)]
            + [whole(vector) for vector in vectors],
            out_specs=[blocks(features)] * 2,
        ),
        compiler_params=pltpu.CompilerParams(vmem_limit_bytes=32 * 1024 * 1024),
        cost_estimate=LIGHT,
        name="first_norm",
    )(*rows, *projs, x, *vectors)


def hidden_half(low, up, up_bias, branch=None):
    tokens, features = low.shape
    hidden = up.shape[1]
    block = row_block(tokens)
    cut = min(hidden, 512)

    def kernel(low_ref, up_ref, bias_ref, *refs):
        act_ref, slope_ref = refs[4:6] if branch else refs
        low = low_ref[...]
        for at in range(0, hidden, cut):
            part = slice(at, at + cut)
            act, slope = gelu_both(dot(low, up_ref[:, part]) + bias_ref[:, part].astype(f32))
            act_ref[:, part] = act.astype(bf16)
            slope_ref[:, part] = slope.astype(bf16)
        if branch:
            resid_ref, gain_ref, shift_ref, down_ref = refs[:4]
            normed = normalize(resid_ref[...], gain_ref[...].astype(f32), shift_ref[...].astype(f32))[0]
            refs[6][...] = normed + dot(act_ref[...], down_ref[...])

    def blocks(size):
        return pl.BlockSpec((block, size), lambda k: (k, 0))

    args = [low, up, up_bias.reshape(1, hidden)]
    in_specs = [blocks(features)] + [whole(array) for array in args[1:]]
    out_shape = [jax.ShapeDtypeStruct((tokens, hidden), bf16)] * 2
    out_specs = [blocks(hidden)] * 2
    if branch:
        resid, gain, shift, down = branch
        more = [gain.reshape(1, features), shift.reshape(1, features), down]
        args += [resid] + more
        in_specs += [blocks(features)] + [whole(array) for array in more]
        out_shape.append(jax.ShapeDtypeStruct((tokens, features), f32))
        out_specs.append(blocks(features))
    return pl.pallas_call(
        kernel,
        out_shape=out_shape,
        grid_spec=pl.GridSpec(grid=(tokens // block,), in_specs=in_specs, out_specs=out_specs),
        compiler_params=pltpu.CompilerParams(vmem_limit_bytes=48 * 1024 * 1024),
        cost_estimate=LIGHT,
        name="hidden_half",
    )(*args)


def second_norm(base, act, down, out_grad, vectors, own_len):
    tokens, features = base.shape
    hidden = act.shape[1]
    block = row_block(tokens)
    length = tokens // own_len.shape[0]
    vectors = [vector.reshape(1, features) for vector in vectors]

    def kernel(length_ref, base_ref, act_ref, down_ref, grad_ref, bias_ref, gain_ref, shift_ref, out_ref, back_ref, low_ref, sums_ref):
        step = pl.program_id(0)
        resid = base_ref[...] + dot(act_ref[...], down_ref[...]) + bias_ref[...].astype(f32)
        gain = gain_ref[...].astype(f32)
        normed, scaled, inverse = normalize(resid, gain, shift_ref[...].astype(f32))
        out_ref[...] = normed.astype(bf16)
        at = step * block + lax.broadcasted_iota(jnp.int32, (block, 1), 0)
        live = (at % length) < length_ref[step * block // length]
        grad = jnp.where(live, grad_ref[...].astype(f32), 0.0)
        back = norm_back(grad, gain, scaled, inverse)
        back_ref[...] = back
        low_ref[...] = back.astype(bf16)
        sums = [jnp.sum(rows, 0, keepdims=True) for rows in (back, grad * scaled, grad)]

        @pl.when(step == 0)
        def _():
            sums_ref[...] = jnp.zeros_like(sums_ref)

        sums_ref[...] += place_rows(sums, sums_ref.shape)

    rows = pl.BlockSpec((block, features), lambda k, _: (k, 0))
    return pl.pallas_call(
        kernel,
        out_shape=(
            jax.ShapeDtypeStruct((tokens, features), bf16),
            jax.ShapeDtypeStruct((tokens, features), f32),
            jax.ShapeDtypeStruct((tokens, features), bf16),
            jax.ShapeDtypeStruct((8, features), f32),
        ),
        grid_spec=pltpu.PrefetchScalarGridSpec(
            num_scalar_prefetch=1,
            grid=(tokens // block,),
            in_specs=[rows, pl.BlockSpec((block, hidden), lambda k, _: (k, 0)), whole(down), rows]
            + [whole(vector) for vector in vectors],
            out_specs=[rows, rows, rows, pl.BlockSpec((8, features), lambda k, _: (0, 0))],
        ),
        compiler_params=pltpu.CompilerParams(vmem_limit_bytes=48 * 1024 * 1024),
        cost_estimate=LIGHT,
        name="second_norm",
    )(own_len, base, act, down, out_grad, *vectors)


def hidden_back(g_resid, slopes, resid_one, gain, downs, ups, projs, own_len):
    tokens, features = g_resid.shape
    hidden, width = slopes[0].shape[1], projs[0].shape[0]
    block = row_block(tokens)
    length = tokens // own_len.shape[0]
    cut = min(hidden, 768)
    gain = gain.reshape(1, features)

    def kernel(
        length_ref, g_ref, slope_a, slope_b, normed_ref, gain_ref, down_a, down_b, up_a, up_b, proj_a, proj_b,
        pre_a, pre_b, resid_ref, low_ref, att_a, att_b, sums_ref, bias_ref,
    ):
        step = pl.program_id(0)

        @pl.when(step == 0)
        def _():
            sums_ref[...] = jnp.zeros_like(sums_ref)
            bias_ref[...] = jnp.zeros_like(bias_ref)

        start = step * block
        live = (start % length) < length_ref[start // length]

        @pl.when(live)
        def _():
            total = g_ref[...]
            low = total.astype(bf16)
            for k, (slope, down, up, pre) in enumerate(
                ((slope_a, down_a, up_a, pre_a), (slope_b, down_b, up_b, pre_b))
            ):
                for at in range(0, hidden, cut):
                    part = slice(at, at + cut)
                    g_pre = (dot_t(low, down[part, :]) * slope[:, part].astype(f32)).astype(bf16)
                    pre[:, part] = g_pre
                    row = jnp.sum(g_pre.astype(f32), 0, keepdims=True)
                    bias_ref[:, part] += place_rows([row if j == k else jnp.zeros_like(row) for j in range(2)], (8, cut))
                    total = total + dot_t(g_pre, up[:, part])
            gain = gain_ref[...].astype(f32)
            _, scaled, inverse = normalize(normed_ref[...], gain, 0.0)
            back = norm_back(total, gain, scaled, inverse)
            resid_ref[...] = back
            low = back.astype(bf16)
            low_ref[...] = low
            att_a[...] = dot_t(low, proj_a[...]).astype(bf16)
            att_b[...] = dot_t(low, proj_b[...]).astype(bf16)
            sums = [jnp.sum(rows, 0, keepdims=True) for rows in (back, total * scaled, total)]
            sums_ref[...] += place_rows(sums, sums_ref.shape)

        @pl.when(jnp.logical_not(live))
        def _():
            for ref in (pre_a, pre_b, resid_ref, low_ref, att_a, att_b):
                ref[...] = jnp.zeros_like(ref)

    def rows(size):
        return pl.BlockSpec((block, size), lambda k, _: (k, 0))

    def shape(size, dtype):
        return jax.ShapeDtypeStruct((tokens, size), dtype)

    return pl.pallas_call(
        kernel,
        out_shape=(
            shape(hidden, bf16), shape(hidden, bf16), shape(features, f32), shape(features, bf16),
            shape(width, bf16), shape(width, bf16),
            jax.ShapeDtypeStruct((8, features), f32), jax.ShapeDtypeStruct((8, hidden), f32),
        ),
        grid_spec=pltpu.PrefetchScalarGridSpec(
            num_scalar_prefetch=1,
            grid=(tokens // block,),
            in_specs=[rows(features), rows(hidden), rows(hidden), rows(features)]
            + [whole(array) for array in (gain, *downs, *ups, *projs)],
            out_specs=[
                rows(hidden), rows(hidden), rows(features), rows(features), rows(width), rows(width),
                pl.BlockSpec((8, features), lambda k, _: (0, 0)), pl.BlockSpec((8, hidden), lambda k, _: (0, 0)),
            ],
        ),
        compiler_params=pltpu.CompilerParams(vmem_limit_bytes=56 * 1024 * 1024),
        cost_estimate=LIGHT,
        name="hidden_back",
    )(own_len, g_resid, *slopes, resid_one, gain, *downs, *ups, *projs)


def token_grads(a, b, core, more=None, slots=None):
    tokens, size = a.shape
    width = b.shape[1]
    half = size // 2
    slots = half if slots is None else slots
    cut = min(width, 768)

    def kernel(core_ref, a_ref, b_ref, *refs):
        out_ref = refs[2] if more else refs[0]
        flat = a_ref[...].T
        for at in range(0, width, cut):
            out_ref[:half, at : at + cut] = dot(flat, b_ref[:, at : at + cut]).astype(bf16)
        if more:
            product_ref = refs[3]
            rows, columns = product_ref.shape
            beside = width // columns
            block = rows // 2 // beside
            step = pl.program_id(0)

            @pl.when(step == 0)
            def _():
                product_ref[...] = t_dot(refs[0][...], refs[1][...]).astype(bf16)

            for h in range(2):

                @pl.when(step == h)
                def _():
                    for k in range(beside):
                        at = h * (rows // 2) + k * block
                        out_ref[half : half + block, k * columns : (k + 1) * columns] = product_ref[at : at + block, :]

            out_ref[half + block :, :] = jnp.zeros((slots - half - block, width), bf16)

    args = [a, b, *(more or ())]
    scratch = [pltpu.VMEM((more[0].shape[1], more[1].shape[1]), bf16)] if more else []
    return pl.pallas_call(
        kernel,
        out_shape=jax.ShapeDtypeStruct((2, slots, width), bf16),
        grid_spec=pltpu.PrefetchScalarGridSpec(
            num_scalar_prefetch=1,
            grid=(2,),
            in_specs=[pl.BlockSpec((tokens, half), lambda h, _: (0, h))] + [whole(array) for array in args[1:]],
            out_specs=pl.BlockSpec((None, slots, width), lambda h, core: (h ^ core[0], 0, 0)),
            scratch_shapes=scratch,
        ),
        compiler_params=pltpu.CompilerParams(vmem_limit_bytes=48 * 1024 * 1024),
        cost_estimate=LIGHT,
        name="token_grads",
    )(core[None], *args)


def plane_grads(flat, g, core):
    features, tokens = flat.shape
    planes, _, width = g.shape
    half = features // 2

    def kernel(core_ref, flat_ref, g_ref, out_ref):
        out_ref[...] = dot(flat_ref[...], g_ref[...]).astype(bf16)

    return pl.pallas_call(
        kernel,
        out_shape=jax.ShapeDtypeStruct((2, planes, half, width), bf16),
        grid_spec=pltpu.PrefetchScalarGridSpec(
            num_scalar_prefetch=1,
            grid=(2, planes),
            in_specs=[
                pl.BlockSpec((half, tokens), lambda h, c, core: (h, 0)),
                pl.BlockSpec((None, tokens, width), lambda h, c, core: (c, 0, 0)),
            ],
            out_specs=pl.BlockSpec((None, None, half, width), lambda h, c, core: (h ^ core[0], c, 0, 0)),
        ),
        compiler_params=pltpu.CompilerParams(vmem_limit_bytes=48 * 1024 * 1024),
        cost_estimate=LIGHT,
        name="plane_grads",
    )(core[None], flat, g)


def input_grad(g_resid, gs, weights):
    tokens, features = g_resid.shape
    planes, _, width = gs[0].shape
    block = row_block(tokens)

    def kernel(resid_ref, g_a, g_b, weight_a, weight_b, out_ref):
        total = resid_ref[...]
        for g, weight in ((g_a, weight_a), (g_b, weight_b)):
            for c in range(planes):
                total = total + dot_t(g[c], weight[c])
        out_ref[...] = total.astype(bf16)

    rows = pl.BlockSpec((block, features), lambda k: (k, 0))
    plane_rows = pl.BlockSpec((planes, block, width), lambda k: (0, k, 0))
    return pl.pallas_call(
        kernel,
        out_shape=jax.ShapeDtypeStruct((tokens, features), bf16),
        grid_spec=pl.GridSpec(
            grid=(tokens // block,),
            in_specs=[rows, plane_rows, plane_rows] + [whole(weight) for weight in weights],
            out_specs=rows,
        ),
        compiler_params=pltpu.CompilerParams(vmem_limit_bytes=48 * 1024 * 1024),
        cost_estimate=LIGHT,
        name="input_grad",
    )(g_resid, *gs, *weights)


def body(
    hidden_in, seq_lengths, live_seqs, out_grad, query_key_value_matrix, query_bias, value_bias,
    projection_matrix, proj_bias, norm1_gain, norm1_shift, up_matrix, up_bias, down_matrix,
    down_bias, norm2_gain, norm2_shift,
):
    seq_count, length, features = hidden_in.shape
    width = query_key_value_matrix.shape[2]
    heads = width // HS
    tokens = seq_count * length
    side = lax.axis_index("tensor")
    own_len = lax.dynamic_slice_in_dim(seq_lengths, side * seq_count, seq_count)
    owned = lax.dynamic_index_in_dim(live_seqs, side, 0, keepdims=False)
    own_len = jnp.where(lax.iota(jnp.int32, seq_count) < owned, own_len, 0)

    x = hidden_in.reshape(tokens, features)
    core, quarter = lax.axis_index("dp") & 1, lax.axis_index("dp") & 3
    qkv_w = query_key_value_matrix.transpose(1, 0, 2).reshape(3 * features, width)
    qkv_get = Gather(pick(qkv_w, 2, core), False)
    biases = jnp.concatenate([query_bias, value_bias, up_bias])
    biases_o = flip(biases)
    up_get = Gather(pick(up_matrix, 4, quarter), True)
    proj_get = Gather(pick(projection_matrix, 2, core), False)
    down_get = Gather(pick(down_matrix, 2, core), False)

    def project(weight, bias):
        bias = jnp.stack([bias[:width], jnp.zeros((width,), bias.dtype), bias[width : 2 * width]])
        rows = jnp.einsum("tv,cvw->ctw", x, weight.reshape(3, features, width), preferred_element_type=f32)
        return (rows + bias.astype(f32)[:, None, :]).astype(bf16)

    qkv_rows = [project(qkv_w, biases)]
    attended = [attend(qkv_rows[0], own_len)]
    attended = tie(attended, qkv_get)
    qkv_get.cores()
    flat = x.T
    (flat,) = tie([flat], qkv_get)
    qkv_o = qkv_get.finish()
    qkv_rows.append(project(qkv_o, biases_o))
    qkv_rows = tie(qkv_rows, up_get)
    up_get.beside()
    attended.append(attend(qkv_rows[1], own_len))
    attended = tie(attended, proj_get)
    proj_get.cores()
    projs = [projection_matrix, proj_get.finish()]
    resid_one, normed_low = first_norm(attended, projs, x, [proj_bias, norm1_gain, norm1_shift])
    (normed_low,) = tie([normed_low], up_get)
    up_get.cores()
    ups, downs = [up_matrix], [down_matrix]
    act_a, slope_a, base = hidden_half(
        normed_low, up_matrix, biases[2 * width :], (resid_one, norm1_gain, norm1_shift, down_matrix)
    )
    base, normed_low = tie([base, normed_low], up_get, down_get)
    down_get.cores()
    ups.append(up_get.finish())
    act_b, slope_b = hidden_half(normed_low, ups[1], biases_o[2 * width :])
    downs.append(down_get.finish())
    activated, slopes = [act_a, act_b], [slope_a, slope_b]
    out_hidden, g_resid_two, g_mlp, sums_two = second_norm(
        base, act_b, downs[1], out_grad.reshape(tokens, features), [down_bias, norm2_gain, norm2_shift], own_len
    )
    out_hidden = out_hidden.reshape(hidden_in.shape)

    down_sum, up_sum, qkv_sum = Reduction(), Reduction(), Reduction()
    groups = down_sum.groups
    last = len(groups) - 1

    down_sum.cores(token_grads(act_b, g_mlp, core))
    down_own = token_grads(act_a, g_mlp, core)
    g_resid_two, down_own = tie([g_resid_two, down_own], down_sum)
    down_sum.sides(7)
    down_sum.own_cores(down_own)
    g_pre_a, g_pre_b, g_resid_one, g_attn, att_a, att_b, sums_one, bias_sums = hidden_back(
        g_resid_two, slopes, resid_one, norm1_gain, downs, ups, projs, own_len
    )
    (g_pre_b,) = down_sum.first_side([g_pre_b])
    half, proj_half = features // 2, width // 4
    up_slots = -(-(half + proj_half) // 128) * 128
    up_sum.cores(token_grads(normed_low, g_pre_b, core, (attended[1], g_attn), up_slots))
    down_sum.meet()
    g_pre_a, att_b = tie([g_pre_a, att_b], down_sum, up_sum)
    up_sum.sides()
    down_sum.scatter(groups[1])
    up_sum.own_cores(token_grads(normed_low, g_pre_a, core, (attended[0], g_attn), up_slots))

    def plane_halves(g):
        grads = plane_grads(flat, g, core)
        return [grads[k].reshape(-1, width) for k in range(2)]

    g_qkv_o = attend_back(qkv_rows[1], att_b, own_len)
    (g_qkv_o,) = tie(up_sum.first_side([g_qkv_o]), down_sum)
    for group in groups[2:]:
        down_sum.scatter(group)
    qkv_sum.cores(plane_halves(g_qkv_o))
    up_sum.meet()
    (att_a,) = tie([att_a], up_sum, down_sum, qkv_sum)
    qkv_sum.sides()
    up_sum.scatter(groups[1])
    down_sum.gather(last)
    g_qkv_a = attend_back(qkv_rows[0], att_a, own_len)
    (g_qkv_a,) = qkv_sum.first_side([g_qkv_a])
    g_qkv = [g_qkv_a, g_qkv_o]
    qkv_sum.own_cores(plane_halves(g_qkv_a))
    sums = [jnp.sum(g.astype(f32), 1) for g in g_qkv]
    ups_rows = up_bias.shape[0] // features
    vectors = []
    for k in range(2):
        up_rows = [bias_sums[k, r * features : (r + 1) * features] for r in range(ups_rows)]
        shared = [sums_one[r] for r in range(3)] + [sums_two[r] for r in range(3)]
        vectors.append(stack_rows(shared + up_rows + [jnp.concatenate([sums[k][0], sums[k][2]])], features))
    vector_sum = VectorSum(*vectors)
    grad_hidden = input_grad(g_resid_one, g_qkv, [w.reshape(3, features, width) for w in (qkv_w, qkv_o)])

    def step(*holders):
        tie([], *holders)

    (grad_hidden,) = tie([grad_hidden], up_sum, down_sum)
    qkv_sum.meet()
    for group in groups[2:]:
        up_sum.scatter(group)
    down_sum.gather(last - 1)
    step(qkv_sum, up_sum, down_sum, vector_sum)
    qkv_sum.scatter(groups[1])
    up_sum.gather(last)
    for k in range(last - 2, -1, -1):
        down_sum.gather(k)
    vector_sum.hop()
    step(qkv_sum, up_sum, down_sum, vector_sum)
    down_grad = down_sum.finish()
    for group in groups[2:]:
        qkv_sum.scatter(group)
    up_sum.gather(last - 1)
    vector_sum.hop()
    step(qkv_sum, up_sum, vector_sum)
    qkv_sum.gather(last)
    for k in range(last - 2, -1, -1):
        up_sum.gather(k)
    vector_sum.hop()
    step(qkv_sum, up_sum, vector_sum)
    qkv_sum.gather(last - 1)
    up_grad = up_sum.finish(rows=half)
    proj_grad = up_sum.finish(parts=((half, 0), (half, features)), rows=proj_half, width=features)
    vector_sum.hop()
    step(qkv_sum, vector_sum)
    for k in range(last - 2, -1, -1):
        qkv_sum.gather(k)
    vector = vector_sum.finish()
    qkv_grad = qkv_sum.finish(parts=tuple((c * half, 0) for c in range(3)), rows=half, planes=3)
    grad_hidden = grad_hidden.reshape(hidden_in.shape)
    return (
        out_hidden,
        grad_hidden,
        qkv_grad.reshape(3, features, width).transpose(1, 0, 2),
        vector[6 + ups_rows, :width],
        vector[6 + ups_rows, width:],
        proj_grad,
        vector[0],
        vector[1],
        vector[2],
        up_grad,
        vector[6 : 6 + ups_rows].reshape(-1),
        down_grad,
        vector[3],
        vector[4],
        vector[5],
    )


def solution(mesh):
    rows = P(("dp", "tensor"), None, None)
    placed = (
        rows, P("dp"), P("dp"), rows, P(None, None, "tensor"), P("tensor"), P("tensor"),
        P("tensor", None), P(), P(), P(), P(None, "tensor"), P("tensor"), P("tensor", None),
        P(), P(), P(),
    )
    outs = (
        rows, rows, P(None, None, "tensor"), P("tensor"), P("tensor"), P("tensor", None), P(), P(),
        P(), P(None, "tensor"), P("tensor"), P("tensor", None), P(), P(), P(),
    )
    return jax.shard_map(body, mesh=mesh, in_specs=placed, out_specs=outs, check_vma=False)
```

```python
import jax
import jax.numpy as jnp
from jax import lax
from jax.experimental import pallas as pl
from jax.experimental.pallas import tpu as pltpu
from jax.sharding import PartitionSpec as P

HS = 64
epsilon = 1e-06
f32 = jnp.float32
bf16 = jnp.bfloat16
LIGHT = pl.CostEstimate(flops=1, bytes_accessed=1, transcendentals=0)


def flip(value):
    return lax.ppermute(value, "tensor", [(0, 1), (1, 0)])


def hop(value, mask):
    count = lax.axis_size("dp")
    return lax.ppermute(value, "dp", [(i, i ^ mask) for i in range(count)])


def dp_groups():
    count = lax.axis_size("dp")
    bits = count.bit_length() - 1
    groups, at = [], 0
    for width in [1, 1] + [2] * bits:
        width = min(width, bits - at)
        if width > 0:
            groups.append((at, width))
        at += width
    return groups


def member(group):
    at, width = group
    return (lax.axis_index("dp") >> at) & ((1 << width) - 1)


def pick(rows, pieces, which):
    count, width = rows.shape
    return lax.dynamic_index_in_dim(rows.reshape(pieces, count // pieces, width), which, 0, keepdims=False)


def tie(values, *holders):
    arrays = list(values) + [array for holder in holders for array in holder.came]
    arrays = list(lax.optimization_barrier(tuple(arrays)))
    at = len(values)
    for holder in holders:
        holder.came = arrays[at : at + len(holder.came)]
        at += len(holder.came)
    return arrays[: len(values)]


def by_bit(bit, zero, one):
    return jnp.where(bit == 0, zero, one)


class Gather:
    def __init__(self, sent, spread):
        self.spread = spread
        self.came = [flip(sent)]

    def beside(self):
        row = member((1, 1))
        (mine,) = self.came
        (other,) = self.came = [hop(mine, 2)]
        self.mine = mine

    def cores(self):
        if self.spread:
            row = member((1, 1))
            (other,) = self.came
            self.parts = [by_bit(row, self.mine, other), by_bit(row, other, self.mine)]
        else:
            self.parts = self.came
        self.came = [hop(part, 1) for part in self.parts]

    def finish(self):
        core = member((0, 1))
        rows = []
        for mine, other in zip(self.parts, self.came):
            rows += [by_bit(core, mine, other), by_bit(core, other, mine)]
        return jnp.concatenate(rows, 0)


class Reduction:
    def __init__(self):
        self.groups = dp_groups()

    def cores(self, other):
        self.core = member(self.groups[0])
        self.keep = other[0]
        self.came = [hop(other[1], 1)]

    def sides(self, eighths=6):
        away = (self.keep.astype(f32) + self.came[0].astype(f32)).astype(bf16)
        first = away.shape[0] * eighths // 8
        self.came = [flip(part) for part in (away[:first], away[first:]) if part.shape[0] > 0]

    def first_side(self, values):
        *values, self.came[0] = lax.optimization_barrier((*values, self.came[0]))
        return values

    def own_cores(self, own):
        self.total = own[0].astype(f32)
        self.own_came = hop(own[1], 1)

    def meet(self):
        self.came = [jnp.concatenate(self.came, 0), self.own_came]

    def settle(self):
        for rows in self.came:
            self.total = self.total + rows.astype(f32)

    def scatter(self, group):
        self.settle()
        at, width = group
        pieces, me = 1 << width, member(group)
        low = self.total.astype(bf16)
        self.came = [hop(pick(low, pieces, me ^ j), j << at) for j in range(1, pieces)]
        self.total = pick(self.total, pieces, me)

    def gather(self, k):
        if k == len(self.groups) - 1:
            self.settle()
            self.result = self.total.astype(bf16)
        else:
            self.result = assemble([self.result] + self.came, member(self.groups[k + 1]), bf16)
        at, width = self.groups[k]
        self.came = [hop(self.result, j << at) for j in range(1, 1 << width)]

    def finish(self, **shape):
        return assemble([self.result] + self.came, self.core, f32, **shape)


def assemble(slots, me, dtype, parts=(0,), rows=None, planes=1, beside=1):
    count = len(slots)
    rows = slots[0].shape[0] if rows is None else rows
    width = slots[0].shape[1]
    each = len(parts) // planes // beside

    def kernel(me_ref, *refs):
        step = pl.program_id(0) ^ me_ref[0]
        for j in range(count):

            @pl.when(step == j)
            def _():
                for p, row in enumerate(parts):
                    at, column = p // beside % each * rows, p % beside * width
                    refs[-1][p // beside // each, 0, at : at + rows, column : column + width] = refs[j][
                        row : row + rows, :
                    ].astype(dtype)

    out = pl.pallas_call(
        kernel,
        out_shape=jax.ShapeDtypeStruct((planes, count, each * rows, beside * width), dtype),
        grid_spec=pltpu.PrefetchScalarGridSpec(
            num_scalar_prefetch=1,
            grid=(count,),
            in_specs=[pl.BlockSpec(slot.shape, lambda k, _: (0, 0)) for slot in slots],
            out_specs=pl.BlockSpec((planes, 1, each * rows, beside * width), lambda k, _: (0, k, 0, 0)),
        ),
        compiler_params=pltpu.CompilerParams(vmem_limit_bytes=48 * 1024 * 1024),
        cost_estimate=LIGHT,
        name="assemble",
    )(me[None].astype(jnp.int32), *slots)
    return out.reshape(planes * count * each * rows, beside * width)


class VectorSum:
    def __init__(self, own, other):
        self.total, self.mask = own, 1
        self.came = [flip(other)]

    def hop(self):
        if self.mask < lax.axis_size("dp"):
            self.total = self.total + self.came[0]
            self.came = [hop(self.total, self.mask)]
            self.mask *= 2

    def finish(self):
        while self.mask < lax.axis_size("dp"):
            self.hop()
        return self.total + self.came[0]


def stack_rows(vectors, features):
    count = -(-len(vectors) // 8) * 8
    place = lax.broadcasted_iota(jnp.int32, (count, features), 0)
    out = jnp.zeros((count, features), f32)
    for k, vector in enumerate(vectors):
        out = jnp.where(place == k, vector[None, :], out)
    return out


def normalize(resid, gain, shift):
    average = jnp.mean(resid, -1, keepdims=True)
    centred = resid - average
    inverse = lax.rsqrt(jnp.mean(centred * centred, -1, keepdims=True) + epsilon)
    scaled = centred * inverse
    return (scaled * gain + shift, scaled, inverse)


def head_lanes(shape, head):
    return (lax.broadcasted_iota(jnp.int32, shape, 1) >= HS) == (head == 1)


def only_head(rows, head):
    return jnp.where(head_lanes(rows.shape, head), rows, jnp.zeros_like(rows))


def attend_kernel(length_ref, query_ref, key_ref, value_ref, out_ref):
    total = query_ref.shape[0]
    length = length_ref[pl.program_id(0)]
    step = min(total, 256)
    block = min(total, 128)

    def with_keys(count):
        keys, values = key_ref[:count, :], value_ref[:count, :]
        valid = lax.broadcasted_iota(jnp.int32, (1, count), 1) < length
        for at in range(0, total, step):
            query = query_ref[at : at + step, :] * jnp.bfloat16(0.125)
            parts = []
            for head in range(2):
                scores = jnp.where(valid, dot_t(only_head(query, head), keys), -1000000000.0)
                shifted = jnp.exp(scores - jnp.max(scores, -1, keepdims=True))
                probs = shifted * (1.0 / jnp.sum(shifted, -1, keepdims=True))
                parts.append(dot(probs.astype(bf16), values))
            out_ref[at : at + step, :] = jnp.where(head_lanes(parts[0].shape, 0), *parts).astype(bf16)

    @pl.when(length == 0)
    def _():
        average = jnp.sum(value_ref[...].astype(f32), 0, keepdims=True) * (1.0 / total)
        out_ref[...] = jnp.broadcast_to(average, out_ref.shape).astype(bf16)

    for count in range(block, total + 1, block):
        pl.when((length > count - block) & (length <= count))(lambda count=count: with_keys(count))


def attend(qkv, own_len):
    _, tokens, width = qkv.shape
    seqs = own_len.shape[0]
    length, pairs = tokens // seqs, width // (2 * HS)
    block = (length, 2 * HS)
    return pl.pallas_call(
        attend_kernel,
        out_shape=jax.ShapeDtypeStruct((tokens, width), bf16),
        grid_spec=pltpu.PrefetchScalarGridSpec(
            num_scalar_prefetch=1,
            grid=(seqs, pairs),
            in_specs=[pl.BlockSpec((None,) + block, lambda s, p, _, c=c: (c, s, p)) for c in range(3)],
            out_specs=pl.BlockSpec(block, lambda s, p, _: (s, p)),
        ),
        compiler_params=pltpu.CompilerParams(vmem_limit_bytes=48 * 1024 * 1024),
        cost_estimate=LIGHT,
        name="attend",
    )(own_len, qkv, qkv, qkv)


def attend_back_kernel(length_ref, query_ref, key_ref, value_ref, g_out_ref, out_ref):
    total = query_ref.shape[0]
    length = length_ref[pl.program_id(0)]
    pair = pl.program_id(1)
    block = min(total, 128)
    lanes = pl.ds(pl.multiple_of(pair * 2 * HS, 2 * HS), 2 * HS)

    def with_keys(count):
        keys, values = key_ref[:count, :], value_ref[:count, :]
        valid = lax.broadcasted_iota(jnp.int32, (count, 1), 0) < length
        step = min(count, 256)
        starts = list(range(0, count, step))
        g_key = jnp.zeros((count, 2 * HS), f32)
        g_value = jnp.zeros((count, 2 * HS), f32)
        for at in starts:
            end = min(at + step, count)
            query = query_ref[at:end, :] * jnp.bfloat16(0.125)
            g_out = g_out_ref[at:end, :]
            g_query = jnp.zeros((end - at, 2 * HS), f32)
            for head in range(2):
                query_head, g_head = only_head(query, head), only_head(g_out, head)
                scores = jnp.where(valid, dot_t(keys, query_head), -1000000000.0)
                shifted = jnp.exp(scores - jnp.max(scores, 0, keepdims=True))
                probs = shifted * (1.0 / jnp.sum(shifted, 0, keepdims=True))
                g_probs = dot_t(values, g_head)
                delta = jnp.sum(g_probs * probs, 0, keepdims=True)
                g_scores = (probs * (g_probs - delta)).astype(bf16)
                g_key = g_key + dot(g_scores, query_head)
                g_value = g_value + dot(probs.astype(bf16), g_head)
                g_query = g_query + t_dot(g_scores, only_head(keys, head))
            out_ref[0, at:end, lanes] = (g_query * 0.125).astype(bf16)
        out_ref[1, :count, lanes] = g_key.astype(bf16)
        out_ref[2, :count, lanes] = g_value.astype(bf16)
        if count < total:
            for c in range(3):
                out_ref[c, count:, lanes] = jnp.zeros((total - count, 2 * HS), bf16)

    @pl.when(length == 0)
    def _():
        for c in range(3):
            out_ref[c, :, lanes] = jnp.zeros((total, 2 * HS), bf16)

    for count in range(block, total + 1, block):
        pl.when((length > count - block) & (length <= count))(lambda count=count: with_keys(count))


def attend_back(qkv, g_out, own_len):
    tokens, width = g_out.shape
    seqs = own_len.shape[0]
    length, pairs = tokens // seqs, width // (2 * HS)
    block = (length, 2 * HS)
    return pl.pallas_call(
        attend_back_kernel,
        out_shape=jax.ShapeDtypeStruct((3, tokens, width), bf16),
        grid_spec=pltpu.PrefetchScalarGridSpec(
            num_scalar_prefetch=1,
            grid=(seqs, pairs),
            in_specs=[pl.BlockSpec((None,) + block, lambda s, p, _, c=c: (c, s, p)) for c in range(3)]
            + [pl.BlockSpec(block, lambda s, p, _: (s, p))],
            out_specs=pl.BlockSpec((3, length, width), lambda s, p, _: (0, s, 0)),
        ),
        compiler_params=pltpu.CompilerParams(vmem_limit_bytes=48 * 1024 * 1024),
        cost_estimate=LIGHT,
        name="attend_back",
    )(own_len, qkv, qkv, qkv, g_out)


def dot(a, b):
    return jnp.dot(a, b, preferred_element_type=f32)


def dot_t(a, b):
    return lax.dot_general(a, b, (((1,), (1,)), ((), ())), preferred_element_type=f32)


def t_dot(a, b):
    return lax.dot_general(a, b, (((0,), (0,)), ((), ())), preferred_element_type=f32)


def gelu_both(inner):
    cumulative = 0.5 * (1.0 + lax.erf(inner * 0.7071067811865476))
    density = 0.3989422804014327 * jnp.exp(-0.5 * inner * inner)
    return inner * cumulative, cumulative + inner * density


def row_block(tokens):
    return min(tokens, 256)


def whole(array):
    return pl.BlockSpec(array.shape, lambda *_: (0,) * array.ndim, pipeline_mode=pl.Buffered(1))


def place_rows(vectors, shape):
    place = lax.broadcasted_iota(jnp.int32, shape, 0)
    out = jnp.zeros(shape, f32)
    for k, vector in enumerate(vectors):
        out = jnp.where(place == k, vector, out)
    return out


def norm_back(grad_rows, gain, scaled, inverse):
    weighted = grad_rows * gain
    return inverse * (
        weighted
        - jnp.mean(weighted, -1, keepdims=True)
        - scaled * jnp.mean(weighted * scaled, -1, keepdims=True)
    )


def first_norm(rows, projs, x, vectors):
    tokens, features = x.shape
    width = rows[0].shape[1]
    block = row_block(tokens)
    vectors = [vector.reshape(1, features) for vector in vectors]

    def kernel(att_a, att_b, proj_a, proj_b, x_ref, bias_ref, gain_ref, shift_ref, resid_ref, low_ref):
        branch = dot(att_a[...], proj_a[...]) + dot(att_b[...], proj_b[...])
        resid = x_ref[...].astype(f32) + branch + bias_ref[...].astype(f32)
        resid_ref[...] = resid
        low_ref[...] = normalize(resid, gain_ref[...].astype(f32), shift_ref[...].astype(f32))[0].astype(bf16)

    def blocks(size):
        return pl.BlockSpec((block, size), lambda k: (k, 0))

    return pl.pallas_call(
        kernel,
        out_shape=(jax.ShapeDtypeStruct((tokens, features), f32), jax.ShapeDtypeStruct((tokens, features), bf16)),
        grid_spec=pl.GridSpec(
            grid=(tokens // block,),
            in_specs=[blocks(width)] * 2 + [whole(proj) for proj in projs] + [blocks(features)]
            + [whole(vector) for vector in vectors],
            out_specs=[blocks(features)] * 2,
        ),
        compiler_params=pltpu.CompilerParams(vmem_limit_bytes=32 * 1024 * 1024),
        cost_estimate=LIGHT,
        name="first_norm",
    )(*rows, *projs, x, *vectors)


def hidden_half(low, up, up_bias, branch=None):
    tokens, features = low.shape
    hidden = up.shape[1]
    block = row_block(tokens)
    cut = min(hidden, 512)

    def kernel(low_ref, up_ref, bias_ref, *refs):
        act_ref, slope_ref = refs[4:6] if branch else refs
        low = low_ref[...]
        for at in range(0, hidden, cut):
            part = slice(at, at + cut)
            act, slope = gelu_both(dot(low, up_ref[:, part]) + bias_ref[:, part].astype(f32))
            act_ref[:, part] = act.astype(bf16)
            slope_ref[:, part] = slope.astype(bf16)
        if branch:
            resid_ref, gain_ref, shift_ref, down_ref = refs[:4]
            normed = normalize(resid_ref[...], gain_ref[...].astype(f32), shift_ref[...].astype(f32))[0]
            refs[6][...] = normed + dot(act_ref[...], down_ref[...])

    def blocks(size):
        return pl.BlockSpec((block, size), lambda k: (k, 0))

    args = [low, up, up_bias.reshape(1, hidden)]
    in_specs = [blocks(features)] + [whole(array) for array in args[1:]]
    out_shape = [jax.ShapeDtypeStruct((tokens, hidden), bf16)] * 2
    out_specs = [blocks(hidden)] * 2
    if branch:
        resid, gain, shift, down = branch
        more = [gain.reshape(1, features), shift.reshape(1, features), down]
        args += [resid] + more
        in_specs += [blocks(features)] + [whole(array) for array in more]
        out_shape.append(jax.ShapeDtypeStruct((tokens, features), f32))
        out_specs.append(blocks(features))
    return pl.pallas_call(
        kernel,
        out_shape=out_shape,
        grid_spec=pl.GridSpec(grid=(tokens // block,), in_specs=in_specs, out_specs=out_specs),
        compiler_params=pltpu.CompilerParams(vmem_limit_bytes=48 * 1024 * 1024),
        cost_estimate=LIGHT,
        name="hidden_half",
    )(*args)


def second_norm(base, act, down, out_grad, vectors, own_len):
    tokens, features = base.shape
    hidden = act.shape[1]
    block = row_block(tokens)
    length = tokens // own_len.shape[0]
    vectors = [vector.reshape(1, features) for vector in vectors]

    def kernel(length_ref, base_ref, act_ref, down_ref, grad_ref, bias_ref, gain_ref, shift_ref, out_ref, back_ref, low_ref, sums_ref):
        step = pl.program_id(0)
        resid = base_ref[...] + dot(act_ref[...], down_ref[...]) + bias_ref[...].astype(f32)
        gain = gain_ref[...].astype(f32)
        normed, scaled, inverse = normalize(resid, gain, shift_ref[...].astype(f32))
        out_ref[...] = normed.astype(bf16)
        at = step * block + lax.broadcasted_iota(jnp.int32, (block, 1), 0)
        live = (at % length) < length_ref[step * block // length]
        grad = jnp.where(live, grad_ref[...].astype(f32), 0.0)
        back = norm_back(grad, gain, scaled, inverse)
        back_ref[...] = back
        low_ref[...] = back.astype(bf16)
        sums = [jnp.sum(rows, 0, keepdims=True) for rows in (back, grad * scaled, grad)]

        @pl.when(step == 0)
        def _():
            sums_ref[...] = jnp.zeros_like(sums_ref)

        sums_ref[...] += place_rows(sums, sums_ref.shape)

    rows = pl.BlockSpec((block, features), lambda k, _: (k, 0))
    return pl.pallas_call(
        kernel,
        out_shape=(
            jax.ShapeDtypeStruct((tokens, features), bf16),
            jax.ShapeDtypeStruct((tokens, features), f32),
            jax.ShapeDtypeStruct((tokens, features), bf16),
            jax.ShapeDtypeStruct((8, features), f32),
        ),
        grid_spec=pltpu.PrefetchScalarGridSpec(
            num_scalar_prefetch=1,
            grid=(tokens // block,),
            in_specs=[rows, pl.BlockSpec((block, hidden), lambda k, _: (k, 0)), whole(down), rows]
            + [whole(vector) for vector in vectors],
            out_specs=[rows, rows, rows, pl.BlockSpec((8, features), lambda k, _: (0, 0))],
        ),
        compiler_params=pltpu.CompilerParams(vmem_limit_bytes=48 * 1024 * 1024),
        cost_estimate=LIGHT,
        name="second_norm",
    )(own_len, base, act, down, out_grad, *vectors)


def hidden_back(low, slopes, downs, own_len):
    tokens, features = low.shape
    hidden = slopes[0].shape[1]
    block = row_block(tokens)
    length = tokens // own_len.shape[0]
    cut = min(hidden, 768)

    def kernel(length_ref, low_ref, slope_a, slope_b, down_a, down_b, pre_a, pre_b, bias_ref):
        step = pl.program_id(0)

        @pl.when(step == 0)
        def _():
            bias_ref[...] = jnp.zeros_like(bias_ref)

        start = step * block
        live = (start % length) < length_ref[start // length]

        @pl.when(live)
        def _():
            low = low_ref[...]
            for k, (slope, down, pre) in enumerate(((slope_a, down_a, pre_a), (slope_b, down_b, pre_b))):
                for at in range(0, hidden, cut):
                    part = slice(at, at + cut)
                    g_pre = (dot_t(low, down[part, :]) * slope[:, part].astype(f32)).astype(bf16)
                    pre[:, part] = g_pre
                    bias_ref[k : k + 1, part] += jnp.sum(g_pre.astype(f32), 0, keepdims=True)

        @pl.when(jnp.logical_not(live))
        def _():
            for ref in (pre_a, pre_b):
                ref[...] = jnp.zeros_like(ref)

    def rows(size):
        return pl.BlockSpec((block, size), lambda k, _: (k, 0))

    return pl.pallas_call(
        kernel,
        out_shape=(
            jax.ShapeDtypeStruct((tokens, hidden), bf16), jax.ShapeDtypeStruct((tokens, hidden), bf16),
            jax.ShapeDtypeStruct((8, hidden), f32),
        ),
        grid_spec=pltpu.PrefetchScalarGridSpec(
            num_scalar_prefetch=1,
            grid=(tokens // block,),
            in_specs=[rows(features), rows(hidden), rows(hidden)] + [whole(down) for down in downs],
            out_specs=[rows(hidden), rows(hidden), pl.BlockSpec((8, hidden), lambda k, _: (0, 0))],
        ),
        compiler_params=pltpu.CompilerParams(vmem_limit_bytes=48 * 1024 * 1024),
        cost_estimate=LIGHT,
        name="hidden_back",
    )(own_len, low, *slopes, *downs)


def first_norm_back(g_resid, g_pres, resid_one, gain, ups, projs, own_len):
    tokens, features = g_resid.shape
    hidden, width = g_pres[0].shape[1], projs[0].shape[0]
    block = row_block(tokens)
    length = tokens // own_len.shape[0]
    gain = gain.reshape(1, features)

    def kernel(
        length_ref, g_ref, pre_a, pre_b, normed_ref, gain_ref, up_a, up_b, proj_a, proj_b,
        resid_ref, low_ref, att_a, att_b, sums_ref,
    ):
        step = pl.program_id(0)

        @pl.when(step == 0)
        def _():
            sums_ref[...] = jnp.zeros_like(sums_ref)

        start = step * block
        live = (start % length) < length_ref[start // length]

        @pl.when(live)
        def _():
            total = g_ref[...] + dot_t(pre_a[...], up_a[...]) + dot_t(pre_b[...], up_b[...])
            gain = gain_ref[...].astype(f32)
            _, scaled, inverse = normalize(normed_ref[...], gain, 0.0)
            back = norm_back(total, gain, scaled, inverse)
            resid_ref[...] = back
            low = back.astype(bf16)
            low_ref[...] = low
            att_a[...] = dot_t(low, proj_a[...]).astype(bf16)
            att_b[...] = dot_t(low, proj_b[...]).astype(bf16)
            sums = [jnp.sum(rows, 0, keepdims=True) for rows in (back, total * scaled, total)]
            sums_ref[...] += place_rows(sums, sums_ref.shape)

        @pl.when(jnp.logical_not(live))
        def _():
            for ref in (resid_ref, low_ref, att_a, att_b):
                ref[...] = jnp.zeros_like(ref)

    def rows(size):
        return pl.BlockSpec((block, size), lambda k, _: (k, 0))

    def shape(size, dtype):
        return jax.ShapeDtypeStruct((tokens, size), dtype)

    return pl.pallas_call(
        kernel,
        out_shape=(
            shape(features, f32), shape(features, bf16), shape(width, bf16), shape(width, bf16),
            jax.ShapeDtypeStruct((8, features), f32),
        ),
        grid_spec=pltpu.PrefetchScalarGridSpec(
            num_scalar_prefetch=1,
            grid=(tokens // block,),
            in_specs=[rows(features), rows(hidden), rows(hidden), rows(features)]
            + [whole(array) for array in (gain, *ups, *projs)],
            out_specs=[
                rows(features), rows(features), rows(width), rows(width), pl.BlockSpec((8, features), lambda k, _: (0, 0)),
            ],
        ),
        compiler_params=pltpu.CompilerParams(vmem_limit_bytes=48 * 1024 * 1024),
        cost_estimate=LIGHT,
        name="first_norm_back",
    )(own_len, g_resid, *g_pres, resid_one, gain, *ups, *projs)


def token_grads(a, b, core):
    tokens, size = a.shape
    width = b.shape[1]
    half = size // 2
    cut = min(width, 768)

    def kernel(core_ref, a_ref, b_ref, keep_ref, sent_ref):
        def product(out_ref):
            flat = a_ref[...].T
            for at in range(0, width, cut):
                out_ref[:, at : at + cut] = dot(flat, b_ref[:, at : at + cut]).astype(bf16)

        mine = pl.program_id(0) == 1
        pl.when(mine)(lambda: product(keep_ref))
        pl.when(jnp.logical_not(mine))(lambda: product(sent_ref))

    return pl.pallas_call(
        kernel,
        out_shape=(jax.ShapeDtypeStruct((half, width), bf16),) * 2,
        grid_spec=pltpu.PrefetchScalarGridSpec(
            num_scalar_prefetch=1,
            grid=(2,),
            in_specs=[pl.BlockSpec((tokens, half), lambda h, core: (0, 1 - (h ^ core[0]))), whole(b)],
            out_specs=[pl.BlockSpec((half, width), lambda h, _: (0, 0))] * 2,
        ),
        compiler_params=pltpu.CompilerParams(vmem_limit_bytes=48 * 1024 * 1024),
        cost_estimate=LIGHT,
        name="token_grads",
    )(core[None], a, b)


def plane_grads(flat, g, att, g_attn, core):
    features, tokens = flat.shape
    planes, _, width = g.shape
    half = features // 2
    rows = att.shape[1] // 2
    beside = features // width

    def kernel(core_ref, flat_ref, g_ref, att_ref, g_attn_ref, keep_ref, sent_ref, last_ref):
        step, plane = pl.program_id(0), pl.program_id(1)
        mine = step == 1

        @pl.when((step == 0) & (plane == 0))
        def _():
            last_ref[...] = t_dot(att_ref[...], g_attn_ref[...]).astype(bf16)

        def product(out_ref):
            at = pl.multiple_of(plane * half, half)
            out_ref[pl.ds(at, half), :] = dot(flat_ref[...], g_ref[...]).astype(bf16)

            @pl.when(plane == 0)
            def _():
                which = 1 - (step ^ core_ref[0])
                for h in range(2):

                    @pl.when(which == h)
                    def _():
                        for k in range(beside):
                            at = planes * half + k * rows
                            out_ref[at : at + rows, :] = last_ref[h * rows : (h + 1) * rows, k * width : (k + 1) * width]

        pl.when(mine)(lambda: product(keep_ref))
        pl.when(jnp.logical_not(mine))(lambda: product(sent_ref))

    size = planes * half + beside * rows
    return pl.pallas_call(
        kernel,
        out_shape=(jax.ShapeDtypeStruct((size, width), bf16),) * 2,
        grid_spec=pltpu.PrefetchScalarGridSpec(
            num_scalar_prefetch=1,
            grid=(2, planes),
            in_specs=[
                pl.BlockSpec((half, tokens), lambda h, c, core: (1 - (h ^ core[0]), 0)),
                pl.BlockSpec((None, tokens, width), lambda h, c, core: (c, 0, 0)),
                whole(att),
                whole(g_attn),
            ],
            out_specs=[pl.BlockSpec((size, width), lambda h, c, core: (0, 0))] * 2,
            scratch_shapes=[pltpu.VMEM((att.shape[1], features), bf16)],
        ),
        compiler_params=pltpu.CompilerParams(vmem_limit_bytes=48 * 1024 * 1024),
        cost_estimate=LIGHT,
        name="plane_grads",
    )(core[None], flat, g, att, g_attn)


def input_grad(g_resid, gs, weights):
    tokens, features = g_resid.shape
    planes, _, width = gs[0].shape
    block = row_block(tokens)

    def kernel(resid_ref, g_a, g_b, weight_a, weight_b, out_ref):
        total = resid_ref[...]
        for g, weight in ((g_a, weight_a), (g_b, weight_b)):
            for c in range(planes):
                total = total + dot_t(g[c], weight[c])
        out_ref[...] = total.astype(bf16)

    rows = pl.BlockSpec((block, features), lambda k: (k, 0))
    plane_rows = pl.BlockSpec((planes, block, width), lambda k: (0, k, 0))
    return pl.pallas_call(
        kernel,
        out_shape=jax.ShapeDtypeStruct((tokens, features), bf16),
        grid_spec=pl.GridSpec(
            grid=(tokens // block,),
            in_specs=[rows, plane_rows, plane_rows] + [whole(weight) for weight in weights],
            out_specs=rows,
        ),
        compiler_params=pltpu.CompilerParams(vmem_limit_bytes=48 * 1024 * 1024),
        cost_estimate=LIGHT,
        name="input_grad",
    )(g_resid, *gs, *weights)


def body(
    hidden_in, seq_lengths, live_seqs, out_grad, query_key_value_matrix, query_bias, value_bias,
    projection_matrix, proj_bias, norm1_gain, norm1_shift, up_matrix, up_bias, down_matrix,
    down_bias, norm2_gain, norm2_shift,
):
    seq_count, length, features = hidden_in.shape
    width = query_key_value_matrix.shape[2]
    heads = width // HS
    tokens = seq_count * length
    side = lax.axis_index("tensor")
    own_len = lax.dynamic_slice_in_dim(seq_lengths, side * seq_count, seq_count)
    owned = lax.dynamic_index_in_dim(live_seqs, side, 0, keepdims=False)
    own_len = jnp.where(lax.iota(jnp.int32, seq_count) < owned, own_len, 0)

    x = hidden_in.reshape(tokens, features)
    core, quarter = lax.axis_index("dp") & 1, lax.axis_index("dp") & 3
    qkv_w = query_key_value_matrix.transpose(1, 0, 2).reshape(3 * features, width)
    qkv_get = Gather(pick(qkv_w, 2, core), False)
    biases = jnp.concatenate([query_bias, value_bias, up_bias])
    biases_o = flip(biases)
    up_get = Gather(pick(up_matrix, 4, quarter), True)

    def project(weight, bias):
        bias = jnp.stack([bias[:width], jnp.zeros((width,), bias.dtype), bias[width : 2 * width]])
        rows = jnp.einsum("tv,cvw->ctw", x, weight.reshape(3, features, width), preferred_element_type=f32)
        return (rows + bias.astype(f32)[:, None, :]).astype(bf16)

    qkv_rows = [project(qkv_w, biases)]
    attended = [attend(qkv_rows[0], own_len)]
    proj_sent, down_sent = pick(projection_matrix, 2, core), pick(down_matrix, 2, core)
    attended[0], proj_sent, down_sent = tie([attended[0], proj_sent, down_sent], qkv_get)
    qkv_get.cores()
    proj_get = Gather(proj_sent, False)
    flat = x.T
    (flat,) = tie([flat], qkv_get)
    qkv_o = qkv_get.finish()
    qkv_rows.append(project(qkv_o, biases_o))
    *qkv_rows, down_sent = tie([*qkv_rows, down_sent], up_get)
    up_get.beside()
    down_get = Gather(down_sent, False)
    attended.append(attend(qkv_rows[1], own_len))
    attended = tie(attended, proj_get)
    proj_get.cores()
    attended = tie(attended, proj_get, up_get)
    up_get.cores()
    projs = [projection_matrix, proj_get.finish()]
    resid_one, normed_low = first_norm(attended, projs, x, [proj_bias, norm1_gain, norm1_shift])
    ups, downs = [up_matrix], [down_matrix]
    act_a, slope_a, base = hidden_half(
        normed_low, up_matrix, biases[2 * width :], (resid_one, norm1_gain, norm1_shift, down_matrix)
    )
    base, normed_low = tie([base, normed_low], up_get, down_get)
    down_get.cores()
    ups.append(up_get.finish())
    act_b, slope_b = hidden_half(normed_low, ups[1], biases_o[2 * width :])
    downs.append(down_get.finish())
    activated, slopes = [act_a, act_b], [slope_a, slope_b]
    out_hidden, g_resid_two, g_mlp, sums_two = second_norm(
        base, act_b, downs[1], out_grad.reshape(tokens, features), [down_bias, norm2_gain, norm2_shift], own_len
    )
    out_hidden = out_hidden.reshape(hidden_in.shape)

    down_sum, up_sum, qkv_sum = Reduction(), Reduction(), Reduction()
    groups = down_sum.groups
    last = len(groups) - 1

    down_sum.cores(token_grads(act_b, g_mlp, core))
    down_own = token_grads(act_a, g_mlp, core)
    g_mlp, *down_own = tie([g_mlp, *down_own], down_sum)
    down_sum.sides(3)
    down_sum.own_cores(down_own)
    g_pre_a, g_pre_b, bias_sums = hidden_back(g_mlp, slopes, downs, own_len)
    g_pre_a, g_pre_b = down_sum.first_side([g_pre_a, g_pre_b])
    up_sum.cores(token_grads(normed_low, g_pre_b, core))
    up_own = token_grads(normed_low, g_pre_a, core)
    down_sum.meet()
    g_resid_two, *up_own = tie([g_resid_two, *up_own], down_sum, up_sum)
    up_sum.sides(8)
    down_sum.scatter(groups[1])
    up_sum.own_cores(up_own)
    g_resid_one, g_attn, att_a, att_b, sums_one = first_norm_back(
        g_resid_two, [g_pre_a, g_pre_b], resid_one, norm1_gain, ups, projs, own_len
    )
    g_qkv_o = attend_back(qkv_rows[1], att_b, own_len)
    (g_qkv_o,) = tie(up_sum.first_side([g_qkv_o]), down_sum)
    for group in groups[2:]:
        down_sum.scatter(group)
    qkv_sum.cores(plane_grads(flat, g_qkv_o, attended[1], g_attn, core))
    up_sum.meet()
    (att_a,) = tie([att_a], up_sum, down_sum, qkv_sum)
    qkv_sum.sides()
    up_sum.scatter(groups[1])
    down_sum.gather(last)
    g_qkv_a = attend_back(qkv_rows[0], att_a, own_len)
    (g_qkv_a,) = qkv_sum.first_side([g_qkv_a])
    g_qkv = [g_qkv_a, g_qkv_o]
    qkv_sum.own_cores(plane_grads(flat, g_qkv_a, attended[0], g_attn, core))
    sums = [jnp.sum(g.astype(f32), 1) for g in g_qkv]
    ups_rows = up_bias.shape[0] // features
    vectors = []
    for k in range(2):
        up_rows = [bias_sums[k, r * features : (r + 1) * features] for r in range(ups_rows)]
        shared = [sums_one[r] for r in range(3)] + [sums_two[r] for r in range(3)]
        vectors.append(stack_rows(shared + up_rows + [jnp.concatenate([sums[k][0], sums[k][2]])], features))
    vector_sum = VectorSum(*vectors)
    grad_hidden = input_grad(g_resid_one, g_qkv, [w.reshape(3, features, width) for w in (qkv_w, qkv_o)])

    def step(*holders):
        tie([], *holders)

    (grad_hidden,) = tie([grad_hidden], up_sum, down_sum)
    qkv_sum.meet()
    for group in groups[2:]:
        up_sum.scatter(group)
    down_sum.gather(last - 1)
    step(qkv_sum, up_sum, down_sum, vector_sum)
    qkv_sum.scatter(groups[1])
    up_sum.gather(last)
    for k in range(last - 2, -1, -1):
        down_sum.gather(k)
    vector_sum.hop()
    step(qkv_sum, up_sum, down_sum, vector_sum)
    down_grad = down_sum.finish()
    for group in groups[2:]:
        qkv_sum.scatter(group)
    up_sum.gather(last - 1)
    vector_sum.hop()
    step(qkv_sum, up_sum, vector_sum)
    qkv_sum.gather(last)
    for k in range(last - 2, -1, -1):
        up_sum.gather(k)
    vector_sum.hop()
    step(qkv_sum, up_sum, vector_sum)
    qkv_sum.gather(last - 1)
    up_grad = up_sum.finish()
    vector_sum.hop()
    step(qkv_sum, vector_sum)
    for k in range(last - 2, -1, -1):
        qkv_sum.gather(k)
    vector = vector_sum.finish()
    half, proj_half = features // 2, width // 2
    qkv_grad = qkv_sum.finish(parts=tuple(c * half for c in range(3)), rows=half, planes=3)
    proj_grad = qkv_sum.finish(
        parts=tuple(3 * half + k * proj_half for k in range(features // width)), rows=proj_half, beside=features // width
    )
    grad_hidden = grad_hidden.reshape(hidden_in.shape)
    return (
        out_hidden,
        grad_hidden,
        qkv_grad.reshape(3, features, width).transpose(1, 0, 2),
        vector[6 + ups_rows, :width],
        vector[6 + ups_rows, width:],
        proj_grad,
        vector[0],
        vector[1],
        vector[2],
        up_grad,
        vector[6 : 6 + ups_rows].reshape(-1),
        down_grad,
        vector[3],
        vector[4],
        vector[5],
    )


def solution(mesh):
    rows = P(("dp", "tensor"), None, None)
    placed = (
        rows, P("dp"), P("dp"), rows, P(None, None, "tensor"), P("tensor"), P("tensor"),
        P("tensor", None), P(), P(), P(), P(None, "tensor"), P("tensor"), P("tensor", None),
        P(), P(), P(),
    )
    outs = (
        rows, rows, P(None, None, "tensor"), P("tensor"), P("tensor"), P("tensor", None), P(), P(),
        P(), P(None, "tensor"), P("tensor"), P("tensor", None), P(), P(), P(),
    )
    return jax.shard_map(body, mesh=mesh, in_specs=placed, out_specs=outs, check_vma=False)
```

```python
import jax
import jax.numpy as jnp
from jax import lax
from jax.experimental import pallas as pl
from jax.experimental.pallas import tpu as pltpu
from jax.sharding import PartitionSpec as P

HS = 64
epsilon = 1e-06
f32 = jnp.float32
bf16 = jnp.bfloat16
LIGHT = pl.CostEstimate(flops=1, bytes_accessed=1, transcendentals=0)


def flip(value):
    return lax.ppermute(value, "tensor", [(0, 1), (1, 0)])


def hop(value, mask):
    count = lax.axis_size("dp")
    return lax.ppermute(value, "dp", [(i, i ^ mask) for i in range(count)])


def dp_groups():
    count = lax.axis_size("dp")
    bits = count.bit_length() - 1
    groups, at = [], 0
    for width in [1, 1] + [2] * bits:
        width = min(width, bits - at)
        if width > 0:
            groups.append((at, width))
        at += width
    return groups


def member(group):
    at, width = group
    return (lax.axis_index("dp") >> at) & ((1 << width) - 1)


def pick(rows, pieces, which):
    count, width = rows.shape
    return lax.dynamic_index_in_dim(rows.reshape(pieces, count // pieces, width), which, 0, keepdims=False)


def tie(values, *holders):
    arrays = list(values) + [array for holder in holders for array in holder.came]
    arrays = list(lax.optimization_barrier(tuple(arrays)))
    at = len(values)
    for holder in holders:
        holder.came = arrays[at : at + len(holder.came)]
        at += len(holder.came)
    return arrays[: len(values)]


def by_bit(bit, zero, one):
    return jnp.where(bit == 0, zero, one)


class Gather:
    def __init__(self, sent, spread):
        self.spread = spread
        self.came = [flip(sent)]

    def beside(self):
        row = member((1, 1))
        (mine,) = self.came
        (other,) = self.came = [hop(mine, 2)]
        self.mine = mine

    def cores(self):
        if self.spread:
            row = member((1, 1))
            (other,) = self.came
            self.parts = [by_bit(row, self.mine, other), by_bit(row, other, self.mine)]
        else:
            self.parts = self.came
        self.came = [hop(part, 1) for part in self.parts]

    def finish(self):
        core = member((0, 1))
        rows = []
        for mine, other in zip(self.parts, self.came):
            rows += [by_bit(core, mine, other), by_bit(core, other, mine)]
        return jnp.concatenate(rows, 0)


class Reduction:
    def __init__(self):
        self.groups = dp_groups()

    def cores(self, other):
        self.core = member(self.groups[0])
        self.keep = other[0]
        self.came = [hop(other[1], 1)]

    def sides(self, eighths=6):
        away = (self.keep.astype(f32) + self.came[0].astype(f32)).astype(bf16)
        first = away.shape[0] * eighths // 8
        self.came = [flip(part) for part in (away[:first], away[first:]) if part.shape[0] > 0]

    def first_side(self, values):
        *values, self.came[0] = lax.optimization_barrier((*values, self.came[0]))
        return values

    def own_cores(self, own):
        self.total = own[0]
        self.own_came = hop(own[1], 1)

    def meet(self):
        self.came = [jnp.concatenate(self.came, 0) if len(self.came) > 1 else self.came[0], self.own_came]

    def scatter(self, group):
        at, width = group
        pieces, me = 1 << width, member(group)
        terms = [self.total] + self.came

        def piece(which):
            return sum(pick(term, pieces, which).astype(f32) for term in terms)

        self.came = [hop(piece(me ^ j).astype(bf16), j << at) for j in range(1, pieces)]
        self.total = piece(me)

    def gather(self, k):
        if k == len(self.groups) - 1:
            self.result = sum(term.astype(f32) for term in [self.total] + self.came).astype(bf16)
        else:
            self.result = assemble([self.result] + self.came, member(self.groups[k + 1]), bf16)
        at, width = self.groups[k]
        self.came = [hop(self.result, j << at) for j in range(1, 1 << width)]

    def finish(self, **shape):
        return assemble([self.result] + self.came, self.core, f32, **shape)


def assemble(slots, me, dtype, parts=(0,), rows=None, planes=1, beside=1):
    count = len(slots)
    rows = slots[0].shape[0] if rows is None else rows
    width = slots[0].shape[1]
    each = len(parts) // planes // beside

    def kernel(me_ref, *refs):
        step = pl.program_id(0) ^ me_ref[0]
        for j in range(count):

            @pl.when(step == j)
            def _():
                for p, row in enumerate(parts):
                    at, column = p // beside % each * rows, p % beside * width
                    refs[-1][p // beside // each, 0, at : at + rows, column : column + width] = refs[j][
                        row : row + rows, :
                    ].astype(dtype)

    out = pl.pallas_call(
        kernel,
        out_shape=jax.ShapeDtypeStruct((planes, count, each * rows, beside * width), dtype),
        grid_spec=pltpu.PrefetchScalarGridSpec(
            num_scalar_prefetch=1,
            grid=(count,),
            in_specs=[pl.BlockSpec(slot.shape, lambda k, _: (0, 0)) for slot in slots],
            out_specs=pl.BlockSpec((planes, 1, each * rows, beside * width), lambda k, _: (0, k, 0, 0)),
        ),
        compiler_params=pltpu.CompilerParams(vmem_limit_bytes=48 * 1024 * 1024),
        cost_estimate=LIGHT,
        name="assemble",
    )(me[None].astype(jnp.int32), *slots)
    return out.reshape(planes * count * each * rows, beside * width)


class VectorSum:
    def __init__(self, own, other):
        self.total, self.mask = own, 1
        self.came = [flip(other)]

    def hop(self):
        if self.mask < lax.axis_size("dp"):
            self.total = self.total + self.came[0]
            self.came = [hop(self.total, self.mask)]
            self.mask *= 2

    def finish(self):
        while self.mask < lax.axis_size("dp"):
            self.hop()
        return self.total + self.came[0]


def stack_rows(vectors, features):
    count = -(-len(vectors) // 8) * 8
    place = lax.broadcasted_iota(jnp.int32, (count, features), 0)
    out = jnp.zeros((count, features), f32)
    for k, vector in enumerate(vectors):
        out = jnp.where(place == k, vector[None, :], out)
    return out


def normalize(resid, gain, shift):
    average = jnp.mean(resid, -1, keepdims=True)
    centred = resid - average
    inverse = lax.rsqrt(jnp.mean(centred * centred, -1, keepdims=True) + epsilon)
    scaled = centred * inverse
    return (scaled * gain + shift, scaled, inverse)


def head_lanes(shape, head):
    return (lax.broadcasted_iota(jnp.int32, shape, 1) >= HS) == (head == 1)


def only_head(rows, head):
    return jnp.where(head_lanes(rows.shape, head), rows, jnp.zeros_like(rows))


def masked(scores, length):
    cut = max(scores.shape[0] - 128, 0)
    place = cut + lax.broadcasted_iota(jnp.int32, (scores.shape[0] - cut, 1), 0)
    last = jnp.where(place < length, scores[cut:], -1000000000.0)
    return jnp.concatenate([scores[:cut], last], 0) if cut else last


def attend_kernel(length_ref, query_ref, key_ref, value_ref, out_ref, log_ref):
    total = query_ref.shape[0]
    length = length_ref[pl.program_id(0)]
    block = min(total, 128)

    def with_keys(count):
        keys, values = key_ref[:count, :], value_ref[:count, :]
        query = query_ref[...] * jnp.bfloat16(0.125)
        out = jnp.zeros((2 * HS, total), f32)
        for head in range(2):
            scores = masked(dot_t(keys, only_head(query, head)), length)
            highest = jnp.max(scores, 0, keepdims=True)
            shifted = jnp.exp(scores - highest)
            sums = jnp.sum(shifted, 0, keepdims=True)
            log_ref[head : head + 1, :] = highest + jnp.log(sums)
            out = out + dot(only_head(values, head).T, shifted.astype(bf16)) * (1.0 / sums)
        out_ref[...] = out.T.astype(bf16)

    @pl.when(length == 0)
    def _():
        average = jnp.sum(value_ref[...].astype(f32), 0, keepdims=True) * (1.0 / total)
        out_ref[...] = jnp.broadcast_to(average, out_ref.shape).astype(bf16)
        log_ref[...] = jnp.zeros_like(log_ref)

    for count in range(block, total + 1, block):
        pl.when((length > count - block) & (length <= count))(lambda count=count: with_keys(count))


def attend(qkv, own_len):
    _, tokens, width = qkv.shape
    seqs = own_len.shape[0]
    length, pairs = tokens // seqs, width // (2 * HS)
    block = (length, 2 * HS)
    return pl.pallas_call(
        attend_kernel,
        out_shape=(
            jax.ShapeDtypeStruct((tokens, width), bf16), jax.ShapeDtypeStruct((seqs, pairs, 2, length), f32)
        ),
        grid_spec=pltpu.PrefetchScalarGridSpec(
            num_scalar_prefetch=1,
            grid=(seqs, pairs),
            in_specs=[pl.BlockSpec((None,) + block, lambda s, p, _, c=c: (c, s, p)) for c in range(3)],
            out_specs=[
                pl.BlockSpec(block, lambda s, p, _: (s, p)),
                pl.BlockSpec((None, None, 2, length), lambda s, p, _: (s, p, 0, 0)),
            ],
        ),
        compiler_params=pltpu.CompilerParams(vmem_limit_bytes=48 * 1024 * 1024),
        cost_estimate=LIGHT,
        name="attend",
    )(own_len, qkv, qkv, qkv)


def attend_back_kernel(length_ref, query_ref, key_ref, value_ref, g_out_ref, log_ref, out_ref):
    total = query_ref.shape[0]
    length = length_ref[pl.program_id(0)]
    pair = pl.program_id(1)
    block = min(total, 128)
    lanes = pl.ds(pl.multiple_of(pair * 2 * HS, 2 * HS), 2 * HS)

    def with_keys(count):
        keys, values = key_ref[:count, :], value_ref[:count, :]
        query = query_ref[:count, :] * jnp.bfloat16(0.125)
        g_out = g_out_ref[:count, :]
        g_key = jnp.zeros((count, 2 * HS), f32)
        g_value = jnp.zeros((count, 2 * HS), f32)
        g_query = jnp.zeros((2 * HS, count), f32)
        for head in range(2):
            query_head, g_head = only_head(query, head), only_head(g_out, head)
            scores = masked(dot_t(keys, query_head), length)
            probs = jnp.exp(scores - log_ref[head : head + 1, :count])
            g_probs = dot_t(values, g_head)
            delta = jnp.sum(g_probs * probs, 0, keepdims=True)
            g_scores = (probs * (g_probs - delta)).astype(bf16)
            g_value = g_value + dot(probs.astype(bf16), g_head)
            g_key = g_key + dot(g_scores, query_head)
            g_query = g_query + dot(only_head(keys, head).T, g_scores)
        out_ref[0, :count, lanes] = (g_query.T * 0.125).astype(bf16)
        out_ref[1, :count, lanes] = g_key.astype(bf16)
        out_ref[2, :count, lanes] = g_value.astype(bf16)
        if count < total:
            for c in range(3):
                out_ref[c, count:, lanes] = jnp.zeros((total - count, 2 * HS), bf16)

    @pl.when(length == 0)
    def _():
        for c in range(3):
            out_ref[c, :, lanes] = jnp.zeros((total, 2 * HS), bf16)

    for count in range(block, total + 1, block):
        pl.when((length > count - block) & (length <= count))(lambda count=count: with_keys(count))


def attend_back(qkv, g_out, logs, own_len):
    tokens, width = g_out.shape
    seqs = own_len.shape[0]
    length, pairs = tokens // seqs, width // (2 * HS)
    block = (length, 2 * HS)
    return pl.pallas_call(
        attend_back_kernel,
        out_shape=jax.ShapeDtypeStruct((3, tokens, width), bf16),
        grid_spec=pltpu.PrefetchScalarGridSpec(
            num_scalar_prefetch=1,
            grid=(seqs, pairs),
            in_specs=[pl.BlockSpec((None,) + block, lambda s, p, _, c=c: (c, s, p)) for c in range(3)]
            + [
                pl.BlockSpec(block, lambda s, p, _: (s, p)),
                pl.BlockSpec((None, None, 2, length), lambda s, p, _: (s, p, 0, 0)),
            ],
            out_specs=pl.BlockSpec((3, length, width), lambda s, p, _: (0, s, 0)),
        ),
        compiler_params=pltpu.CompilerParams(vmem_limit_bytes=48 * 1024 * 1024),
        cost_estimate=LIGHT,
        name="attend_back",
    )(own_len, qkv, qkv, qkv, g_out, logs)


def dot(a, b):
    return jnp.dot(a, b, preferred_element_type=f32)


def dot_t(a, b):
    return lax.dot_general(a, b, (((1,), (1,)), ((), ())), preferred_element_type=f32)


def t_dot(a, b):
    return lax.dot_general(a, b, (((0,), (0,)), ((), ())), preferred_element_type=f32)


def gelu_both(inner):
    cumulative = 0.5 * (1.0 + lax.erf(inner * 0.7071067811865476))
    density = 0.3989422804014327 * jnp.exp(-0.5 * inner * inner)
    return inner * cumulative, cumulative + inner * density


def row_block(tokens):
    return min(tokens, 256)


def whole(array):
    return pl.BlockSpec(array.shape, lambda *_: (0,) * array.ndim, pipeline_mode=pl.Buffered(1))


def place_rows(vectors, shape):
    place = lax.broadcasted_iota(jnp.int32, shape, 0)
    out = jnp.zeros(shape, f32)
    for k, vector in enumerate(vectors):
        out = jnp.where(place == k, vector, out)
    return out


def norm_back(grad_rows, gain, scaled, inverse):
    weighted = grad_rows * gain
    return inverse * (
        weighted
        - jnp.mean(weighted, -1, keepdims=True)
        - scaled * jnp.mean(weighted * scaled, -1, keepdims=True)
    )


def first_norm(rows, projs, x, vectors):
    tokens, features = x.shape
    width = rows[0].shape[1]
    block = row_block(tokens)
    vectors = [vector.reshape(1, features) for vector in vectors]

    def kernel(att_a, att_b, proj_a, proj_b, x_ref, bias_ref, gain_ref, shift_ref, resid_ref, low_ref):
        branch = dot(att_a[...], proj_a[...]) + dot(att_b[...], proj_b[...])
        resid = x_ref[...].astype(f32) + branch + bias_ref[...].astype(f32)
        resid_ref[...] = resid
        low_ref[...] = normalize(resid, gain_ref[...].astype(f32), shift_ref[...].astype(f32))[0].astype(bf16)

    def blocks(size):
        return pl.BlockSpec((block, size), lambda k: (k, 0))

    return pl.pallas_call(
        kernel,
        out_shape=(jax.ShapeDtypeStruct((tokens, features), f32), jax.ShapeDtypeStruct((tokens, features), bf16)),
        grid_spec=pl.GridSpec(
            grid=(tokens // block,),
            in_specs=[blocks(width)] * 2 + [whole(proj) for proj in projs] + [blocks(features)]
            + [whole(vector) for vector in vectors],
            out_specs=[blocks(features)] * 2,
        ),
        compiler_params=pltpu.CompilerParams(vmem_limit_bytes=32 * 1024 * 1024),
        cost_estimate=LIGHT,
        name="first_norm",
    )(*rows, *projs, x, *vectors)


def hidden_half(low, up, up_bias, branch=None):
    tokens, features = low.shape
    hidden = up.shape[1]
    block = row_block(tokens)
    cut = min(hidden, 512)

    def kernel(low_ref, up_ref, bias_ref, *refs):
        act_ref, slope_ref = refs[4:6] if branch else refs
        low = low_ref[...]
        for at in range(0, hidden, cut):
            part = slice(at, at + cut)
            act, slope = gelu_both(dot(low, up_ref[:, part]) + bias_ref[:, part].astype(f32))
            act_ref[:, part] = act.astype(bf16)
            slope_ref[:, part] = slope.astype(bf16)
        if branch:
            resid_ref, gain_ref, shift_ref, down_ref = refs[:4]
            normed = normalize(resid_ref[...], gain_ref[...].astype(f32), shift_ref[...].astype(f32))[0]
            refs[6][...] = normed + dot(act_ref[...], down_ref[...])

    def blocks(size):
        return pl.BlockSpec((block, size), lambda k: (k, 0))

    args = [low, up, up_bias.reshape(1, hidden)]
    in_specs = [blocks(features)] + [whole(array) for array in args[1:]]
    out_shape = [jax.ShapeDtypeStruct((tokens, hidden), bf16)] * 2
    out_specs = [blocks(hidden)] * 2
    if branch:
        resid, gain, shift, down = branch
        more = [gain.reshape(1, features), shift.reshape(1, features), down]
        args += [resid] + more
        in_specs += [blocks(features)] + [whole(array) for array in more]
        out_shape.append(jax.ShapeDtypeStruct((tokens, features), f32))
        out_specs.append(blocks(features))
    return pl.pallas_call(
        kernel,
        out_shape=out_shape,
        grid_spec=pl.GridSpec(grid=(tokens // block,), in_specs=in_specs, out_specs=out_specs),
        compiler_params=pltpu.CompilerParams(vmem_limit_bytes=48 * 1024 * 1024),
        cost_estimate=LIGHT,
        name="hidden_half",
    )(*args)


def second_norm(base, act, down, out_grad, vectors, own_len):
    tokens, features = base.shape
    hidden = act.shape[1]
    block = row_block(tokens)
    length = tokens // own_len.shape[0]
    vectors = [vector.reshape(1, features) for vector in vectors]

    def kernel(length_ref, base_ref, act_ref, down_ref, grad_ref, bias_ref, gain_ref, shift_ref, out_ref, back_ref, low_ref, sums_ref):
        step = pl.program_id(0)
        resid = base_ref[...] + dot(act_ref[...], down_ref[...]) + bias_ref[...].astype(f32)
        gain = gain_ref[...].astype(f32)
        normed, scaled, inverse = normalize(resid, gain, shift_ref[...].astype(f32))
        out_ref[...] = normed.astype(bf16)
        at = step * block + lax.broadcasted_iota(jnp.int32, (block, 1), 0)
        live = (at % length) < length_ref[step * block // length]
        grad = jnp.where(live, grad_ref[...].astype(f32), 0.0)
        back = norm_back(grad, gain, scaled, inverse)
        back_ref[...] = back
        low_ref[...] = back.astype(bf16)
        sums = [jnp.sum(rows, 0, keepdims=True) for rows in (back, grad * scaled, grad)]

        @pl.when(step == 0)
        def _():
            sums_ref[...] = jnp.zeros_like(sums_ref)

        sums_ref[...] += place_rows(sums, sums_ref.shape)

    rows = pl.BlockSpec((block, features), lambda k, _: (k, 0))
    return pl.pallas_call(
        kernel,
        out_shape=(
            jax.ShapeDtypeStruct((tokens, features), bf16),
            jax.ShapeDtypeStruct((tokens, features), f32),
            jax.ShapeDtypeStruct((tokens, features), bf16),
            jax.ShapeDtypeStruct((8, features), f32),
        ),
        grid_spec=pltpu.PrefetchScalarGridSpec(
            num_scalar_prefetch=1,
            grid=(tokens // block,),
            in_specs=[rows, pl.BlockSpec((block, hidden), lambda k, _: (k, 0)), whole(down), rows]
            + [whole(vector) for vector in vectors],
            out_specs=[rows, rows, rows, pl.BlockSpec((8, features), lambda k, _: (0, 0))],
        ),
        compiler_params=pltpu.CompilerParams(vmem_limit_bytes=48 * 1024 * 1024),
        cost_estimate=LIGHT,
        name="second_norm",
    )(own_len, base, act, down, out_grad, *vectors)


def hidden_back(low, slopes, downs, own_len):
    tokens, features = low.shape
    hidden = slopes[0].shape[1]
    block = row_block(tokens)
    length = tokens // own_len.shape[0]
    cut = min(hidden, 768)

    def kernel(length_ref, low_ref, slope_a, slope_b, down_a, down_b, pre_a, pre_b, bias_ref):
        step = pl.program_id(0)

        @pl.when(step == 0)
        def _():
            bias_ref[...] = jnp.zeros_like(bias_ref)

        start = step * block
        live = (start % length) < length_ref[start // length]

        @pl.when(live)
        def _():
            low = low_ref[...]
            for k, (slope, down, pre) in enumerate(((slope_a, down_a, pre_a), (slope_b, down_b, pre_b))):
                for at in range(0, hidden, cut):
                    part = slice(at, at + cut)
                    g_pre = (dot_t(low, down[part, :]) * slope[:, part].astype(f32)).astype(bf16)
                    pre[:, part] = g_pre
                    bias_ref[k : k + 1, part] += jnp.sum(g_pre.astype(f32), 0, keepdims=True)

        @pl.when(jnp.logical_not(live))
        def _():
            for ref in (pre_a, pre_b):
                ref[...] = jnp.zeros_like(ref)

    def rows(size):
        return pl.BlockSpec((block, size), lambda k, _: (k, 0))

    return pl.pallas_call(
        kernel,
        out_shape=(
            jax.ShapeDtypeStruct((tokens, hidden), bf16), jax.ShapeDtypeStruct((tokens, hidden), bf16),
            jax.ShapeDtypeStruct((8, hidden), f32),
        ),
        grid_spec=pltpu.PrefetchScalarGridSpec(
            num_scalar_prefetch=1,
            grid=(tokens // block,),
            in_specs=[rows(features), rows(hidden), rows(hidden)] + [whole(down) for down in downs],
            out_specs=[rows(hidden), rows(hidden), pl.BlockSpec((8, hidden), lambda k, _: (0, 0))],
        ),
        compiler_params=pltpu.CompilerParams(vmem_limit_bytes=48 * 1024 * 1024),
        cost_estimate=LIGHT,
        name="hidden_back",
    )(own_len, low, *slopes, *downs)


def first_norm_back(g_resid, g_pres, resid_one, gain, ups, projs, own_len):
    tokens, features = g_resid.shape
    hidden, width = g_pres[0].shape[1], projs[0].shape[0]
    block = row_block(tokens)
    length = tokens // own_len.shape[0]
    gain = gain.reshape(1, features)

    def kernel(
        length_ref, g_ref, pre_a, pre_b, normed_ref, gain_ref, up_a, up_b, proj_a, proj_b,
        resid_ref, low_ref, att_a, att_b, sums_ref,
    ):
        step = pl.program_id(0)

        @pl.when(step == 0)
        def _():
            sums_ref[...] = jnp.zeros_like(sums_ref)

        start = step * block
        live = (start % length) < length_ref[start // length]

        @pl.when(live)
        def _():
            total = g_ref[...] + dot_t(pre_a[...], up_a[...]) + dot_t(pre_b[...], up_b[...])
            gain = gain_ref[...].astype(f32)
            _, scaled, inverse = normalize(normed_ref[...], gain, 0.0)
            back = norm_back(total, gain, scaled, inverse)
            resid_ref[...] = back
            low = back.astype(bf16)
            low_ref[...] = low
            att_a[...] = dot_t(low, proj_a[...]).astype(bf16)
            att_b[...] = dot_t(low, proj_b[...]).astype(bf16)
            sums = [jnp.sum(rows, 0, keepdims=True) for rows in (back, total * scaled, total)]
            sums_ref[...] += place_rows(sums, sums_ref.shape)

        @pl.when(jnp.logical_not(live))
        def _():
            for ref in (resid_ref, low_ref, att_a, att_b):
                ref[...] = jnp.zeros_like(ref)

    def rows(size):
        return pl.BlockSpec((block, size), lambda k, _: (k, 0))

    def shape(size, dtype):
        return jax.ShapeDtypeStruct((tokens, size), dtype)

    return pl.pallas_call(
        kernel,
        out_shape=(
            shape(features, f32), shape(features, bf16), shape(width, bf16), shape(width, bf16),
            jax.ShapeDtypeStruct((8, features), f32),
        ),
        grid_spec=pltpu.PrefetchScalarGridSpec(
            num_scalar_prefetch=1,
            grid=(tokens // block,),
            in_specs=[rows(features), rows(hidden), rows(hidden), rows(features)]
            + [whole(array) for array in (gain, *ups, *projs)],
            out_specs=[
                rows(features), rows(features), rows(width), rows(width), pl.BlockSpec((8, features), lambda k, _: (0, 0)),
            ],
        ),
        compiler_params=pltpu.CompilerParams(vmem_limit_bytes=48 * 1024 * 1024),
        cost_estimate=LIGHT,
        name="first_norm_back",
    )(own_len, g_resid, *g_pres, resid_one, gain, *ups, *projs)


def token_grads(a, b, core):
    tokens, size = a.shape
    width = b.shape[1]
    half = size // 2
    cut = min(width, 768)

    def kernel(core_ref, a_ref, b_ref, keep_ref, sent_ref):
        def product(out_ref):
            flat = a_ref[...].T
            for at in range(0, width, cut):
                out_ref[:, at : at + cut] = dot(flat, b_ref[:, at : at + cut]).astype(bf16)

        mine = pl.program_id(0) == 1
        pl.when(mine)(lambda: product(keep_ref))
        pl.when(jnp.logical_not(mine))(lambda: product(sent_ref))

    return pl.pallas_call(
        kernel,
        out_shape=(jax.ShapeDtypeStruct((half, width), bf16),) * 2,
        grid_spec=pltpu.PrefetchScalarGridSpec(
            num_scalar_prefetch=1,
            grid=(2,),
            in_specs=[pl.BlockSpec((tokens, half), lambda h, core: (0, 1 - (h ^ core[0]))), whole(b)],
            out_specs=[pl.BlockSpec((half, width), lambda h, _: (0, 0))] * 2,
        ),
        compiler_params=pltpu.CompilerParams(vmem_limit_bytes=48 * 1024 * 1024),
        cost_estimate=LIGHT,
        name="token_grads",
    )(core[None], a, b)


def plane_grads(flat, g, att, g_attn, core):
    features, tokens = flat.shape
    planes, _, width = g.shape
    half = features // 2
    rows = att.shape[1] // 2
    beside = features // width

    def kernel(core_ref, flat_ref, g_ref, att_ref, g_attn_ref, keep_ref, sent_ref, last_ref):
        step, plane = pl.program_id(0), pl.program_id(1)
        mine = step == 1

        @pl.when((step == 0) & (plane == 0))
        def _():
            last_ref[...] = t_dot(att_ref[...], g_attn_ref[...]).astype(bf16)

        def product(out_ref):
            at = pl.multiple_of(plane * half, half)
            out_ref[pl.ds(at, half), :] = dot(flat_ref[...], g_ref[...]).astype(bf16)

            @pl.when(plane == 0)
            def _():
                which = 1 - (step ^ core_ref[0])
                for h in range(2):

                    @pl.when(which == h)
                    def _():
                        for k in range(beside):
                            at = planes * half + k * rows
                            out_ref[at : at + rows, :] = last_ref[h * rows : (h + 1) * rows, k * width : (k + 1) * width]

        pl.when(mine)(lambda: product(keep_ref))
        pl.when(jnp.logical_not(mine))(lambda: product(sent_ref))

    size = planes * half + beside * rows
    return pl.pallas_call(
        kernel,
        out_shape=(jax.ShapeDtypeStruct((size, width), bf16),) * 2,
        grid_spec=pltpu.PrefetchScalarGridSpec(
            num_scalar_prefetch=1,
            grid=(2, planes),
            in_specs=[
                pl.BlockSpec((half, tokens), lambda h, c, core: (1 - (h ^ core[0]), 0)),
                pl.BlockSpec((None, tokens, width), lambda h, c, core: (c, 0, 0)),
                whole(att),
                whole(g_attn),
            ],
            out_specs=[pl.BlockSpec((size, width), lambda h, c, core: (0, 0))] * 2,
            scratch_shapes=[pltpu.VMEM((att.shape[1], features), bf16)],
        ),
        compiler_params=pltpu.CompilerParams(vmem_limit_bytes=48 * 1024 * 1024),
        cost_estimate=LIGHT,
        name="plane_grads",
    )(core[None], flat, g, att, g_attn)


def input_grad(g_resid, gs, weights):
    tokens, features = g_resid.shape
    planes, _, width = gs[0].shape
    block = row_block(tokens)

    def kernel(resid_ref, g_a, g_b, weight_a, weight_b, out_ref):
        total = resid_ref[...]
        for g, weight in ((g_a, weight_a), (g_b, weight_b)):
            for c in range(planes):
                total = total + dot_t(g[c], weight[c])
        out_ref[...] = total.astype(bf16)

    rows = pl.BlockSpec((block, features), lambda k: (k, 0))
    plane_rows = pl.BlockSpec((planes, block, width), lambda k: (0, k, 0))
    return pl.pallas_call(
        kernel,
        out_shape=jax.ShapeDtypeStruct((tokens, features), bf16),
        grid_spec=pl.GridSpec(
            grid=(tokens // block,),
            in_specs=[rows, plane_rows, plane_rows] + [whole(weight) for weight in weights],
            out_specs=rows,
        ),
        compiler_params=pltpu.CompilerParams(vmem_limit_bytes=48 * 1024 * 1024),
        cost_estimate=LIGHT,
        name="input_grad",
    )(g_resid, *gs, *weights)


def body(
    hidden_in, seq_lengths, live_seqs, out_grad, query_key_value_matrix, query_bias, value_bias,
    projection_matrix, proj_bias, norm1_gain, norm1_shift, up_matrix, up_bias, down_matrix,
    down_bias, norm2_gain, norm2_shift,
):
    seq_count, length, features = hidden_in.shape
    width = query_key_value_matrix.shape[2]
    heads = width // HS
    tokens = seq_count * length
    side = lax.axis_index("tensor")
    own_len = lax.dynamic_slice_in_dim(seq_lengths, side * seq_count, seq_count)
    owned = lax.dynamic_index_in_dim(live_seqs, side, 0, keepdims=False)
    own_len = jnp.where(lax.iota(jnp.int32, seq_count) < owned, own_len, 0)

    x = hidden_in.reshape(tokens, features)
    core, quarter = lax.axis_index("dp") & 1, lax.axis_index("dp") & 3
    qkv_w = query_key_value_matrix.transpose(1, 0, 2).reshape(3 * features, width)
    qkv_get = Gather(pick(qkv_w, 2, core), False)
    biases = jnp.concatenate([query_bias, value_bias, up_bias])
    biases_o = flip(biases)
    up_get = Gather(pick(up_matrix, 4, quarter), True)

    def project(weight, bias):
        bias = jnp.stack([bias[:width], jnp.zeros((width,), bias.dtype), bias[width : 2 * width]])
        rows = jnp.einsum("tv,cvw->ctw", x, weight.reshape(3, features, width), preferred_element_type=f32)
        return (rows + bias.astype(f32)[:, None, :]).astype(bf16)

    qkv_rows = [project(qkv_w, biases)]
    rows, logs_a = attend(qkv_rows[0], own_len)
    attended = [rows]
    proj_sent, down_sent = pick(projection_matrix, 2, core), pick(down_matrix, 2, core)
    attended[0], proj_sent, down_sent = tie([attended[0], proj_sent, down_sent], qkv_get)
    qkv_get.cores()
    proj_get = Gather(proj_sent, False)
    flat = x.T
    (flat,) = tie([flat], qkv_get)
    qkv_o = qkv_get.finish()
    qkv_rows.append(project(qkv_o, biases_o))
    *qkv_rows, down_sent = tie([*qkv_rows, down_sent], up_get)
    up_get.beside()
    down_get = Gather(down_sent, False)
    rows, logs_b = attend(qkv_rows[1], own_len)
    attended.append(rows)
    attended = tie(attended, proj_get)
    proj_get.cores()
    attended = tie(attended, proj_get, up_get)
    up_get.cores()
    projs = [projection_matrix, proj_get.finish()]
    resid_one, normed_low = first_norm(attended, projs, x, [proj_bias, norm1_gain, norm1_shift])
    ups, downs = [up_matrix], [down_matrix]
    act_a, slope_a, base = hidden_half(
        normed_low, up_matrix, biases[2 * width :], (resid_one, norm1_gain, norm1_shift, down_matrix)
    )
    base, normed_low = tie([base, normed_low], up_get, down_get)
    down_get.cores()
    ups.append(up_get.finish())
    act_b, slope_b = hidden_half(normed_low, ups[1], biases_o[2 * width :])
    downs.append(down_get.finish())
    activated, slopes = [act_a, act_b], [slope_a, slope_b]
    out_hidden, g_resid_two, g_mlp, sums_two = second_norm(
        base, act_b, downs[1], out_grad.reshape(tokens, features), [down_bias, norm2_gain, norm2_shift], own_len
    )
    out_hidden = out_hidden.reshape(hidden_in.shape)

    down_sum, up_sum, qkv_sum = Reduction(), Reduction(), Reduction()
    groups = down_sum.groups
    last = len(groups) - 1

    down_sum.cores(token_grads(act_b, g_mlp, core))
    down_own = token_grads(act_a, g_mlp, core)
    g_mlp, *down_own = tie([g_mlp, *down_own], down_sum)
    down_sum.sides(5)
    down_sum.own_cores(down_own)
    g_pre_a, g_pre_b, bias_sums = hidden_back(g_mlp, slopes, downs, own_len)
    up_other = token_grads(normed_low, g_pre_b, core)
    g_pre_a, *up_other = down_sum.first_side([g_pre_a, *up_other])
    up_sum.cores(up_other)
    up_own = token_grads(normed_low, g_pre_a, core)
    down_sum.meet()
    g_resid_two, *up_own = tie([g_resid_two, *up_own], down_sum, up_sum)
    up_sum.sides(8)
    down_sum.scatter(groups[1])
    up_sum.own_cores(up_own)
    g_resid_one, g_attn, att_a, att_b, sums_one = first_norm_back(
        g_resid_two, [g_pre_a, g_pre_b], resid_one, norm1_gain, ups, projs, own_len
    )
    g_qkv_o = attend_back(qkv_rows[1], att_b, logs_b, own_len)
    up_sum.meet()
    (g_qkv_o,) = tie([g_qkv_o], up_sum, down_sum)
    up_sum.scatter(groups[1])
    for group in groups[2:]:
        down_sum.scatter(group)
    qkv_sum.cores(plane_grads(flat, g_qkv_o, attended[1], g_attn, core))
    (att_a,) = tie([att_a], up_sum, down_sum, qkv_sum)
    qkv_sum.sides(4)
    down_sum.gather(last)
    g_qkv_a = attend_back(qkv_rows[0], att_a, logs_a, own_len)
    (g_qkv_a,) = qkv_sum.first_side([g_qkv_a])
    g_qkv = [g_qkv_a, g_qkv_o]
    qkv_own = tie(plane_grads(flat, g_qkv_a, attended[0], g_attn, core), down_sum, up_sum)
    qkv_sum.own_cores(qkv_own)
    for group in groups[2:]:
        up_sum.scatter(group)
    sums = [jnp.sum(g.astype(f32), 1) for g in g_qkv]
    ups_rows = up_bias.shape[0] // features
    vectors = []
    for k in range(2):
        up_rows = [bias_sums[k, r * features : (r + 1) * features] for r in range(ups_rows)]
        shared = [sums_one[r] for r in range(3)] + [sums_two[r] for r in range(3)]
        vectors.append(stack_rows(shared + up_rows + [jnp.concatenate([sums[k][0], sums[k][2]])], features))
    vector_sum = VectorSum(*vectors)
    grad_hidden = input_grad(g_resid_one, g_qkv, [w.reshape(3, features, width) for w in (qkv_w, qkv_o)])

    def step():
        tie([], qkv_sum, up_sum, down_sum, vector_sum)

    qkv_sum.meet()
    (grad_hidden,) = tie([grad_hidden], qkv_sum, up_sum, down_sum, vector_sum)
    qkv_sum.scatter(groups[1])
    up_sum.gather(last)
    vector_sum.hop()
    step()
    for group in groups[2:]:
        qkv_sum.scatter(group)
    for k in range(last - 1, 0, -1):
        down_sum.gather(k)
    vector_sum.hop()
    step()
    qkv_sum.gather(last)
    for k in range(last - 1, 0, -1):
        up_sum.gather(k)
    down_sum.gather(0)
    vector_sum.hop()
    step()
    for k in range(last - 1, 0, -1):
        qkv_sum.gather(k)
    up_sum.gather(0)
    down_grad = down_sum.finish()
    vector_sum.hop()
    step()
    qkv_sum.gather(0)
    up_grad = up_sum.finish()
    vector = vector_sum.finish()
    half, proj_half = features // 2, width // 2
    qkv_grad = qkv_sum.finish(parts=tuple(c * half for c in range(3)), rows=half, planes=3)
    proj_grad = qkv_sum.finish(
        parts=tuple(3 * half + k * proj_half for k in range(features // width)), rows=proj_half, beside=features // width
    )
    grad_hidden = grad_hidden.reshape(hidden_in.shape)
    return (
        out_hidden,
        grad_hidden,
        qkv_grad.reshape(3, features, width).transpose(1, 0, 2),
        vector[6 + ups_rows, :width],
        vector[6 + ups_rows, width:],
        proj_grad,
        vector[0],
        vector[1],
        vector[2],
        up_grad,
        vector[6 : 6 + ups_rows].reshape(-1),
        down_grad,
        vector[3],
        vector[4],
        vector[5],
    )


def solution(mesh):
    rows = P(("dp", "tensor"), None, None)
    placed = (
        rows, P("dp"), P("dp"), rows, P(None, None, "tensor"), P("tensor"), P("tensor"),
        P("tensor", None), P(), P(), P(), P(None, "tensor"), P("tensor"), P("tensor", None),
        P(), P(), P(),
    )
    outs = (
        rows, rows, P(None, None, "tensor"), P("tensor"), P("tensor"), P("tensor", None), P(), P(),
        P(), P(None, "tensor"), P("tensor"), P("tensor", None), P(), P(), P(),
    )
    return jax.shard_map(body, mesh=mesh, in_specs=placed, out_specs=outs, check_vma=False)
```

```python
import jax
import jax.numpy as jnp
from jax import lax
from jax.experimental import pallas as pl
from jax.experimental.pallas import tpu as pltpu
from jax.sharding import PartitionSpec as P

HS = 64
epsilon = 1e-06
f32 = jnp.float32
bf16 = jnp.bfloat16
LIGHT = pl.CostEstimate(flops=1, bytes_accessed=1, transcendentals=0)


def flip(value):
    return lax.ppermute(value, "tensor", [(0, 1), (1, 0)])


def hop(value, mask):
    count = lax.axis_size("dp")
    return lax.ppermute(value, "dp", [(i, i ^ mask) for i in range(count)])


def dp_groups():
    count = lax.axis_size("dp")
    bits = count.bit_length() - 1
    groups, at = [], 0
    for width in [1, 1] + [2] * bits:
        width = min(width, bits - at)
        if width > 0:
            groups.append((at, width))
        at += width
    return groups


def member(group):
    at, width = group
    return (lax.axis_index("dp") >> at) & ((1 << width) - 1)


def pick(rows, pieces, which):
    count, width = rows.shape
    return lax.dynamic_index_in_dim(rows.reshape(pieces, count // pieces, width), which, 0, keepdims=False)


def tie(values, *holders):
    arrays = list(values) + [array for holder in holders for array in holder.came]
    arrays = list(lax.optimization_barrier(tuple(arrays)))
    at = len(values)
    for holder in holders:
        holder.came = arrays[at : at + len(holder.came)]
        at += len(holder.came)
    return arrays[: len(values)]


def by_bit(bit, zero, one):
    return jnp.where(bit == 0, zero, one)


class Gather:
    def __init__(self, sent, spread):
        self.spread = spread
        self.came = [flip(sent)]

    def beside(self):
        row = member((1, 1))
        (mine,) = self.came
        (other,) = self.came = [hop(mine, 2)]
        self.mine = mine

    def cores(self):
        if self.spread:
            row = member((1, 1))
            (other,) = self.came
            self.parts = [by_bit(row, self.mine, other), by_bit(row, other, self.mine)]
        else:
            self.parts = self.came
        self.came = [hop(part, 1) for part in self.parts]

    def finish(self):
        core = member((0, 1))
        rows = []
        for mine, other in zip(self.parts, self.came):
            rows += [by_bit(core, mine, other), by_bit(core, other, mine)]
        return jnp.concatenate(rows, 0)


class Reduction:
    def __init__(self):
        self.groups = dp_groups()

    def cores(self, other):
        self.core = member(self.groups[0])
        self.keep = other[0]
        self.came = [hop(other[1], 1)]

    def sides(self, eighths=6):
        away = (self.keep.astype(f32) + self.came[0].astype(f32)).astype(bf16)
        first = away.shape[0] * eighths // 8
        self.came = [flip(part) for part in (away[:first], away[first:]) if part.shape[0] > 0]

    def first_side(self, values):
        *values, self.came[0] = lax.optimization_barrier((*values, self.came[0]))
        return values

    def own_cores(self, own):
        self.total = own[0]
        self.own_came = hop(own[1], 1)

    def meet(self):
        self.came = [jnp.concatenate(self.came, 0) if len(self.came) > 1 else self.came[0], self.own_came]

    def scatter(self, group):
        at, width = group
        pieces, me = 1 << width, member(group)
        terms = [self.total] + self.came

        def piece(which):
            return sum(pick(term, pieces, which).astype(f32) for term in terms)

        self.came = [hop(piece(me ^ j).astype(bf16), j << at) for j in range(1, pieces)]
        self.total = piece(me)

    def gather(self, k):
        if k == len(self.groups) - 1:
            self.result = sum(term.astype(f32) for term in [self.total] + self.came).astype(bf16)
        else:
            self.result = assemble([self.result] + self.came, member(self.groups[k + 1]), bf16)
        at, width = self.groups[k]
        self.came = [hop(self.result, j << at) for j in range(1, 1 << width)]

    def finish(self, **shape):
        return assemble([self.result] + self.came, self.core, f32, **shape)


def assemble(slots, me, dtype, parts=(0,), rows=None, planes=1, beside=1):
    count = len(slots)
    rows = slots[0].shape[0] if rows is None else rows
    width = slots[0].shape[1]
    each = len(parts) // planes // beside

    def kernel(me_ref, *refs):
        step = pl.program_id(0) ^ me_ref[0]
        for j in range(count):

            @pl.when(step == j)
            def _():
                for p, row in enumerate(parts):
                    at, column = p // beside % each * rows, p % beside * width
                    refs[-1][p // beside // each, 0, at : at + rows, column : column + width] = refs[j][
                        row : row + rows, :
                    ].astype(dtype)

    out = pl.pallas_call(
        kernel,
        out_shape=jax.ShapeDtypeStruct((planes, count, each * rows, beside * width), dtype),
        grid_spec=pltpu.PrefetchScalarGridSpec(
            num_scalar_prefetch=1,
            grid=(count,),
            in_specs=[pl.BlockSpec(slot.shape, lambda k, _: (0, 0)) for slot in slots],
            out_specs=pl.BlockSpec((planes, 1, each * rows, beside * width), lambda k, _: (0, k, 0, 0)),
        ),
        compiler_params=pltpu.CompilerParams(vmem_limit_bytes=48 * 1024 * 1024),
        cost_estimate=LIGHT,
        name="assemble",
    )(me[None].astype(jnp.int32), *slots)
    return out.reshape(planes * count * each * rows, beside * width)


class VectorSum:
    def __init__(self, own, other):
        self.total, self.mask = own, 1
        self.came = [flip(other)]

    def hop(self):
        if self.mask < lax.axis_size("dp"):
            self.total = self.total + self.came[0]
            self.came = [hop(self.total, self.mask)]
            self.mask *= 2

    def finish(self):
        while self.mask < lax.axis_size("dp"):
            self.hop()
        return self.total + self.came[0]


def stack_rows(vectors, features):
    count = -(-len(vectors) // 8) * 8
    place = lax.broadcasted_iota(jnp.int32, (count, features), 0)
    out = jnp.zeros((count, features), f32)
    for k, vector in enumerate(vectors):
        out = jnp.where(place == k, vector[None, :], out)
    return out


def normalize(resid, gain, shift):
    average = jnp.mean(resid, -1, keepdims=True)
    centred = resid - average
    inverse = lax.rsqrt(jnp.mean(centred * centred, -1, keepdims=True) + epsilon)
    scaled = centred * inverse
    return (scaled * gain + shift, scaled, inverse)


def head_lanes(shape, head):
    return (lax.broadcasted_iota(jnp.int32, shape, 1) >= HS) == (head == 1)


def only_head(rows, head):
    return jnp.where(head_lanes(rows.shape, head), rows, jnp.zeros_like(rows))


def masked(scores, length):
    cut = max(scores.shape[0] - 128, 0)
    place = cut + lax.broadcasted_iota(jnp.int32, (scores.shape[0] - cut, 1), 0)
    last = jnp.where(place < length, scores[cut:], -1000000000.0)
    return jnp.concatenate([scores[:cut], last], 0) if cut else last


def attend_kernel(length_ref, query_ref, key_ref, value_ref, out_ref, log_ref):
    total = query_ref.shape[0]
    length = length_ref[pl.program_id(0)]
    block = min(total, 128)

    def with_keys(count):
        keys, values = key_ref[:count, :], value_ref[:count, :]
        query = query_ref[...] * jnp.bfloat16(0.125)
        out = jnp.zeros((2 * HS, total), f32)
        for head in range(2):
            scores = masked(dot_t(keys, only_head(query, head)), length)
            highest = jnp.max(scores, 0, keepdims=True)
            shifted = jnp.exp(scores - highest)
            sums = jnp.sum(shifted, 0, keepdims=True)
            log_ref[head : head + 1, :] = highest + jnp.log(sums)
            out = out + dot(only_head(values, head).T, shifted.astype(bf16)) * (1.0 / sums)
        out_ref[...] = out.T.astype(bf16)

    @pl.when(length == 0)
    def _():
        average = jnp.sum(value_ref[...].astype(f32), 0, keepdims=True) * (1.0 / total)
        out_ref[...] = jnp.broadcast_to(average, out_ref.shape).astype(bf16)
        log_ref[...] = jnp.zeros_like(log_ref)

    for count in range(block, total + 1, block):
        pl.when((length > count - block) & (length <= count))(lambda count=count: with_keys(count))


def attend(qkv, own_len):
    _, tokens, width = qkv.shape
    seqs = own_len.shape[0]
    length, pairs = tokens // seqs, width // (2 * HS)
    block = (length, 2 * HS)
    return pl.pallas_call(
        attend_kernel,
        out_shape=(
            jax.ShapeDtypeStruct((tokens, width), bf16), jax.ShapeDtypeStruct((seqs, pairs, 2, length), f32)
        ),
        grid_spec=pltpu.PrefetchScalarGridSpec(
            num_scalar_prefetch=1,
            grid=(seqs, pairs),
            in_specs=[pl.BlockSpec((None,) + block, lambda s, p, _, c=c: (c, s, p)) for c in range(3)],
            out_specs=[
                pl.BlockSpec(block, lambda s, p, _: (s, p)),
                pl.BlockSpec((None, None, 2, length), lambda s, p, _: (s, p, 0, 0)),
            ],
        ),
        compiler_params=pltpu.CompilerParams(vmem_limit_bytes=48 * 1024 * 1024),
        cost_estimate=LIGHT,
        name="attend",
    )(own_len, qkv, qkv, qkv)


def attend_back_kernel(length_ref, query_ref, key_ref, value_ref, g_out_ref, log_ref, out_ref):
    total = query_ref.shape[0]
    length = length_ref[pl.program_id(0)]
    pair = pl.program_id(1)
    block = min(total, 128)
    lanes = pl.ds(pl.multiple_of(pair * 2 * HS, 2 * HS), 2 * HS)

    def with_keys(count):
        keys, values = key_ref[:count, :], value_ref[:count, :]
        query = query_ref[:count, :] * jnp.bfloat16(0.125)
        g_out = g_out_ref[:count, :]
        g_key = jnp.zeros((count, 2 * HS), f32)
        g_value = jnp.zeros((count, 2 * HS), f32)
        g_query = jnp.zeros((2 * HS, count), f32)
        for head in range(2):
            query_head, g_head = only_head(query, head), only_head(g_out, head)
            scores = masked(dot_t(keys, query_head), length)
            probs = jnp.exp(scores - log_ref[head : head + 1, :count])
            g_probs = dot_t(values, g_head)
            delta = jnp.sum(g_probs * probs, 0, keepdims=True)
            g_scores = (probs * (g_probs - delta)).astype(bf16)
            g_value = g_value + dot(probs.astype(bf16), g_head)
            g_key = g_key + dot(g_scores, query_head)
            g_query = g_query + dot(only_head(keys, head).T, g_scores)
        out_ref[0, :count, lanes] = (g_query.T * 0.125).astype(bf16)
        out_ref[1, :count, lanes] = g_key.astype(bf16)
        out_ref[2, :count, lanes] = g_value.astype(bf16)
        if count < total:
            for c in range(3):
                out_ref[c, count:, lanes] = jnp.zeros((total - count, 2 * HS), bf16)

    @pl.when(length == 0)
    def _():
        for c in range(3):
            out_ref[c, :, lanes] = jnp.zeros((total, 2 * HS), bf16)

    for count in range(block, total + 1, block):
        pl.when((length > count - block) & (length <= count))(lambda count=count: with_keys(count))


def attend_back(qkv, g_out, logs, own_len):
    tokens, width = g_out.shape
    seqs = own_len.shape[0]
    length, pairs = tokens // seqs, width // (2 * HS)
    block = (length, 2 * HS)
    return pl.pallas_call(
        attend_back_kernel,
        out_shape=jax.ShapeDtypeStruct((3, tokens, width), bf16),
        grid_spec=pltpu.PrefetchScalarGridSpec(
            num_scalar_prefetch=1,
            grid=(seqs, pairs),
            in_specs=[pl.BlockSpec((None,) + block, lambda s, p, _, c=c: (c, s, p)) for c in range(3)]
            + [
                pl.BlockSpec(block, lambda s, p, _: (s, p)),
                pl.BlockSpec((None, None, 2, length), lambda s, p, _: (s, p, 0, 0)),
            ],
            out_specs=pl.BlockSpec((3, length, width), lambda s, p, _: (0, s, 0)),
        ),
        compiler_params=pltpu.CompilerParams(vmem_limit_bytes=48 * 1024 * 1024),
        cost_estimate=LIGHT,
        name="attend_back",
    )(own_len, qkv, qkv, qkv, g_out, logs)


def dot(a, b):
    return jnp.dot(a, b, preferred_element_type=f32)


def dot_t(a, b):
    return lax.dot_general(a, b, (((1,), (1,)), ((), ())), preferred_element_type=f32)


def t_dot(a, b):
    return lax.dot_general(a, b, (((0,), (0,)), ((), ())), preferred_element_type=f32)


def gelu_both(inner):
    cumulative = 0.5 * (1.0 + lax.erf(inner * 0.7071067811865476))
    density = 0.3989422804014327 * jnp.exp(-0.5 * inner * inner)
    return inner * cumulative, cumulative + inner * density


def row_block(tokens):
    return min(tokens, 256)


def whole(array):
    return pl.BlockSpec(array.shape, lambda *_: (0,) * array.ndim, pipeline_mode=pl.Buffered(1))


def place_rows(vectors, shape):
    place = lax.broadcasted_iota(jnp.int32, shape, 0)
    out = jnp.zeros(shape, f32)
    for k, vector in enumerate(vectors):
        out = jnp.where(place == k, vector, out)
    return out


def norm_back(grad_rows, gain, scaled, inverse):
    weighted = grad_rows * gain
    return inverse * (
        weighted
        - jnp.mean(weighted, -1, keepdims=True)
        - scaled * jnp.mean(weighted * scaled, -1, keepdims=True)
    )


def first_norm(rows, projs, x, vectors):
    tokens, features = x.shape
    width = rows[0].shape[1]
    block = row_block(tokens)
    vectors = [vector.reshape(1, features) for vector in vectors]

    def kernel(att_a, att_b, proj_a, proj_b, x_ref, bias_ref, gain_ref, shift_ref, resid_ref, low_ref):
        branch = dot(att_a[...], proj_a[...]) + dot(att_b[...], proj_b[...])
        resid = x_ref[...].astype(f32) + branch + bias_ref[...].astype(f32)
        resid_ref[...] = resid
        low_ref[...] = normalize(resid, gain_ref[...].astype(f32), shift_ref[...].astype(f32))[0].astype(bf16)

    def blocks(size):
        return pl.BlockSpec((block, size), lambda k: (k, 0))

    return pl.pallas_call(
        kernel,
        out_shape=(jax.ShapeDtypeStruct((tokens, features), f32), jax.ShapeDtypeStruct((tokens, features), bf16)),
        grid_spec=pl.GridSpec(
            grid=(tokens // block,),
            in_specs=[blocks(width)] * 2 + [whole(proj) for proj in projs] + [blocks(features)]
            + [whole(vector) for vector in vectors],
            out_specs=[blocks(features)] * 2,
        ),
        compiler_params=pltpu.CompilerParams(vmem_limit_bytes=32 * 1024 * 1024),
        cost_estimate=LIGHT,
        name="first_norm",
    )(*rows, *projs, x, *vectors)


def hidden_half(low, up, up_bias, branch=None):
    tokens, features = low.shape
    hidden = up.shape[1]
    block = row_block(tokens)
    cut = min(hidden, 512)

    def kernel(low_ref, up_ref, bias_ref, *refs):
        act_ref, slope_ref = refs[4:6] if branch else refs
        low = low_ref[...]
        for at in range(0, hidden, cut):
            part = slice(at, at + cut)
            act, slope = gelu_both(dot(low, up_ref[:, part]) + bias_ref[:, part].astype(f32))
            act_ref[:, part] = act.astype(bf16)
            slope_ref[:, part] = slope.astype(bf16)
        if branch:
            resid_ref, gain_ref, shift_ref, down_ref = refs[:4]
            normed = normalize(resid_ref[...], gain_ref[...].astype(f32), shift_ref[...].astype(f32))[0]
            refs[6][...] = normed + dot(act_ref[...], down_ref[...])

    def blocks(size):
        return pl.BlockSpec((block, size), lambda k: (k, 0))

    args = [low, up, up_bias.reshape(1, hidden)]
    in_specs = [blocks(features)] + [whole(array) for array in args[1:]]
    out_shape = [jax.ShapeDtypeStruct((tokens, hidden), bf16)] * 2
    out_specs = [blocks(hidden)] * 2
    if branch:
        resid, gain, shift, down = branch
        more = [gain.reshape(1, features), shift.reshape(1, features), down]
        args += [resid] + more
        in_specs += [blocks(features)] + [whole(array) for array in more]
        out_shape.append(jax.ShapeDtypeStruct((tokens, features), f32))
        out_specs.append(blocks(features))
    return pl.pallas_call(
        kernel,
        out_shape=out_shape,
        grid_spec=pl.GridSpec(grid=(tokens // block,), in_specs=in_specs, out_specs=out_specs),
        compiler_params=pltpu.CompilerParams(vmem_limit_bytes=48 * 1024 * 1024),
        cost_estimate=LIGHT,
        name="hidden_half",
    )(*args)


def second_norm(base, act, down, out_grad, vectors, own_len):
    tokens, features = base.shape
    hidden = act.shape[1]
    block = row_block(tokens)
    length = tokens // own_len.shape[0]
    vectors = [vector.reshape(1, features) for vector in vectors]

    def kernel(length_ref, base_ref, act_ref, down_ref, grad_ref, bias_ref, gain_ref, shift_ref, out_ref, back_ref, low_ref, sums_ref):
        step = pl.program_id(0)
        resid = base_ref[...] + dot(act_ref[...], down_ref[...]) + bias_ref[...].astype(f32)
        gain = gain_ref[...].astype(f32)
        normed, scaled, inverse = normalize(resid, gain, shift_ref[...].astype(f32))
        out_ref[...] = normed.astype(bf16)
        at = step * block + lax.broadcasted_iota(jnp.int32, (block, 1), 0)
        live = (at % length) < length_ref[step * block // length]
        grad = jnp.where(live, grad_ref[...].astype(f32), 0.0)
        back = norm_back(grad, gain, scaled, inverse)
        back_ref[...] = back
        low_ref[...] = back.astype(bf16)
        sums = [jnp.sum(rows, 0, keepdims=True) for rows in (back, grad * scaled, grad)]

        @pl.when(step == 0)
        def _():
            sums_ref[...] = jnp.zeros_like(sums_ref)

        sums_ref[...] += place_rows(sums, sums_ref.shape)

    rows = pl.BlockSpec((block, features), lambda k, _: (k, 0))
    return pl.pallas_call(
        kernel,
        out_shape=(
            jax.ShapeDtypeStruct((tokens, features), bf16),
            jax.ShapeDtypeStruct((tokens, features), f32),
            jax.ShapeDtypeStruct((tokens, features), bf16),
            jax.ShapeDtypeStruct((8, features), f32),
        ),
        grid_spec=pltpu.PrefetchScalarGridSpec(
            num_scalar_prefetch=1,
            grid=(tokens // block,),
            in_specs=[rows, pl.BlockSpec((block, hidden), lambda k, _: (k, 0)), whole(down), rows]
            + [whole(vector) for vector in vectors],
            out_specs=[rows, rows, rows, pl.BlockSpec((8, features), lambda k, _: (0, 0))],
        ),
        compiler_params=pltpu.CompilerParams(vmem_limit_bytes=48 * 1024 * 1024),
        cost_estimate=LIGHT,
        name="second_norm",
    )(own_len, base, act, down, out_grad, *vectors)


def hidden_back(low, slopes, downs, own_len):
    tokens, features = low.shape
    hidden = slopes[0].shape[1]
    block = row_block(tokens)
    length = tokens // own_len.shape[0]
    cut = min(hidden, 768)

    def kernel(length_ref, low_ref, slope_a, slope_b, down_a, down_b, pre_a, pre_b, bias_ref):
        step = pl.program_id(0)

        @pl.when(step == 0)
        def _():
            bias_ref[...] = jnp.zeros_like(bias_ref)

        start = step * block
        live = (start % length) < length_ref[start // length]

        @pl.when(live)
        def _():
            low = low_ref[...]
            for k, (slope, down, pre) in enumerate(((slope_a, down_a, pre_a), (slope_b, down_b, pre_b))):
                for at in range(0, hidden, cut):
                    part = slice(at, at + cut)
                    g_pre = (dot_t(low, down[part, :]) * slope[:, part].astype(f32)).astype(bf16)
                    pre[:, part] = g_pre
                    bias_ref[k : k + 1, part] += jnp.sum(g_pre.astype(f32), 0, keepdims=True)

        @pl.when(jnp.logical_not(live))
        def _():
            for ref in (pre_a, pre_b):
                ref[...] = jnp.zeros_like(ref)

    def rows(size):
        return pl.BlockSpec((block, size), lambda k, _: (k, 0))

    return pl.pallas_call(
        kernel,
        out_shape=(
            jax.ShapeDtypeStruct((tokens, hidden), bf16), jax.ShapeDtypeStruct((tokens, hidden), bf16),
            jax.ShapeDtypeStruct((8, hidden), f32),
        ),
        grid_spec=pltpu.PrefetchScalarGridSpec(
            num_scalar_prefetch=1,
            grid=(tokens // block,),
            in_specs=[rows(features), rows(hidden), rows(hidden)] + [whole(down) for down in downs],
            out_specs=[rows(hidden), rows(hidden), pl.BlockSpec((8, hidden), lambda k, _: (0, 0))],
        ),
        compiler_params=pltpu.CompilerParams(vmem_limit_bytes=48 * 1024 * 1024),
        cost_estimate=LIGHT,
        name="hidden_back",
    )(own_len, low, *slopes, *downs)


def first_norm_back(g_resid, g_pres, resid_one, gain, ups, projs, own_len):
    tokens, features = g_resid.shape
    hidden, width = g_pres[0].shape[1], projs[0].shape[0]
    block = row_block(tokens)
    length = tokens // own_len.shape[0]
    gain = gain.reshape(1, features)

    def kernel(
        length_ref, g_ref, pre_a, pre_b, normed_ref, gain_ref, up_a, up_b, proj_a, proj_b,
        resid_ref, low_ref, att_a, att_b, sums_ref,
    ):
        step = pl.program_id(0)

        @pl.when(step == 0)
        def _():
            sums_ref[...] = jnp.zeros_like(sums_ref)

        start = step * block
        live = (start % length) < length_ref[start // length]

        @pl.when(live)
        def _():
            total = g_ref[...] + dot_t(pre_a[...], up_a[...]) + dot_t(pre_b[...], up_b[...])
            gain = gain_ref[...].astype(f32)
            _, scaled, inverse = normalize(normed_ref[...], gain, 0.0)
            back = norm_back(total, gain, scaled, inverse)
            resid_ref[...] = back
            low = back.astype(bf16)
            low_ref[...] = low
            att_a[...] = dot_t(low, proj_a[...]).astype(bf16)
            att_b[...] = dot_t(low, proj_b[...]).astype(bf16)
            sums = [jnp.sum(rows, 0, keepdims=True) for rows in (back, total * scaled, total)]
            sums_ref[...] += place_rows(sums, sums_ref.shape)

        @pl.when(jnp.logical_not(live))
        def _():
            for ref in (resid_ref, low_ref, att_a, att_b):
                ref[...] = jnp.zeros_like(ref)

    def rows(size):
        return pl.BlockSpec((block, size), lambda k, _: (k, 0))

    def shape(size, dtype):
        return jax.ShapeDtypeStruct((tokens, size), dtype)

    return pl.pallas_call(
        kernel,
        out_shape=(
            shape(features, f32), shape(features, bf16), shape(width, bf16), shape(width, bf16),
            jax.ShapeDtypeStruct((8, features), f32),
        ),
        grid_spec=pltpu.PrefetchScalarGridSpec(
            num_scalar_prefetch=1,
            grid=(tokens // block,),
            in_specs=[rows(features), rows(hidden), rows(hidden), rows(features)]
            + [whole(array) for array in (gain, *ups, *projs)],
            out_specs=[
                rows(features), rows(features), rows(width), rows(width), pl.BlockSpec((8, features), lambda k, _: (0, 0)),
            ],
        ),
        compiler_params=pltpu.CompilerParams(vmem_limit_bytes=48 * 1024 * 1024),
        cost_estimate=LIGHT,
        name="first_norm_back",
    )(own_len, g_resid, *g_pres, resid_one, gain, *ups, *projs)


def token_grads(a, b, core):
    tokens, size = a.shape
    width = b.shape[1]
    half = size // 2
    cut = min(width, 768)

    def kernel(core_ref, a_ref, b_ref, keep_ref, sent_ref):
        def product(out_ref):
            flat = a_ref[...].T
            for at in range(0, width, cut):
                out_ref[:, at : at + cut] = dot(flat, b_ref[:, at : at + cut]).astype(bf16)

        mine = pl.program_id(0) == 1
        pl.when(mine)(lambda: product(keep_ref))
        pl.when(jnp.logical_not(mine))(lambda: product(sent_ref))

    return pl.pallas_call(
        kernel,
        out_shape=(jax.ShapeDtypeStruct((half, width), bf16),) * 2,
        grid_spec=pltpu.PrefetchScalarGridSpec(
            num_scalar_prefetch=1,
            grid=(2,),
            in_specs=[pl.BlockSpec((tokens, half), lambda h, core: (0, 1 - (h ^ core[0]))), whole(b)],
            out_specs=[pl.BlockSpec((half, width), lambda h, _: (0, 0))] * 2,
        ),
        compiler_params=pltpu.CompilerParams(vmem_limit_bytes=48 * 1024 * 1024),
        cost_estimate=LIGHT,
        name="token_grads",
    )(core[None], a, b)


def plane_grads(flat, g, att, g_attn, core):
    features, tokens = flat.shape
    planes, _, width = g.shape
    half = features // 2
    rows = att.shape[1] // 2
    beside = features // width

    def kernel(core_ref, flat_ref, g_ref, att_ref, g_attn_ref, keep_ref, sent_ref, last_ref):
        step, plane = pl.program_id(0), pl.program_id(1)
        mine = step == 1

        @pl.when((step == 0) & (plane == 0))
        def _():
            last_ref[...] = t_dot(att_ref[...], g_attn_ref[...]).astype(bf16)

        def product(out_ref):
            at = pl.multiple_of(plane * half, half)
            out_ref[pl.ds(at, half), :] = dot(flat_ref[...], g_ref[...]).astype(bf16)

            @pl.when(plane == 0)
            def _():
                which = 1 - (step ^ core_ref[0])
                for h in range(2):

                    @pl.when(which == h)
                    def _():
                        for k in range(beside):
                            at = planes * half + k * rows
                            out_ref[at : at + rows, :] = last_ref[h * rows : (h + 1) * rows, k * width : (k + 1) * width]

        pl.when(mine)(lambda: product(keep_ref))
        pl.when(jnp.logical_not(mine))(lambda: product(sent_ref))

    size = planes * half + beside * rows
    return pl.pallas_call(
        kernel,
        out_shape=(jax.ShapeDtypeStruct((size, width), bf16),) * 2,
        grid_spec=pltpu.PrefetchScalarGridSpec(
            num_scalar_prefetch=1,
            grid=(2, planes),
            in_specs=[
                pl.BlockSpec((half, tokens), lambda h, c, core: (1 - (h ^ core[0]), 0)),
                pl.BlockSpec((None, tokens, width), lambda h, c, core: (c, 0, 0)),
                whole(att),
                whole(g_attn),
            ],
            out_specs=[pl.BlockSpec((size, width), lambda h, c, core: (0, 0))] * 2,
            scratch_shapes=[pltpu.VMEM((att.shape[1], features), bf16)],
        ),
        compiler_params=pltpu.CompilerParams(vmem_limit_bytes=48 * 1024 * 1024),
        cost_estimate=LIGHT,
        name="plane_grads",
    )(core[None], flat, g, att, g_attn)


def input_grad(g_resid, gs, weights):
    tokens, features = g_resid.shape
    planes, _, width = gs[0].shape
    block = row_block(tokens)

    def kernel(resid_ref, g_a, g_b, weight_a, weight_b, out_ref):
        total = resid_ref[...]
        for g, weight in ((g_a, weight_a), (g_b, weight_b)):
            for c in range(planes):
                total = total + dot_t(g[c], weight[c])
        out_ref[...] = total.astype(bf16)

    rows = pl.BlockSpec((block, features), lambda k: (k, 0))
    plane_rows = pl.BlockSpec((planes, block, width), lambda k: (0, k, 0))
    return pl.pallas_call(
        kernel,
        out_shape=jax.ShapeDtypeStruct((tokens, features), bf16),
        grid_spec=pl.GridSpec(
            grid=(tokens // block,),
            in_specs=[rows, plane_rows, plane_rows] + [whole(weight) for weight in weights],
            out_specs=rows,
        ),
        compiler_params=pltpu.CompilerParams(vmem_limit_bytes=48 * 1024 * 1024),
        cost_estimate=LIGHT,
        name="input_grad",
    )(g_resid, *gs, *weights)


def body(
    hidden_in, seq_lengths, live_seqs, out_grad, query_key_value_matrix, query_bias, value_bias,
    projection_matrix, proj_bias, norm1_gain, norm1_shift, up_matrix, up_bias, down_matrix,
    down_bias, norm2_gain, norm2_shift,
):
    seq_count, length, features = hidden_in.shape
    width = query_key_value_matrix.shape[2]
    heads = width // HS
    tokens = seq_count * length
    side = lax.axis_index("tensor")
    own_len = lax.dynamic_slice_in_dim(seq_lengths, side * seq_count, seq_count)
    owned = lax.dynamic_index_in_dim(live_seqs, side, 0, keepdims=False)
    own_len = jnp.where(lax.iota(jnp.int32, seq_count) < owned, own_len, 0)

    x = hidden_in.reshape(tokens, features)
    core, quarter = lax.axis_index("dp") & 1, lax.axis_index("dp") & 3
    qkv_w = query_key_value_matrix.transpose(1, 0, 2).reshape(3 * features, width)
    qkv_get = Gather(pick(qkv_w, 2, core), False)
    biases = jnp.concatenate([query_bias, value_bias, up_bias])
    biases_o = flip(biases)
    up_get = Gather(pick(up_matrix, 4, quarter), True)

    def project(weight, bias):
        bias = jnp.stack([bias[:width], jnp.zeros((width,), bias.dtype), bias[width : 2 * width]])
        rows = jnp.einsum("tv,cvw->ctw", x, weight.reshape(3, features, width), preferred_element_type=f32)
        return (rows + bias.astype(f32)[:, None, :]).astype(bf16)

    qkv_rows = [project(qkv_w, biases)]
    rows, logs_a = attend(qkv_rows[0], own_len)
    attended = [rows]
    proj_sent, down_sent = pick(projection_matrix, 2, core), pick(down_matrix, 2, core)
    attended[0], proj_sent, down_sent = tie([attended[0], proj_sent, down_sent], qkv_get)
    qkv_get.cores()
    proj_get = Gather(proj_sent, False)
    flat = x.T
    (flat,) = tie([flat], qkv_get)
    qkv_o = qkv_get.finish()
    qkv_rows.append(project(qkv_o, biases_o))
    *qkv_rows, down_sent = tie([*qkv_rows, down_sent], up_get)
    up_get.beside()
    down_get = Gather(down_sent, False)
    rows, logs_b = attend(qkv_rows[1], own_len)
    attended.append(rows)
    attended = tie(attended, proj_get)
    proj_get.cores()
    attended = tie(attended, proj_get, up_get)
    up_get.cores()
    projs = [projection_matrix, proj_get.finish()]
    resid_one, normed_low = first_norm(attended, projs, x, [proj_bias, norm1_gain, norm1_shift])
    ups, downs = [up_matrix], [down_matrix]
    act_a, slope_a, base = hidden_half(
        normed_low, up_matrix, biases[2 * width :], (resid_one, norm1_gain, norm1_shift, down_matrix)
    )
    base, normed_low = tie([base, normed_low], up_get, down_get)
    down_get.cores()
    ups.append(up_get.finish())
    act_b, slope_b = hidden_half(normed_low, ups[1], biases_o[2 * width :])
    downs.append(down_get.finish())
    activated, slopes = [act_a, act_b], [slope_a, slope_b]
    out_hidden, g_resid_two, g_mlp, sums_two = second_norm(
        base, act_b, downs[1], out_grad.reshape(tokens, features), [down_bias, norm2_gain, norm2_shift], own_len
    )
    out_hidden = out_hidden.reshape(hidden_in.shape)

    down_sum, up_sum, qkv_sum = Reduction(), Reduction(), Reduction()
    groups = down_sum.groups
    last = len(groups) - 1

    down_sum.cores(token_grads(act_b, g_mlp, core))
    down_own = token_grads(act_a, g_mlp, core)
    g_mlp, *down_own = tie([g_mlp, *down_own], down_sum)
    down_sum.sides(5)
    down_sum.own_cores(down_own)
    g_pre_a, g_pre_b, bias_sums = hidden_back(g_mlp, slopes, downs, own_len)
    up_other = token_grads(normed_low, g_pre_b, core)
    g_pre_a, *up_other = down_sum.first_side([g_pre_a, *up_other])
    up_sum.cores(up_other)
    up_own = token_grads(normed_low, g_pre_a, core)
    down_sum.meet()
    g_resid_two, *up_own = tie([g_resid_two, *up_own], down_sum, up_sum)
    up_sum.sides(8)
    down_sum.scatter(groups[1])
    up_sum.own_cores(up_own)
    g_resid_one, g_attn, att_a, att_b, sums_one = first_norm_back(
        g_resid_two, [g_pre_a, g_pre_b], resid_one, norm1_gain, ups, projs, own_len
    )
    (att_b,) = tie([att_b], down_sum)
    for group in groups[2:]:
        down_sum.scatter(group)
    g_qkv_o = attend_back(qkv_rows[1], att_b, logs_b, own_len)
    up_sum.meet()
    (g_qkv_o,) = tie([g_qkv_o], up_sum)
    up_sum.scatter(groups[1])
    qkv_sum.cores(tie(plane_grads(flat, g_qkv_o, attended[1], g_attn, core), down_sum))
    (att_a,) = tie([att_a], qkv_sum)
    qkv_sum.sides(4)
    down_sum.gather(last)
    g_qkv_a = attend_back(qkv_rows[0], att_a, logs_a, own_len)
    (g_qkv_a,) = qkv_sum.first_side([g_qkv_a])
    g_qkv = [g_qkv_a, g_qkv_o]
    qkv_own = tie(plane_grads(flat, g_qkv_a, attended[0], g_attn, core), down_sum, up_sum)
    qkv_sum.own_cores(qkv_own)
    for group in groups[2:]:
        up_sum.scatter(group)
    sums = [jnp.sum(g.astype(f32), 1) for g in g_qkv]
    ups_rows = up_bias.shape[0] // features
    vectors = []
    for k in range(2):
        up_rows = [bias_sums[k, r * features : (r + 1) * features] for r in range(ups_rows)]
        shared = [sums_one[r] for r in range(3)] + [sums_two[r] for r in range(3)]
        vectors.append(stack_rows(shared + up_rows + [jnp.concatenate([sums[k][0], sums[k][2]])], features))
    vector_sum = VectorSum(*vectors)
    grad_hidden = input_grad(g_resid_one, g_qkv, [w.reshape(3, features, width) for w in (qkv_w, qkv_o)])

    def step():
        tie([], qkv_sum, up_sum, down_sum, vector_sum)

    qkv_sum.meet()
    (grad_hidden,) = tie([grad_hidden], qkv_sum, up_sum, down_sum, vector_sum)
    qkv_sum.scatter(groups[1])
    up_sum.gather(last)
    vector_sum.hop()
    step()
    for group in groups[2:]:
        qkv_sum.scatter(group)
    for k in range(last - 1, 0, -1):
        down_sum.gather(k)
    vector_sum.hop()
    step()
    qkv_sum.gather(last)
    for k in range(last - 1, 0, -1):
        up_sum.gather(k)
    down_sum.gather(0)
    vector_sum.hop()
    step()
    for k in range(last - 1, 0, -1):
        qkv_sum.gather(k)
    up_sum.gather(0)
    down_grad = down_sum.finish()
    vector_sum.hop()
    step()
    qkv_sum.gather(0)
    up_grad = up_sum.finish()
    vector = vector_sum.finish()
    half, proj_half = features // 2, width // 2
    qkv_grad = qkv_sum.finish(parts=tuple(c * half for c in range(3)), rows=half, planes=3)
    proj_grad = qkv_sum.finish(
        parts=tuple(3 * half + k * proj_half for k in range(features // width)), rows=proj_half, beside=features // width
    )
    grad_hidden = grad_hidden.reshape(hidden_in.shape)
    return (
        out_hidden,
        grad_hidden,
        qkv_grad.reshape(3, features, width).transpose(1, 0, 2),
        vector[6 + ups_rows, :width],
        vector[6 + ups_rows, width:],
        proj_grad,
        vector[0],
        vector[1],
        vector[2],
        up_grad,
        vector[6 : 6 + ups_rows].reshape(-1),
        down_grad,
        vector[3],
        vector[4],
        vector[5],
    )


def solution(mesh):
    rows = P(("dp", "tensor"), None, None)
    placed = (
        rows, P("dp"), P("dp"), rows, P(None, None, "tensor"), P("tensor"), P("tensor"),
        P("tensor", None), P(), P(), P(), P(None, "tensor"), P("tensor"), P("tensor", None),
        P(), P(), P(),
    )
    outs = (
        rows, rows, P(None, None, "tensor"), P("tensor"), P("tensor"), P("tensor", None), P(), P(),
        P(), P(None, "tensor"), P("tensor"), P("tensor", None), P(), P(), P(),
    )
    return jax.shard_map(body, mesh=mesh, in_specs=placed, out_specs=outs, check_vma=False)
```

```python
import jax
import jax.numpy as jnp
from jax import lax
from jax.experimental import pallas as pl
from jax.experimental.pallas import tpu as pltpu
from jax.sharding import PartitionSpec as P

HS = 64
epsilon = 1e-06
f32 = jnp.float32
bf16 = jnp.bfloat16
LIGHT = pl.CostEstimate(flops=1, bytes_accessed=1, transcendentals=0)


def flip(value):
    return lax.ppermute(value, "tensor", [(0, 1), (1, 0)])


def hop(value, mask):
    count = lax.axis_size("dp")
    return lax.ppermute(value, "dp", [(i, i ^ mask) for i in range(count)])


def dp_groups():
    count = lax.axis_size("dp")
    bits = count.bit_length() - 1
    groups, at = [], 0
    for width in [1, 1] + [2] * bits:
        width = min(width, bits - at)
        if width > 0:
            groups.append((at, width))
        at += width
    return groups


def member(group):
    at, width = group
    return (lax.axis_index("dp") >> at) & ((1 << width) - 1)


def pick(rows, pieces, which):
    count, width = rows.shape
    return lax.dynamic_index_in_dim(rows.reshape(pieces, count // pieces, width), which, 0, keepdims=False)


def tie(values, *holders):
    arrays = list(values) + [array for holder in holders for array in holder.came]
    arrays = list(lax.optimization_barrier(tuple(arrays)))
    at = len(values)
    for holder in holders:
        holder.came = arrays[at : at + len(holder.came)]
        at += len(holder.came)
    return arrays[: len(values)]


def by_bit(bit, zero, one):
    return jnp.where(bit == 0, zero, one)


class Gather:
    def __init__(self, sent, spread):
        self.spread = spread
        self.came = [flip(sent)]

    def beside(self):
        row = member((1, 1))
        (mine,) = self.came
        (other,) = self.came = [hop(mine, 2)]
        self.mine = mine

    def cores(self):
        if self.spread:
            row = member((1, 1))
            (other,) = self.came
            self.parts = [by_bit(row, self.mine, other), by_bit(row, other, self.mine)]
        else:
            self.parts = self.came
        self.came = [hop(part, 1) for part in self.parts]

    def finish(self):
        core = member((0, 1))
        rows = []
        for mine, other in zip(self.parts, self.came):
            rows += [by_bit(core, mine, other), by_bit(core, other, mine)]
        return jnp.concatenate(rows, 0)


class Reduction:
    def __init__(self):
        self.groups = dp_groups()

    def cores(self, other):
        self.core = member(self.groups[0])
        self.keep = other[0]
        self.came = [hop(other[1], 1)]

    def sides(self, eighths=6):
        away = (self.keep.astype(f32) + self.came[0].astype(f32)).astype(bf16)
        first = away.shape[0] * eighths // 8
        self.came = [flip(part) for part in (away[:first], away[first:]) if part.shape[0] > 0]

    def first_side(self, values):
        *values, self.came[0] = lax.optimization_barrier((*values, self.came[0]))
        return values

    def own_cores(self, own):
        self.total = own[0]
        self.own_came = hop(own[1], 1)

    def meet(self):
        self.came = [jnp.concatenate(self.came, 0) if len(self.came) > 1 else self.came[0], self.own_came]

    def scatter(self, group):
        at, width = group
        pieces, me = 1 << width, member(group)
        terms = [self.total] + self.came

        def piece(which):
            return sum(pick(term, pieces, which).astype(f32) for term in terms)

        self.came = [hop(piece(me ^ j).astype(bf16), j << at) for j in range(1, pieces)]
        self.total = piece(me)

    def gather(self, k):
        if k == len(self.groups) - 1:
            self.result = sum(term.astype(f32) for term in [self.total] + self.came).astype(bf16)
        else:
            self.result = assemble([self.result] + self.came, member(self.groups[k + 1]), bf16)
        at, width = self.groups[k]
        self.came = [hop(self.result, j << at) for j in range(1, 1 << width)]

    def finish(self, **shape):
        return assemble([self.result] + self.came, self.core, f32, **shape)


def assemble(slots, me, dtype, parts=(0,), rows=None, planes=1, beside=1):
    count = len(slots)
    rows = slots[0].shape[0] if rows is None else rows
    width = slots[0].shape[1]
    each = len(parts) // planes // beside

    def kernel(me_ref, *refs):
        step = pl.program_id(0) ^ me_ref[0]
        for j in range(count):

            @pl.when(step == j)
            def _():
                for p, row in enumerate(parts):
                    at, column = p // beside % each * rows, p % beside * width
                    refs[-1][p // beside // each, 0, at : at + rows, column : column + width] = refs[j][
                        row : row + rows, :
                    ].astype(dtype)

    out = pl.pallas_call(
        kernel,
        out_shape=jax.ShapeDtypeStruct((planes, count, each * rows, beside * width), dtype),
        grid_spec=pltpu.PrefetchScalarGridSpec(
            num_scalar_prefetch=1,
            grid=(count,),
            in_specs=[pl.BlockSpec(slot.shape, lambda k, _: (0, 0)) for slot in slots],
            out_specs=pl.BlockSpec((planes, 1, each * rows, beside * width), lambda k, _: (0, k, 0, 0)),
        ),
        compiler_params=pltpu.CompilerParams(vmem_limit_bytes=48 * 1024 * 1024),
        cost_estimate=LIGHT,
        name="assemble",
    )(me[None].astype(jnp.int32), *slots)
    return out.reshape(planes * count * each * rows, beside * width)


class VectorSum:
    def __init__(self, other):
        self.mask = 1
        self.came = [flip(other)]

    def begin(self, own):
        self.total = own
        self.hop()

    def hop(self):
        if self.mask < lax.axis_size("dp"):
            self.total = self.total + self.came[0]
            self.came = [hop(self.total, self.mask)]
            self.mask *= 2

    def finish(self):
        while self.mask < lax.axis_size("dp"):
            self.hop()
        return self.total + self.came[0]


def stack_rows(parts):
    count = -(-sum(part.shape[0] for part in parts) // 8) * 8
    out, at = 0.0, 0
    for part in parts:
        out = out + jnp.pad(part, ((at, count - at - part.shape[0]), (0, 0)))
        at += part.shape[0]
    return out


def normalize(resid, gain, shift):
    average = jnp.mean(resid, -1, keepdims=True)
    centred = resid - average
    inverse = lax.rsqrt(jnp.mean(centred * centred, -1, keepdims=True) + epsilon)
    scaled = centred * inverse
    return (scaled * gain + shift, scaled, inverse)


def head_lanes(shape, head):
    return (lax.broadcasted_iota(jnp.int32, shape, 1) >= HS) == (head == 1)


def only_head(rows, head):
    return jnp.where(head_lanes(rows.shape, head), rows, jnp.zeros_like(rows))


def masked(scores, length):
    cut = max(scores.shape[0] - 128, 0)
    place = cut + lax.broadcasted_iota(jnp.int32, (scores.shape[0] - cut, 1), 0)
    last = jnp.where(place < length, scores[cut:], -1000000000.0)
    return jnp.concatenate([scores[:cut], last], 0) if cut else last


def attend_kernel(length_ref, query_ref, key_ref, value_ref, out_ref, log_ref):
    total = query_ref.shape[0]
    length = length_ref[pl.program_id(0)]
    block = min(total, 128)

    def with_keys(count):
        keys, values = key_ref[:count, :], value_ref[:count, :]
        query = query_ref[...] * jnp.bfloat16(0.125)
        out = jnp.zeros((2 * HS, total), f32)
        for head in range(2):
            scores = masked(dot_t(keys, only_head(query, head)), length)
            highest = jnp.max(scores, 0, keepdims=True)
            shifted = jnp.exp(scores - highest)
            sums = jnp.sum(shifted, 0, keepdims=True)
            log_ref[head : head + 1, :] = highest + jnp.log(sums)
            out = out + dot(only_head(values, head).T, shifted.astype(bf16)) * (1.0 / sums)
        out_ref[...] = out.T.astype(bf16)

    @pl.when(length == 0)
    def _():
        average = jnp.sum(value_ref[...].astype(f32), 0, keepdims=True) * (1.0 / total)
        out_ref[...] = jnp.broadcast_to(average, out_ref.shape).astype(bf16)
        log_ref[...] = jnp.zeros_like(log_ref)

    for count in range(block, total + 1, block):
        pl.when((length > count - block) & (length <= count))(lambda count=count: with_keys(count))


def attend(qkv, own_len):
    _, tokens, width = qkv.shape
    seqs = own_len.shape[0]
    length, pairs = tokens // seqs, width // (2 * HS)
    block = (length, 2 * HS)
    return pl.pallas_call(
        attend_kernel,
        out_shape=(
            jax.ShapeDtypeStruct((tokens, width), bf16), jax.ShapeDtypeStruct((seqs, pairs, 2, length), f32)
        ),
        grid_spec=pltpu.PrefetchScalarGridSpec(
            num_scalar_prefetch=1,
            grid=(seqs, pairs),
            in_specs=[pl.BlockSpec((None,) + block, lambda s, p, _, c=c: (c, s, p)) for c in range(3)],
            out_specs=[
                pl.BlockSpec(block, lambda s, p, _: (s, p)),
                pl.BlockSpec((None, None, 2, length), lambda s, p, _: (s, p, 0, 0)),
            ],
        ),
        compiler_params=pltpu.CompilerParams(vmem_limit_bytes=48 * 1024 * 1024),
        cost_estimate=LIGHT,
        name="attend",
    )(own_len, qkv, qkv, qkv)


def attend_back_kernel(length_ref, query_ref, key_ref, value_ref, g_out_ref, log_ref, out_ref):
    total = query_ref.shape[0]
    length = length_ref[pl.program_id(0)]
    pair = pl.program_id(1)
    block = min(total, 128)
    lanes = pl.ds(pl.multiple_of(pair * 2 * HS, 2 * HS), 2 * HS)

    def with_keys(count):
        keys, values = key_ref[:count, :], value_ref[:count, :]
        query = query_ref[:count, :] * jnp.bfloat16(0.125)
        g_out = g_out_ref[:count, :]
        g_key = jnp.zeros((count, 2 * HS), f32)
        g_value = jnp.zeros((count, 2 * HS), f32)
        g_query = jnp.zeros((2 * HS, count), f32)
        for head in range(2):
            query_head, g_head = only_head(query, head), only_head(g_out, head)
            scores = masked(dot_t(keys, query_head), length)
            probs = jnp.exp(scores - log_ref[head : head + 1, :count])
            g_probs = dot_t(values, g_head)
            delta = jnp.sum(g_probs * probs, 0, keepdims=True)
            g_scores = (probs * (g_probs - delta)).astype(bf16)
            g_value = g_value + dot(probs.astype(bf16), g_head)
            g_key = g_key + dot(g_scores, query_head)
            g_query = g_query + dot(only_head(keys, head).T, g_scores)
        out_ref[0, :count, lanes] = (g_query.T * 0.125).astype(bf16)
        out_ref[1, :count, lanes] = g_key.astype(bf16)
        out_ref[2, :count, lanes] = g_value.astype(bf16)
        if count < total:
            for c in range(3):
                out_ref[c, count:, lanes] = jnp.zeros((total - count, 2 * HS), bf16)

    @pl.when(length == 0)
    def _():
        for c in range(3):
            out_ref[c, :, lanes] = jnp.zeros((total, 2 * HS), bf16)

    for count in range(block, total + 1, block):
        pl.when((length > count - block) & (length <= count))(lambda count=count: with_keys(count))


def attend_back(qkv, g_out, logs, own_len):
    tokens, width = g_out.shape
    seqs = own_len.shape[0]
    length, pairs = tokens // seqs, width // (2 * HS)
    block = (length, 2 * HS)
    return pl.pallas_call(
        attend_back_kernel,
        out_shape=jax.ShapeDtypeStruct((3, tokens, width), bf16),
        grid_spec=pltpu.PrefetchScalarGridSpec(
            num_scalar_prefetch=1,
            grid=(seqs, pairs),
            in_specs=[pl.BlockSpec((None,) + block, lambda s, p, _, c=c: (c, s, p)) for c in range(3)]
            + [
                pl.BlockSpec(block, lambda s, p, _: (s, p)),
                pl.BlockSpec((None, None, 2, length), lambda s, p, _: (s, p, 0, 0)),
            ],
            out_specs=pl.BlockSpec((3, length, width), lambda s, p, _: (0, s, 0)),
        ),
        compiler_params=pltpu.CompilerParams(vmem_limit_bytes=48 * 1024 * 1024),
        cost_estimate=LIGHT,
        name="attend_back",
    )(own_len, qkv, qkv, qkv, g_out, logs)


def dot(a, b):
    return jnp.dot(a, b, preferred_element_type=f32)


def dot_t(a, b):
    return lax.dot_general(a, b, (((1,), (1,)), ((), ())), preferred_element_type=f32)


def t_dot(a, b):
    return lax.dot_general(a, b, (((0,), (0,)), ((), ())), preferred_element_type=f32)


def gelu_both(inner):
    cumulative = 0.5 * (1.0 + lax.erf(inner * 0.7071067811865476))
    density = 0.3989422804014327 * jnp.exp(-0.5 * inner * inner)
    return inner * cumulative, cumulative + inner * density


def row_block(tokens):
    return min(tokens, 256)


def whole(array):
    return pl.BlockSpec(array.shape, lambda *_: (0,) * array.ndim, pipeline_mode=pl.Buffered(1))


def place_rows(vectors, shape):
    place = lax.broadcasted_iota(jnp.int32, shape, 0)
    out = jnp.zeros(shape, f32)
    for k, vector in enumerate(vectors):
        out = jnp.where(place == k, vector, out)
    return out


def norm_back(grad_rows, gain, scaled, inverse):
    weighted = grad_rows * gain
    return inverse * (
        weighted
        - jnp.mean(weighted, -1, keepdims=True)
        - scaled * jnp.mean(weighted * scaled, -1, keepdims=True)
    )


def first_norm(rows, projs, x, vectors):
    tokens, features = x.shape
    width = rows[0].shape[1]
    block = row_block(tokens)
    vectors = [vector.reshape(1, features) for vector in vectors]

    def kernel(att_a, att_b, proj_a, proj_b, x_ref, bias_ref, gain_ref, shift_ref, resid_ref, low_ref):
        branch = dot(att_a[...], proj_a[...]) + dot(att_b[...], proj_b[...])
        resid = x_ref[...].astype(f32) + branch + bias_ref[...].astype(f32)
        resid_ref[...] = resid
        low_ref[...] = normalize(resid, gain_ref[...].astype(f32), shift_ref[...].astype(f32))[0].astype(bf16)

    def blocks(size):
        return pl.BlockSpec((block, size), lambda k: (k, 0))

    return pl.pallas_call(
        kernel,
        out_shape=(jax.ShapeDtypeStruct((tokens, features), f32), jax.ShapeDtypeStruct((tokens, features), bf16)),
        grid_spec=pl.GridSpec(
            grid=(tokens // block,),
            in_specs=[blocks(width)] * 2 + [whole(proj) for proj in projs] + [blocks(features)]
            + [whole(vector) for vector in vectors],
            out_specs=[blocks(features)] * 2,
        ),
        compiler_params=pltpu.CompilerParams(vmem_limit_bytes=32 * 1024 * 1024),
        cost_estimate=LIGHT,
        name="first_norm",
    )(*rows, *projs, x, *vectors)


def hidden_half(low, up, up_bias, branch=None):
    tokens, features = low.shape
    hidden = up.shape[1]
    block = row_block(tokens)
    cut = min(hidden, 512)

    def kernel(low_ref, up_ref, bias_ref, *refs):
        act_ref, slope_ref = refs[4:6] if branch else refs
        low = low_ref[...]
        for at in range(0, hidden, cut):
            part = slice(at, at + cut)
            act, slope = gelu_both(dot(low, up_ref[:, part]) + bias_ref[:, part].astype(f32))
            act_ref[:, part] = act.astype(bf16)
            slope_ref[:, part] = slope.astype(bf16)
        if branch:
            resid_ref, gain_ref, shift_ref, down_ref = refs[:4]
            normed = normalize(resid_ref[...], gain_ref[...].astype(f32), shift_ref[...].astype(f32))[0]
            refs[6][...] = normed + dot(act_ref[...], down_ref[...])

    def blocks(size):
        return pl.BlockSpec((block, size), lambda k: (k, 0))

    args = [low, up, up_bias.reshape(1, hidden)]
    in_specs = [blocks(features)] + [whole(array) for array in args[1:]]
    out_shape = [jax.ShapeDtypeStruct((tokens, hidden), bf16)] * 2
    out_specs = [blocks(hidden)] * 2
    if branch:
        resid, gain, shift, down = branch
        more = [gain.reshape(1, features), shift.reshape(1, features), down]
        args += [resid] + more
        in_specs += [blocks(features)] + [whole(array) for array in more]
        out_shape.append(jax.ShapeDtypeStruct((tokens, features), f32))
        out_specs.append(blocks(features))
    return pl.pallas_call(
        kernel,
        out_shape=out_shape,
        grid_spec=pl.GridSpec(grid=(tokens // block,), in_specs=in_specs, out_specs=out_specs),
        compiler_params=pltpu.CompilerParams(vmem_limit_bytes=48 * 1024 * 1024),
        cost_estimate=LIGHT,
        name="hidden_half",
    )(*args)


def second_norm(base, act, down, out_grad, vectors, own_len):
    tokens, features = base.shape
    hidden = act.shape[1]
    block = row_block(tokens)
    length = tokens // own_len.shape[0]
    vectors = [vector.reshape(1, features) for vector in vectors]

    def kernel(length_ref, base_ref, act_ref, down_ref, grad_ref, bias_ref, gain_ref, shift_ref, out_ref, back_ref, low_ref, sums_ref):
        step = pl.program_id(0)
        resid = base_ref[...] + dot(act_ref[...], down_ref[...]) + bias_ref[...].astype(f32)
        gain = gain_ref[...].astype(f32)
        normed, scaled, inverse = normalize(resid, gain, shift_ref[...].astype(f32))
        out_ref[...] = normed.astype(bf16)
        at = step * block + lax.broadcasted_iota(jnp.int32, (block, 1), 0)
        live = (at % length) < length_ref[step * block // length]
        grad = jnp.where(live, grad_ref[...].astype(f32), 0.0)
        back = norm_back(grad, gain, scaled, inverse)
        back_ref[...] = back
        low_ref[...] = back.astype(bf16)
        sums = [jnp.sum(rows, 0, keepdims=True) for rows in (back, grad * scaled, grad)]

        @pl.when(step == 0)
        def _():
            sums_ref[...] = jnp.zeros_like(sums_ref)

        sums_ref[...] += place_rows(sums, sums_ref.shape)

    rows = pl.BlockSpec((block, features), lambda k, _: (k, 0))
    return pl.pallas_call(
        kernel,
        out_shape=(
            jax.ShapeDtypeStruct((tokens, features), bf16),
            jax.ShapeDtypeStruct((tokens, features), f32),
            jax.ShapeDtypeStruct((tokens, features), bf16),
            jax.ShapeDtypeStruct((8, features), f32),
        ),
        grid_spec=pltpu.PrefetchScalarGridSpec(
            num_scalar_prefetch=1,
            grid=(tokens // block,),
            in_specs=[rows, pl.BlockSpec((block, hidden), lambda k, _: (k, 0)), whole(down), rows]
            + [whole(vector) for vector in vectors],
            out_specs=[rows, rows, rows, pl.BlockSpec((8, features), lambda k, _: (0, 0))],
        ),
        compiler_params=pltpu.CompilerParams(vmem_limit_bytes=48 * 1024 * 1024),
        cost_estimate=LIGHT,
        name="second_norm",
    )(own_len, base, act, down, out_grad, *vectors)


def hidden_back(low, slopes, downs, own_len):
    tokens, features = low.shape
    hidden = slopes[0].shape[1]
    block = row_block(tokens)
    length = tokens // own_len.shape[0]
    cut = min(hidden, 768)

    def kernel(length_ref, low_ref, slope_a, slope_b, down_a, down_b, pre_a, pre_b, bias_ref):
        step = pl.program_id(0)

        @pl.when(step == 0)
        def _():
            bias_ref[...] = jnp.zeros_like(bias_ref)

        start = step * block
        live = (start % length) < length_ref[start // length]

        @pl.when(live)
        def _():
            low = low_ref[...]
            for k, (slope, down, pre) in enumerate(((slope_a, down_a, pre_a), (slope_b, down_b, pre_b))):
                for at in range(0, hidden, cut):
                    part = slice(at, at + cut)
                    g_pre = (dot_t(low, down[part, :]) * slope[:, part].astype(f32)).astype(bf16)
                    pre[:, part] = g_pre
                    bias_ref[k : k + 1, part] += jnp.sum(g_pre.astype(f32), 0, keepdims=True)

        @pl.when(jnp.logical_not(live))
        def _():
            for ref in (pre_a, pre_b):
                ref[...] = jnp.zeros_like(ref)

    def rows(size):
        return pl.BlockSpec((block, size), lambda k, _: (k, 0))

    return pl.pallas_call(
        kernel,
        out_shape=(
            jax.ShapeDtypeStruct((tokens, hidden), bf16), jax.ShapeDtypeStruct((tokens, hidden), bf16),
            jax.ShapeDtypeStruct((8, hidden), f32),
        ),
        grid_spec=pltpu.PrefetchScalarGridSpec(
            num_scalar_prefetch=1,
            grid=(tokens // block,),
            in_specs=[rows(features), rows(hidden), rows(hidden)] + [whole(down) for down in downs],
            out_specs=[rows(hidden), rows(hidden), pl.BlockSpec((8, hidden), lambda k, _: (0, 0))],
        ),
        compiler_params=pltpu.CompilerParams(vmem_limit_bytes=48 * 1024 * 1024),
        cost_estimate=LIGHT,
        name="hidden_back",
    )(own_len, low, *slopes, *downs)


def first_norm_back(g_resid, g_pres, resid_one, gain, ups, projs, own_len):
    tokens, features = g_resid.shape
    hidden, width = g_pres[0].shape[1], projs[0].shape[0]
    block = row_block(tokens)
    length = tokens // own_len.shape[0]
    gain = gain.reshape(1, features)

    def kernel(
        length_ref, g_ref, pre_a, pre_b, normed_ref, gain_ref, up_a, up_b, proj_a, proj_b,
        resid_ref, low_ref, att_a, att_b, sums_ref,
    ):
        step = pl.program_id(0)

        @pl.when(step == 0)
        def _():
            sums_ref[...] = jnp.zeros_like(sums_ref)

        start = step * block
        live = (start % length) < length_ref[start // length]

        @pl.when(live)
        def _():
            total = g_ref[...] + dot_t(pre_a[...], up_a[...]) + dot_t(pre_b[...], up_b[...])
            gain = gain_ref[...].astype(f32)
            _, scaled, inverse = normalize(normed_ref[...], gain, 0.0)
            back = norm_back(total, gain, scaled, inverse)
            resid_ref[...] = back
            low = back.astype(bf16)
            low_ref[...] = low
            att_a[...] = dot_t(low, proj_a[...]).astype(bf16)
            att_b[...] = dot_t(low, proj_b[...]).astype(bf16)
            sums = [jnp.sum(rows, 0, keepdims=True) for rows in (back, total * scaled, total)]
            sums_ref[...] += place_rows(sums, sums_ref.shape)

        @pl.when(jnp.logical_not(live))
        def _():
            for ref in (resid_ref, low_ref, att_a, att_b):
                ref[...] = jnp.zeros_like(ref)

    def rows(size):
        return pl.BlockSpec((block, size), lambda k, _: (k, 0))

    def shape(size, dtype):
        return jax.ShapeDtypeStruct((tokens, size), dtype)

    return pl.pallas_call(
        kernel,
        out_shape=(
            shape(features, f32), shape(features, bf16), shape(width, bf16), shape(width, bf16),
            jax.ShapeDtypeStruct((8, features), f32),
        ),
        grid_spec=pltpu.PrefetchScalarGridSpec(
            num_scalar_prefetch=1,
            grid=(tokens // block,),
            in_specs=[rows(features), rows(hidden), rows(hidden), rows(features)]
            + [whole(array) for array in (gain, *ups, *projs)],
            out_specs=[
                rows(features), rows(features), rows(width), rows(width), pl.BlockSpec((8, features), lambda k, _: (0, 0)),
            ],
        ),
        compiler_params=pltpu.CompilerParams(vmem_limit_bytes=48 * 1024 * 1024),
        cost_estimate=LIGHT,
        name="first_norm_back",
    )(own_len, g_resid, *g_pres, resid_one, gain, *ups, *projs)


def token_grads(a, b, core):
    tokens, size = a.shape
    width = b.shape[1]
    half = size // 2
    cut = min(width, 768)

    def kernel(core_ref, a_ref, b_ref, keep_ref, sent_ref):
        def product(out_ref):
            flat = a_ref[...].T
            for at in range(0, width, cut):
                out_ref[:, at : at + cut] = dot(flat, b_ref[:, at : at + cut]).astype(bf16)

        mine = pl.program_id(0) == 1
        pl.when(mine)(lambda: product(keep_ref))
        pl.when(jnp.logical_not(mine))(lambda: product(sent_ref))

    return pl.pallas_call(
        kernel,
        out_shape=(jax.ShapeDtypeStruct((half, width), bf16),) * 2,
        grid_spec=pltpu.PrefetchScalarGridSpec(
            num_scalar_prefetch=1,
            grid=(2,),
            in_specs=[pl.BlockSpec((tokens, half), lambda h, core: (0, 1 - (h ^ core[0]))), whole(b)],
            out_specs=[pl.BlockSpec((half, width), lambda h, _: (0, 0))] * 2,
        ),
        compiler_params=pltpu.CompilerParams(vmem_limit_bytes=48 * 1024 * 1024),
        cost_estimate=LIGHT,
        name="token_grads",
    )(core[None], a, b)


def plane_grads(flat, g, att, g_attn, core):
    features, tokens = flat.shape
    planes, _, width = g.shape
    half = features // 2
    rows = att.shape[1] // 2
    beside = features // width

    def kernel(core_ref, flat_ref, g_ref, att_ref, g_attn_ref, keep_ref, sent_ref, last_ref):
        step, plane = pl.program_id(0), pl.program_id(1)
        mine = step == 1

        @pl.when((step == 0) & (plane == 0))
        def _():
            last_ref[...] = t_dot(att_ref[...], g_attn_ref[...]).astype(bf16)

        def product(out_ref):
            at = pl.multiple_of(plane * half, half)
            out_ref[pl.ds(at, half), :] = dot(flat_ref[...], g_ref[...]).astype(bf16)

            @pl.when(plane == 0)
            def _():
                which = 1 - (step ^ core_ref[0])
                for h in range(2):

                    @pl.when(which == h)
                    def _():
                        for k in range(beside):
                            at = planes * half + k * rows
                            out_ref[at : at + rows, :] = last_ref[h * rows : (h + 1) * rows, k * width : (k + 1) * width]

        pl.when(mine)(lambda: product(keep_ref))
        pl.when(jnp.logical_not(mine))(lambda: product(sent_ref))

    size = planes * half + beside * rows
    return pl.pallas_call(
        kernel,
        out_shape=(jax.ShapeDtypeStruct((size, width), bf16),) * 2,
        grid_spec=pltpu.PrefetchScalarGridSpec(
            num_scalar_prefetch=1,
            grid=(2, planes),
            in_specs=[
                pl.BlockSpec((half, tokens), lambda h, c, core: (1 - (h ^ core[0]), 0)),
                pl.BlockSpec((None, tokens, width), lambda h, c, core: (c, 0, 0)),
                whole(att),
                whole(g_attn),
            ],
            out_specs=[pl.BlockSpec((size, width), lambda h, c, core: (0, 0))] * 2,
            scratch_shapes=[pltpu.VMEM((att.shape[1], features), bf16)],
        ),
        compiler_params=pltpu.CompilerParams(vmem_limit_bytes=48 * 1024 * 1024),
        cost_estimate=LIGHT,
        name="plane_grads",
    )(core[None], flat, g, att, g_attn)


def input_grad(g_resid, gs, weights):
    tokens, features = g_resid.shape
    planes, _, width = gs[0].shape
    block = row_block(tokens)

    def kernel(resid_ref, g_a, g_b, weight_a, weight_b, out_ref):
        total = resid_ref[...]
        for g, weight in ((g_a, weight_a), (g_b, weight_b)):
            for c in range(planes):
                total = total + dot_t(g[c], weight[c])
        out_ref[...] = total.astype(bf16)

    rows = pl.BlockSpec((block, features), lambda k: (k, 0))
    plane_rows = pl.BlockSpec((planes, block, width), lambda k: (0, k, 0))
    return pl.pallas_call(
        kernel,
        out_shape=jax.ShapeDtypeStruct((tokens, features), bf16),
        grid_spec=pl.GridSpec(
            grid=(tokens // block,),
            in_specs=[rows, plane_rows, plane_rows] + [whole(weight) for weight in weights],
            out_specs=rows,
        ),
        compiler_params=pltpu.CompilerParams(vmem_limit_bytes=48 * 1024 * 1024),
        cost_estimate=LIGHT,
        name="input_grad",
    )(g_resid, *gs, *weights)


def body(
    hidden_in, seq_lengths, live_seqs, out_grad, query_key_value_matrix, query_bias, value_bias,
    projection_matrix, proj_bias, norm1_gain, norm1_shift, up_matrix, up_bias, down_matrix,
    down_bias, norm2_gain, norm2_shift,
):
    seq_count, length, features = hidden_in.shape
    width = query_key_value_matrix.shape[2]
    heads = width // HS
    tokens = seq_count * length
    side = lax.axis_index("tensor")
    own_len = lax.dynamic_slice_in_dim(seq_lengths, side * seq_count, seq_count)
    owned = lax.dynamic_index_in_dim(live_seqs, side, 0, keepdims=False)
    own_len = jnp.where(lax.iota(jnp.int32, seq_count) < owned, own_len, 0)

    x = hidden_in.reshape(tokens, features)
    core, quarter = lax.axis_index("dp") & 1, lax.axis_index("dp") & 3
    qkv_w = query_key_value_matrix.transpose(1, 0, 2).reshape(3 * features, width)
    qkv_get = Gather(pick(qkv_w, 2, core), False)
    biases = jnp.concatenate([query_bias, value_bias, up_bias])
    biases_o = flip(biases)
    up_get = Gather(pick(up_matrix, 4, quarter), True)

    def project(weight, bias):
        bias = jnp.stack([bias[:width], jnp.zeros((width,), bias.dtype), bias[width : 2 * width]])
        rows = jnp.einsum("tv,cvw->ctw", x, weight.reshape(3, features, width), preferred_element_type=f32)
        return (rows + bias.astype(f32)[:, None, :]).astype(bf16)

    qkv_rows = [project(qkv_w, biases)]
    rows, logs_a = attend(qkv_rows[0], own_len)
    attended = [rows]
    proj_sent, down_sent = pick(projection_matrix, 2, core), pick(down_matrix, 2, core)
    attended[0], proj_sent, down_sent = tie([attended[0], proj_sent, down_sent], qkv_get)
    qkv_get.cores()
    proj_get = Gather(proj_sent, False)
    flat = x.T
    (flat,) = tie([flat], qkv_get)
    qkv_o = qkv_get.finish()
    qkv_rows.append(project(qkv_o, biases_o))
    *qkv_rows, down_sent = tie([*qkv_rows, down_sent], up_get)
    up_get.beside()
    down_get = Gather(down_sent, False)
    rows, logs_b = attend(qkv_rows[1], own_len)
    attended.append(rows)
    attended = tie(attended, proj_get)
    proj_get.cores()
    attended = tie(attended, proj_get, up_get)
    up_get.cores()
    projs = [projection_matrix, proj_get.finish()]
    resid_one, normed_low = first_norm(attended, projs, x, [proj_bias, norm1_gain, norm1_shift])
    ups, downs = [up_matrix], [down_matrix]
    act_a, slope_a, base = hidden_half(
        normed_low, up_matrix, biases[2 * width :], (resid_one, norm1_gain, norm1_shift, down_matrix)
    )
    base, normed_low = tie([base, normed_low], up_get, down_get)
    down_get.cores()
    ups.append(up_get.finish())
    act_b, slope_b = hidden_half(normed_low, ups[1], biases_o[2 * width :])
    downs.append(down_get.finish())
    activated, slopes = [act_a, act_b], [slope_a, slope_b]
    out_hidden, g_resid_two, g_mlp, sums_two = second_norm(
        base, act_b, downs[1], out_grad.reshape(tokens, features), [down_bias, norm2_gain, norm2_shift], own_len
    )
    out_hidden = out_hidden.reshape(hidden_in.shape)

    down_sum, up_sum, qkv_sum = Reduction(), Reduction(), Reduction()
    groups = down_sum.groups
    last = len(groups) - 1

    down_sum.cores(token_grads(act_b, g_mlp, core))
    down_own = token_grads(act_a, g_mlp, core)
    g_mlp, *down_own = tie([g_mlp, *down_own], down_sum)
    down_sum.sides(5)
    down_sum.own_cores(down_own)
    g_pre_a, g_pre_b, bias_sums = hidden_back(g_mlp, slopes, downs, own_len)
    up_other = token_grads(normed_low, g_pre_b, core)
    g_pre_a, *up_other = down_sum.first_side([g_pre_a, *up_other])
    up_sum.cores(up_other)
    up_own = token_grads(normed_low, g_pre_a, core)
    down_sum.meet()
    g_resid_two, *up_own = tie([g_resid_two, *up_own], down_sum, up_sum)
    up_sum.sides(8)
    down_sum.scatter(groups[1])
    up_sum.own_cores(up_own)
    g_resid_one, g_attn, att_a, att_b, sums_one = first_norm_back(
        g_resid_two, [g_pre_a, g_pre_b], resid_one, norm1_gain, ups, projs, own_len
    )
    (att_b,) = tie([att_b], down_sum)
    for group in groups[2:]:
        down_sum.scatter(group)
    g_qkv_o = attend_back(qkv_rows[1], att_b, logs_b, own_len)
    up_sum.meet()
    (g_qkv_o,) = tie([g_qkv_o], up_sum)
    up_sum.scatter(groups[1])
    ups_rows = up_bias.shape[0] // features

    def vector_of(side, g):
        sums = jnp.sum(g.astype(f32), 1)
        ends = jnp.concatenate([sums[0], sums[2]]).reshape(1, features)
        return stack_rows([sums_one[:3], sums_two[:3], bias_sums[side].reshape(ups_rows, features), ends])

    qkv_sum.cores(tie(plane_grads(flat, g_qkv_o, attended[1], g_attn, core), down_sum))
    down_sum.gather(last)
    (att_a,) = tie([att_a], qkv_sum)
    qkv_sum.sides(4)
    g_qkv_a = attend_back(qkv_rows[0], att_a, logs_a, own_len)
    (g_qkv_a,) = qkv_sum.first_side([g_qkv_a])
    g_qkv = [g_qkv_a, g_qkv_o]
    qkv_own = tie(plane_grads(flat, g_qkv_a, attended[0], g_attn, core), down_sum, up_sum)
    qkv_sum.own_cores(qkv_own)
    for group in groups[2:]:
        up_sum.scatter(group)
    vector_sum = VectorSum(vector_of(1, g_qkv_o))

    def step():
        tie([], qkv_sum, up_sum, down_sum, vector_sum)

    qkv_sum.meet()
    (g_resid_one,) = tie([g_resid_one], qkv_sum, up_sum, down_sum, vector_sum)
    grad_hidden = input_grad(g_resid_one, g_qkv, [w.reshape(3, features, width) for w in (qkv_w, qkv_o)])
    qkv_sum.scatter(groups[1])
    up_sum.gather(last)
    vector_sum.begin(vector_of(0, g_qkv_a))
    step()
    for group in groups[2:]:
        qkv_sum.scatter(group)
    for k in range(last - 1, 0, -1):
        down_sum.gather(k)
    vector_sum.hop()
    (grad_hidden,) = tie([grad_hidden], qkv_sum, up_sum, down_sum, vector_sum)
    qkv_sum.gather(last)
    for k in range(last - 1, 0, -1):
        up_sum.gather(k)
    down_sum.gather(0)
    vector_sum.hop()
    step()
    for k in range(last - 1, 0, -1):
        qkv_sum.gather(k)
    up_sum.gather(0)
    down_grad = down_sum.finish()
    vector_sum.hop()
    step()
    qkv_sum.gather(0)
    up_grad = up_sum.finish()
    vector = vector_sum.finish()
    half, proj_half = features // 2, width // 2
    qkv_grad = qkv_sum.finish(parts=tuple(c * half for c in range(3)), rows=half, planes=3)
    proj_grad = qkv_sum.finish(
        parts=tuple(3 * half + k * proj_half for k in range(features // width)), rows=proj_half, beside=features // width
    )
    grad_hidden = grad_hidden.reshape(hidden_in.shape)
    return (
        out_hidden,
        grad_hidden,
        qkv_grad.reshape(3, features, width).transpose(1, 0, 2),
        vector[6 + ups_rows, :width],
        vector[6 + ups_rows, width:],
        proj_grad,
        vector[0],
        vector[1],
        vector[2],
        up_grad,
        vector[6 : 6 + ups_rows].reshape(-1),
        down_grad,
        vector[3],
        vector[4],
        vector[5],
    )


def solution(mesh):
    rows = P(("dp", "tensor"), None, None)
    placed = (
        rows, P("dp"), P("dp"), rows, P(None, None, "tensor"), P("tensor"), P("tensor"),
        P("tensor", None), P(), P(), P(), P(None, "tensor"), P("tensor"), P("tensor", None),
        P(), P(), P(),
    )
    outs = (
        rows, rows, P(None, None, "tensor"), P("tensor"), P("tensor"), P("tensor", None), P(), P(),
        P(), P(None, "tensor"), P("tensor"), P("tensor", None), P(), P(), P(),
    )
    return jax.shard_map(body, mesh=mesh, in_specs=placed, out_specs=outs, check_vma=False)
```
